32 devices in a mesh: groups: 2 (over x), ep: 8 (over z, y), sub: 2 (over core).
Axes of the slice: x: 2, y: 2, z: 4, core: 2. Of those that a mesh axis runs over, the one named last changes fastest.
Arguments:
- queries: bfloat16 [256, 2, 128, 576], P(('groups', 'ep', 'sub')), parts along dimension 0, may hold values from -400 to 400
- latent_cache: bfloat16 [256, 256, 576], P(('groups', 'ep', 'sub')), parts along dimension 0, may hold values from -6 to 6
- new_latent: bfloat16 [256, 2, 576], P(('groups', 'ep', 'sub')), parts along dimension 0, may hold values from -8 to 8
- lengths: int32 [256], P(('groups', 'ep', 'sub')), parts along dimension 0, may hold values from 2 to 256, as said below
- moe_input: bfloat16 [512, 3584], P(('groups', 'ep', 'sub')), parts along dimension 0, may hold values from -6 to 6
- gate_scores: float32 [512, 8], P(('groups', 'ep', 'sub')), parts along dimension 0, may hold values from -6 to 6
- expert_ids: int32 [512, 8], P(('groups', 'ep', 'sub')), parts along dimension 0, may hold values from 0 to 13, as said below
- placement: int32 [28, 2], P('groups'), parts along dimension 0, may hold values from 0 to 15, as said below
- w_gate: bfloat16 [32, 3584, 1024], P(('groups', 'ep'), None, 'sub'), parts along dimension 0, as said below
- w_up: bfloat16 [32, 3584, 1024], P(('groups', 'ep'), None, 'sub'), parts along dimension 0, as said below
- w_down: bfloat16 [32, 1024, 3584], P(('groups', 'ep'), 'sub'), parts along dimension 0, as said below
Outputs:
- attn_latent: bfloat16 [256, 2, 128, 512], P(('groups', 'ep', 'sub')), parts along dimension 0
- moe_output: bfloat16 [512, 3584], P(('groups', 'ep', 'sub')), parts along dimension 0
The draws below stay inside these ranges and needn't reach their ends.
There are 2 independent parts, one for each index of `groups`. The reference program is written for one: setup_inputs(seed, part) draws one part's arguments, and reference() takes and returns one part's arrays. A program takes and returns all parts, laid end to end along the dimension named above; each array names one. Nothing has to cross between parts.
Inputs may be any that keep to these rules, and one draw needn't show every extreme that they name: `lengths`: all 8 requests of some device have length 256. `expert_ids`: each row names 8 different experts. One expert, which has a single replica in placement, is named by every row. `placement`: column 0 puts the 14 experts on distinct slots; column 1 equals column 0 except for 2 experts, whose second replicas take the remaining 2 slots. `w_gate`: the slot of an expert's second replica holds the same matrix as its first. `w_up`: the slot of an expert's second replica holds the same matrix as its first. `w_down`: the slot of an expert's second replica holds the same matrix as its first.
All inputs are finite; a program needn't handle non-finite values.
Results may differ from the reference program's by a relative error of at most 0.0064.
Values may be sent and summed in bfloat16 or wider, within the bound.
No kernel may reach another device: no remote copies, remote signals or barrier semaphores. Data moves between devices by JAX's collectives and lax.ppermute only.
A program may use at most 128 MiB of HBM per device.

```python
import jax
import jax.numpy as jnp
from jax import lax

D = 3584
FFE = 1024
H = 128
LATENT_RANK = 512
LATENT = 576
SLOT_EP = 2
TOPK = 8
STEPS = 2
REQ_DEV = 8
CTX = 256
SLOTS = 16
REPLICA_SLOTS = 2
ROUTED_EXPERTS = 14
REQUESTS = 128
TOKENS = 256
N_EP = 8
N_SUB = 2


def routing_orders(key):
    expert_order = jax.random.permutation(jax.random.fold_in(key, 101), ROUTED_EXPERTS).astype(jnp.int32)
    slot_order = jax.random.permutation(jax.random.fold_in(key, 102), SLOTS).astype(jnp.int32)
    return (expert_order, slot_order)


def slot_sources(expert_order, slot_order):
    sources = jnp.arange(SLOTS, dtype=jnp.int32)
    return sources.at[slot_order[ROUTED_EXPERTS:]].set(slot_order[expert_order[1:1 + REPLICA_SLOTS]])


def draw_placement(key, part):
    expert_order, slot_order = routing_orders(key)
    primary = slot_order[:ROUTED_EXPERTS]
    secondary = primary.at[expert_order[1:1 + REPLICA_SLOTS]].set(slot_order[ROUTED_EXPERTS:])
    return jnp.stack([primary, secondary], axis=1).astype(jnp.int32)


def draw_expert_ids(key, part):
    expert_order, slot_order = routing_orders(key)
    key = jax.random.fold_in(key, 2)
    expert_position = jnp.zeros((ROUTED_EXPERTS,), jnp.int32).at[expert_order].set(jnp.arange(ROUTED_EXPERTS, dtype=jnp.int32))
    random_component = jax.random.randint(jax.random.fold_in(key, 1), (TOKENS, ROUTED_EXPERTS), 0, 1024)
    preference_boost = jnp.where(expert_position == 0, 1 << 20, jnp.where(expert_position <= REPLICA_SLOTS, 512, 0))
    selection_priority = (random_component + preference_boost[None, :]) * ROUTED_EXPERTS + expert_position[None, :]
    _, chosen = lax.top_k(selection_priority, TOPK)
    column_keys = jax.random.randint(jax.random.fold_in(key, 2), (TOKENS, TOPK), 0, 4096) * TOPK + jnp.arange(TOPK, dtype=jnp.int32)[None, :]
    shuffle = jnp.argsort(column_keys, axis=1, stable=True)
    return jnp.take_along_axis(chosen, shuffle, axis=1).astype(jnp.int32)


def draw_lengths(key, part):
    key = jax.random.fold_in(key, 3)
    base_lengths = jax.random.randint(jax.random.fold_in(key, 1), (REQUESTS,), 2, CTX + 1)
    full_device = jax.random.randint(jax.random.fold_in(key, 2), (), 0, REQUESTS // REQ_DEV)
    owner = jnp.arange(REQUESTS, dtype=jnp.int32) // REQ_DEV
    return jnp.where(owner == full_device, CTX, base_lengths).astype(jnp.int32)


def draw_latent_cache(key, part):
    key = jax.random.fold_in(key, 4)
    values = jnp.clip(jax.random.normal(jax.random.fold_in(key, 1), (REQUESTS, CTX, LATENT)), -5.0, 5.0)
    return values.astype(jnp.bfloat16)


def draw_queries(key, part):
    key = jax.random.fold_in(key, 5)
    values = jnp.clip(jax.random.normal(jax.random.fold_in(key, 1), (REQUESTS, STEPS, H, LATENT)), -5.0, 5.0)
    return values.astype(jnp.bfloat16)


def draw_w_gate(key, part):
    expert_order, slot_order = routing_orders(key)
    key = jax.random.fold_in(key, 6)
    values = jax.random.normal(key, (SLOTS, D, FFE)) * D ** (-0.5)
    return jnp.take(values, slot_sources(expert_order, slot_order), axis=0).astype(jnp.bfloat16)


def draw_w_up(key, part):
    expert_order, slot_order = routing_orders(key)
    key = jax.random.fold_in(key, 7)
    values = jax.random.normal(key, (SLOTS, D, FFE)) * D ** (-0.5)
    return jnp.take(values, slot_sources(expert_order, slot_order), axis=0).astype(jnp.bfloat16)


def draw_w_down(key, part):
    expert_order, slot_order = routing_orders(key)
    key = jax.random.fold_in(key, 8)
    values = jax.random.normal(key, (SLOTS, FFE, D)) * FFE ** (-0.5)
    return jnp.take(values, slot_sources(expert_order, slot_order), axis=0).astype(jnp.bfloat16)


def steps_of(key, dims, pieces, smallest, high):
    loudness, own = 1.0, jax.random.fold_in(key, 6)
    for dim, shards_of in pieces:
        steps = jnp.exp(jax.random.uniform(jax.random.fold_in(own, dim), (shards_of,), jnp.float32, smallest / len(pieces), high / len(pieces)))
        loudness = loudness * jnp.repeat(steps, dims[dim] // shards_of).reshape([-1 if axis == dim else 1 for axis in range(len(dims))])
    return loudness


def normal_values(key, extent, deviation, bound, split=(), kind=jnp.bfloat16):
    entries = deviation * jax.random.normal(key, extent, jnp.float32)
    if split:
        entries = entries * steps_of(key, extent, split, -0.22, 0.18)
    return jnp.clip(entries, -bound, bound).astype(kind)


def setup_inputs(seed: int = 0, part: int = 0) -> dict:
    keys = jax.random.split(jax.random.key(seed), 12)
    part_keys = jax.random.split(jax.random.fold_in(keys[11], part), 12)
    return {
        "queries": draw_queries(jax.random.fold_in(jax.random.fold_in(keys[11], part), 71), part),
        "latent_cache": draw_latent_cache(jax.random.fold_in(jax.random.fold_in(keys[11], part), 71), part),
        "new_latent": normal_values(part_keys[2], (REQUESTS, STEPS, LATENT), 2.0, 8.0, ((0, 16),)),
        "lengths": draw_lengths(jax.random.fold_in(jax.random.fold_in(keys[11], part), 71), part),
        "moe_input": normal_values(part_keys[4], (TOKENS, D), 1.0, 6.0, ((0, 16),)),
        "gate_scores": normal_values(part_keys[5], (TOKENS, TOPK), 1.5, 6.0, ((0, 16),), jnp.float32),
        "expert_ids": draw_expert_ids(jax.random.fold_in(jax.random.fold_in(keys[11], part), 71), part),
        "placement": draw_placement(jax.random.fold_in(jax.random.fold_in(keys[11], part), 71), part),
        "w_gate": draw_w_gate(jax.random.fold_in(jax.random.fold_in(keys[11], part), 71), part),
        "w_up": draw_w_up(jax.random.fold_in(jax.random.fold_in(keys[11], part), 71), part),
        "w_down": draw_w_down(jax.random.fold_in(jax.random.fold_in(keys[11], part), 71), part),
    }


score_scale = 192.0 ** -0.5
route_scale = 2.5


def attend_request(packed):
    query_rows, cached_latent_rows, incoming_rows, length_value = packed
    flattened_query = query_rows.reshape(STEPS * H, LATENT)
    older = jnp.dot(flattened_query, cached_latent_rows.T, preferred_element_type=jnp.float32) * score_scale
    newer = jnp.dot(flattened_query, incoming_rows.T, preferred_element_type=jnp.float32) * score_scale
    positions = jnp.arange(CTX, dtype=jnp.int32)
    older = jnp.where(positions[None, :] < length_value, older, -jnp.inf)
    row_step = jnp.arange(STEPS * H, dtype=jnp.int32) // H
    newer = jnp.where(jnp.arange(STEPS, dtype=jnp.int32)[None, :] <= row_step[:, None], newer, -jnp.inf)
    highest = jnp.maximum(jnp.max(older, axis=1), jnp.max(newer, axis=1))
    older_exp = jnp.exp(older - highest[:, None])
    newer_exp = jnp.exp(newer - highest[:, None])
    totals = jnp.sum(older_exp, axis=1) + jnp.sum(newer_exp, axis=1)
    older_probability = (older_exp / totals[:, None]).astype(jnp.bfloat16)
    newer_probability = (newer_exp / totals[:, None]).astype(jnp.bfloat16)
    blended = jnp.dot(older_probability, cached_latent_rows[:, :LATENT_RANK], preferred_element_type=jnp.float32)
    blended = blended + jnp.dot(newer_probability, incoming_rows[:, :LATENT_RANK], preferred_element_type=jnp.float32)
    return blended.reshape(STEPS, H, LATENT_RANK).astype(jnp.bfloat16)


def reference(queries, latent_cache, new_latent, lengths, moe_input, gate_scores, expert_ids, placement, w_gate, w_up, w_down):
    attn_latent = lax.map(attend_request, (queries, latent_cache, new_latent, lengths))
    sigmoid_values = jax.nn.sigmoid(gate_scores)
    weights = (route_scale * sigmoid_values / jnp.sum(sigmoid_values, axis=1, keepdims=True)).astype(jnp.bfloat16)
    weights = lax.optimization_barrier(weights)
    parity = jnp.arange(TOKENS, dtype=jnp.int32) % 2
    slot_ids = jnp.where(parity[:, None] == 0, placement[expert_ids, 0], placement[expert_ids, 1])
    slot_match = slot_ids[:, :, None] == jnp.arange(SLOTS, dtype=jnp.int32)[None, None, :]
    slot_weight = jnp.sum(jnp.where(slot_match, weights.astype(jnp.float32)[:, :, None], 0.0), axis=1)
    half_width = FFE // N_SUB

    def device_terms(running, ep_index):
        partial_value = jnp.zeros((TOKENS, D), jnp.float32)
        for sub_index in range(N_SUB):
            lower = sub_index * half_width
            for local_slot in range(SLOT_EP):
                slot_index = ep_index * SLOT_EP + local_slot
                gate_full = lax.dynamic_index_in_dim(w_gate, slot_index, 0, keepdims=False)
                up_full = lax.dynamic_index_in_dim(w_up, slot_index, 0, keepdims=False)
                down_full = lax.dynamic_index_in_dim(w_down, slot_index, 0, keepdims=False)
                gate_values = jnp.dot(moe_input, gate_full[:, lower:lower + half_width], preferred_element_type=jnp.float32)
                upward = jnp.dot(moe_input, up_full[:, lower:lower + half_width], preferred_element_type=jnp.float32)
                active = (jax.nn.silu(gate_values) * upward).astype(jnp.bfloat16)
                column_weight = lax.dynamic_slice_in_dim(slot_weight, slot_index, 1, 1)
                partial_value = partial_value + column_weight * jnp.dot(active, down_full[lower:lower + half_width, :], preferred_element_type=jnp.float32)
        rounded = lax.optimization_barrier(partial_value.astype(jnp.bfloat16))
        running = running + rounded.astype(jnp.float32)
        return running, None

    summed, _ = lax.scan(device_terms, jnp.zeros((TOKENS, D), jnp.float32), jnp.arange(N_EP, dtype=jnp.int32))
    return attn_latent, summed.astype(jnp.bfloat16)
```

```python
import functools

import jax
import jax.numpy as jnp
from jax import lax
from jax.experimental import pallas as pl
from jax.experimental.pallas import tpu as pltpu
from jax.sharding import PartitionSpec as P

LATENT_RANK = 512
SCORE_SCALE = 192.0 ** (-0.5)
ROUTE_SCALE = 2.5
LANES = 128
F32 = jnp.float32
BF16 = jnp.bfloat16


def contract(a, b, dim_a, dim_b):
    return lax.dot_general(
        a, b, (((dim_a,), (dim_b,)), ((), ())), preferred_element_type=F32
    )


def attention_kernel(length_ref, query_ref, cache_ref, new_ref, *rest, first, block):
    out_ref = rest[-1]
    steps, heads = query_ref.shape[1], query_ref.shape[3]
    for b in range(block):
        length = length_ref[first + pl.program_id(0) * block + b]
        q = jnp.concatenate([query_ref[b, s].T for s in range(steps)], axis=0)
        cached = cache_ref[b]
        fresh = new_ref[b]
        older = contract(q, cached, 1, 0) * SCORE_SCALE
        newer = contract(q, fresh, 1, 1) * SCORE_SCALE
        position = lax.broadcasted_iota(jnp.int32, older.shape, 1)
        older = jnp.where(position < length, older, -jnp.inf)
        row = lax.broadcasted_iota(jnp.int32, newer.shape, 0)
        step = lax.broadcasted_iota(jnp.int32, newer.shape, 1)
        newer = jnp.where(step * heads <= row, newer, -jnp.inf)
        highest = jnp.maximum(
            jnp.max(older, axis=1, keepdims=True), jnp.max(newer, axis=1, keepdims=True)
        )
        older = jnp.exp(older - highest)
        newer = jnp.exp(newer - highest)
        total = jnp.sum(older, axis=1, keepdims=True) + jnp.sum(newer, axis=1, keepdims=True)
        blended = contract((older / total).astype(BF16), cached[:LATENT_RANK], 1, 1)
        blended = blended + contract((newer / total).astype(BF16), fresh[:, :LATENT_RANK], 1, 0)
        out_ref[b] = blended.reshape(steps, heads, LATENT_RANK).astype(BF16)


def attention(lengths, queries, cache, fresh, first, count, block, previous):
    requests, steps, latent, heads = queries.shape
    context = cache.shape[2]
    skip = first // block
    in_specs = [
        pl.BlockSpec((block, steps, latent, heads), lambda i, _: (i + skip, 0, 0, 0)),
        pl.BlockSpec((block, latent, context), lambda i, _: (i + skip, 0, 0)),
        pl.BlockSpec((block, steps, latent), lambda i, _: (i + skip, 0, 0)),
    ]
    operands = [queries, cache, fresh]
    aliases = {}
    if previous is not None:
        in_specs.append(pl.BlockSpec(memory_space=pl.ANY))
        operands.append(previous)
        aliases = {4: 0}
    rows = count * steps * heads
    return pl.pallas_call(
        functools.partial(attention_kernel, first=first, block=block),
        grid_spec=pltpu.PrefetchScalarGridSpec(
            num_scalar_prefetch=1,
            grid=(count // block,),
            in_specs=in_specs,
            out_specs=pl.BlockSpec(
                (block, steps, heads, LATENT_RANK), lambda i, _: (i + skip, 0, 0, 0)
            ),
        ),
        out_shape=jax.ShapeDtypeStruct((requests, steps, heads, LATENT_RANK), BF16),
        input_output_aliases=aliases,
        compiler_params=pltpu.CompilerParams(vmem_limit_bytes=14 << 20),
        cost_estimate=pl.CostEstimate(
            flops=rows * context * (latent + LATENT_RANK) * 2,
            bytes_accessed=count * (2 * steps * heads + context) * latent * 2,
            transcendentals=rows * context,
        ),
        name="attention",
    )(lengths, *operands)


def route_kernel(place_ref, rows_ref, score_ref, expert_ref, out_ref, *, experts, slots):
    tokens, width = rows_ref.shape
    sigmoid = jax.nn.sigmoid(score_ref[...])
    weights = ROUTE_SCALE * sigmoid / jnp.sum(sigmoid, axis=0, keepdims=True)
    weights = weights.astype(BF16).astype(F32)
    named = expert_ref[...]
    even = lax.broadcasted_iota(jnp.int32, named.shape, 1) % 2 == 0
    slot = jnp.zeros_like(named)
    for e in range(experts):
        slot = jnp.where(
            named == e, jnp.where(even, place_ref[0, e], place_ref[1, e]), slot
        )
    index = lax.broadcasted_iota(jnp.int32, (LANES, tokens), 0)
    table = jnp.zeros((LANES, tokens), F32)
    for k in range(named.shape[0]):
        table = table + jnp.where(index == slot[k : k + 1], weights[k : k + 1], 0.0)
    row = lax.broadcasted_iota(jnp.int32, (tokens, tokens), 0)
    column = lax.broadcasted_iota(jnp.int32, (tokens, tokens), 1)
    unit = jnp.where(row == column, 1.0, 0.0).astype(BF16)
    out_ref[:, :width] = rows_ref[...]
    out_ref[:, width:] = contract(unit, table.astype(BF16), 1, 1).astype(BF16)


def route(placement, rows, scores, expert_ids, slots):
    tokens, width = rows.shape
    vmem = pl.BlockSpec(memory_space=pltpu.VMEM)
    return pl.pallas_call(
        functools.partial(route_kernel, experts=placement.shape[0], slots=slots),
        in_specs=[pl.BlockSpec(memory_space=pltpu.SMEM), vmem, vmem, vmem],
        out_specs=vmem,
        out_shape=jax.ShapeDtypeStruct((tokens, width + LANES), BF16),
        compiler_params=pltpu.CompilerParams(vmem_limit_bytes=4 << 20),
        name="route",
    )(placement.T, rows, scores.T, expert_ids.T)


def experts_kernel(*refs, parts, tile):
    rows_refs = refs[:parts]
    gate_ref, up_ref, down_ref, chip_ref = refs[parts : parts + 4]
    out_refs = refs[parts + 4 : 2 * parts + 4]
    rows_s, act_s = refs[-2:]
    slots, width, hidden = gate_ref.shape
    start = 0
    for ref in rows_refs:
        rows_s[start : start + ref.shape[0], :] = ref[...]
        start += ref.shape[0]
    table = rows_s[:, width:].astype(F32)
    lane = lax.broadcasted_iota(jnp.int32, table.shape, 1)
    for s in range(slots):
        slot = chip_ref[0] * slots + s
        weight = jnp.sum(jnp.where(lane == slot, table, 0.0), axis=1, keepdims=True)
        rows = rows_s[:, :width]
        gate = jnp.dot(rows, gate_ref[s], preferred_element_type=F32)
        up = jnp.dot(rows, up_ref[s], preferred_element_type=F32)
        act = gate / (1.0 + jnp.exp(-gate)) * up
        act_s[:, s * hidden : (s + 1) * hidden] = (weight * act).astype(BF16)

    def project(i, carry):
        columns = pl.ds(pl.multiple_of(i * tile, tile), tile)
        total = jnp.dot(act_s[:, :hidden], down_ref[0, :, columns], preferred_element_type=F32)
        for s in range(1, slots):
            total = total + jnp.dot(
                act_s[:, s * hidden : (s + 1) * hidden],
                down_ref[s, :, columns],
                preferred_element_type=F32,
            )
        total = total.astype(BF16)
        start = 0
        for ref in out_refs:
            ref[:, columns] = total[start : start + ref.shape[0]]
            start += ref.shape[0]
        return carry

    lax.fori_loop(0, width // tile, project, 0)


def experts(parts, gate, up, down, chip):
    slots, width, hidden = gate.shape
    count = sum(p.shape[0] for p in parts)
    vmem = pl.BlockSpec(memory_space=pltpu.VMEM)
    return pl.pallas_call(
        functools.partial(experts_kernel, parts=len(parts), tile=512),
        in_specs=[vmem] * (len(parts) + 3) + [pl.BlockSpec(memory_space=pltpu.SMEM)],
        out_specs=[vmem] * len(parts),
        out_shape=[jax.ShapeDtypeStruct((p.shape[0], width), BF16) for p in parts],
        scratch_shapes=[
            pltpu.VMEM((count, parts[0].shape[1]), BF16),
            pltpu.VMEM((count, slots * hidden), BF16),
        ],
        compiler_params=pltpu.CompilerParams(vmem_limit_bytes=16 << 20),
        cost_estimate=pl.CostEstimate(
            flops=count * slots * 3 * width * hidden * 2,
            bytes_accessed=count * width * 4,
            transcendentals=count * slots * hidden,
        ),
        name="experts",
    )(*parts, gate, up, down, chip)


def halving_masks(ep):
    bits = []
    bit = ep // 2
    while bit:
        bits.append(bit)
        bit //= 2
    other = bits[:-2] + bits[-2:][::-1]
    return bits, other


def hop(x, ep, sub, masks, turn):
    pairs = [
        (e * sub + s, (e ^ masks[s % 2][turn]) * sub + s) for e in range(ep) for s in range(sub)
    ]
    return lax.ppermute(x, ("ep", "sub"), pairs)


def swap(x):
    return lax.ppermute(x, "sub", [(0, 1), (1, 0)])


def add(*terms):
    total = terms[0].astype(F32)
    for t in terms[1:]:
        total = total + t.astype(F32)
    return total.astype(BF16)


def on_device(
    queries,
    latent_cache,
    new_latent,
    lengths,
    moe_input,
    gate_scores,
    expert_ids,
    placement,
    w_gate,
    w_up,
    w_down,
):
    ep, sub = lax.axis_size("ep"), lax.axis_size("sub")
    masks = halving_masks(ep)
    turns = len(masks[0])
    tokens = moe_input.shape[0]
    requests = queries.shape[0]
    queries_t = queries.transpose(0, 1, 3, 2)
    cache_t = latent_cache.transpose(0, 2, 1)
    weights = [pltpu.with_memory_space_constraint(w, pltpu.VMEM) for w in (w_gate, w_up, w_down)]
    chip = lax.axis_index("ep").astype(jnp.int32)[None]
    slots = ep * w_gate.shape[0]

    part = requests // 4
    state = {"out": None, "next": 0}

    def attend(parts):
        for _ in range(parts):
            state["out"] = attention(
                lengths, queries_t, cache_t, new_latent, state["next"], part, 1, state["out"]
            )
            state["next"] += part

    rows = route(placement, moe_input, gate_scores, expert_ids, slots)
    for turn in range(turns - 1):
        got = hop(rows, ep, sub, masks, turn)
        if turn == 0:
            attend(2)
            got, state["out"] = lax.optimization_barrier((got, state["out"]))
        rows = jnp.concatenate([rows, got], axis=0)

    far = hop(rows, ep, sub, masks, turns - 1)
    near_own, near_other = experts([rows, swap(rows)], *weights, chip)
    near_back = swap(near_other)
    near = add(near_own, near_back)
    far, near = lax.optimization_barrier((far, near))

    far_own, far_other = experts([far, swap(far)], *weights, chip)
    far_sum = add(far_own, swap(far_other))

    total = near
    sent = far_sum
    for turn in range(turns - 1, -1, -1):
        got = hop(sent, ep, sub, masks, turn)
        if turn == turns - 1 or turn == 0:
            attend(1)
            got, state["out"] = lax.optimization_barrier((got, state["out"]))
        half = total.shape[0] // 2
        if turn:
            sent = add(total[half:], got[half:])
            total = add(total[:half], got[:half])
        else:
            total = add(total, got)
    return state["out"], total


def solution(mesh):
    split = ("groups", "ep", "sub")
    return jax.shard_map(
        on_device,
        mesh=mesh,
        in_specs=(
            P(split, None, None, None),
            P(split, None, None),
            P(split, None, None),
            P(split),
            P(split, None),
            P(split, None),
            P(split, None),
            P("groups", None),
            P(("groups", "ep"), None, "sub"),
            P(("groups", "ep"), None, "sub"),
            P(("groups", "ep"), "sub", None),
        ),
        out_specs=(P(split, None, None, None), P(split, None)),
        check_vma=False,
    )
```

```python
import functools

import jax
import jax.numpy as jnp
from jax import lax
from jax.experimental import pallas as pl
from jax.experimental.pallas import tpu as pltpu
from jax.sharding import PartitionSpec as P

LATENT_RANK = 512
SCORE_SCALE = 192.0 ** (-0.5)
ROUTE_SCALE = 2.5
LANES = 128
F32 = jnp.float32
BF16 = jnp.bfloat16


def contract(a, b, dim_a, dim_b):
    return lax.dot_general(
        a, b, (((dim_a,), (dim_b,)), ((), ())), preferred_element_type=F32
    )


def attend_request(q_steps, cached, fresh, length):
    heads = q_steps[0].shape[1]
    q = jnp.concatenate([q.T for q in q_steps], axis=0)
    older = contract(q, cached, 1, 0) * SCORE_SCALE
    newer = contract(q, fresh, 1, 1) * SCORE_SCALE
    position = lax.broadcasted_iota(jnp.int32, older.shape, 1)
    older = jnp.where(position < length, older, -jnp.inf)
    row = lax.broadcasted_iota(jnp.int32, newer.shape, 0)
    step = lax.broadcasted_iota(jnp.int32, newer.shape, 1)
    newer = jnp.where(step * heads <= row, newer, -jnp.inf)
    highest = jnp.maximum(
        jnp.max(older, axis=1, keepdims=True), jnp.max(newer, axis=1, keepdims=True)
    )
    older = jnp.exp(older - highest)
    newer = jnp.exp(newer - highest)
    total = jnp.sum(older, axis=1, keepdims=True) + jnp.sum(newer, axis=1, keepdims=True)
    blended = contract((older / total).astype(BF16), cached[:LATENT_RANK], 1, 1)
    blended = blended + contract((newer / total).astype(BF16), fresh[:, :LATENT_RANK], 1, 0)
    return blended.reshape(len(q_steps), heads, LATENT_RANK).astype(BF16)


def attention_kernel(*refs, first, count, loads, opening):
    length_ref, refs = refs[0], refs[1:]
    sources, refs = refs[:3], refs[3:]
    load_refs, refs = refs[:loads], refs[loads:]
    if not opening:
        refs = refs[1:]
    out_ref, refs = refs[0], refs[1:]
    if opening:
        resident, refs = refs[:3], refs[3:]
    else:
        resident = sources
    loaded, (result, out_sems, load_sems, in_sems) = refs[:loads], refs[loads:]
    requests = resident[0].shape[0]

    arrivals = []
    if opening:
        fresh = pltpu.make_async_copy(sources[2], resident[2], in_sems.at[2, 0])
        fresh.start()
        for lo, hi in ((first, first + count), (first + count, requests)):
            group = []
            if hi > lo:
                for i in range(2):
                    copy = pltpu.make_async_copy(
                        sources[i].at[lo:hi],
                        resident[i].at[lo:hi],
                        in_sems.at[i, 0 if lo == first else 1],
                    )
                    copy.start()
                    group.append(copy)
            arrivals.append(group)
        arrivals[0].append(fresh)
    copies = []
    for i, (source, target) in enumerate(zip(load_refs, loaded)):
        copy = pltpu.make_async_copy(source, target, load_sems.at[i])
        copy.start()
        copies.append(copy)
    if opening:
        for copy in arrivals[0]:
            copy.wait()
        copies += arrivals[1]
    query_ref, cache_ref, new_ref = resident
    for b in range(count):
        r = first + b
        steps = query_ref.shape[1]
        result[b] = attend_request(
            [query_ref[r, s] for s in range(steps)], cache_ref[r], new_ref[r], length_ref[r]
        )
        copy = pltpu.make_async_copy(result.at[b], out_ref.at[r], out_sems.at[b])
        copy.start()
        copies.append(copy)
    for copy in copies:
        copy.wait()


def attention(lengths, inputs, first, count, loads, previous):
    opening = previous is None
    requests, steps, latent, heads = inputs[0].shape
    vmem = pl.BlockSpec(memory_space=pltpu.VMEM)
    hbm = pl.BlockSpec(memory_space=pl.ANY)
    in_specs = [pl.BlockSpec(memory_space=pltpu.SMEM)]
    in_specs += [hbm if opening else vmem] * 3 + [hbm] * len(loads)
    operands = list(inputs)
    if opening:
        operands = [pltpu.with_memory_space_constraint(x, pltpu.HBM) for x in operands]
    else:
        operands = [pltpu.with_memory_space_constraint(x, pltpu.VMEM) for x in operands]
    operands += [pltpu.with_memory_space_constraint(x, pltpu.HBM) for x in loads]
    aliases = {}
    if not opening:
        in_specs.append(hbm)
        aliases = {len(operands) + 1: 0}
        operands.append(pltpu.with_memory_space_constraint(previous, pltpu.HBM))
    kept = (list(inputs) if opening else []) + list(loads)
    outs = pl.pallas_call(
        functools.partial(
            attention_kernel, first=first, count=count, loads=len(loads), opening=opening
        ),
        in_specs=in_specs,
        out_specs=[hbm] + [vmem] * len(kept),
        out_shape=[pltpu.HBM((requests, steps, heads, LATENT_RANK), BF16)]
        + [pltpu.VMEM(x.shape, x.dtype) for x in kept],
        scratch_shapes=[
            pltpu.VMEM((count, steps, heads, LATENT_RANK), BF16),
            pltpu.SemaphoreType.DMA((count,)),
            pltpu.SemaphoreType.DMA((max(len(loads), 1),)),
            pltpu.SemaphoreType.DMA((3, 2)),
        ],
        input_output_aliases=aliases,
        compiler_params=pltpu.CompilerParams(vmem_limit_bytes=12 << 20),
        cost_estimate=pl.CostEstimate(flops=1 << 20, bytes_accessed=1 << 16, transcendentals=0),
        name="attention",
    )(pltpu.with_memory_space_constraint(lengths, pltpu.HBM), *operands)
    out, kept = outs[0], list(outs[1:])
    if opening:
        return out, kept[:3], kept[3:]
    return out, list(inputs), kept


def route_kernel(place_ref, rows_ref, score_ref, expert_ref, out_ref, *, experts, slots):
    tokens, width = rows_ref.shape
    sigmoid = jax.nn.sigmoid(score_ref[...])
    weights = ROUTE_SCALE * sigmoid / jnp.sum(sigmoid, axis=0, keepdims=True)
    weights = weights.astype(BF16).astype(F32)
    named = expert_ref[...]
    even = lax.broadcasted_iota(jnp.int32, named.shape, 1) % 2 == 0
    slot = jnp.zeros_like(named)
    for e in range(experts):
        slot = jnp.where(
            named == e, jnp.where(even, place_ref[0, e], place_ref[1, e]), slot
        )
    index = lax.broadcasted_iota(jnp.int32, (LANES, tokens), 0)
    table = jnp.zeros((LANES, tokens), F32)
    for k in range(named.shape[0]):
        table = table + jnp.where(index == slot[k : k + 1], weights[k : k + 1], 0.0)
    row = lax.broadcasted_iota(jnp.int32, (tokens, tokens), 0)
    column = lax.broadcasted_iota(jnp.int32, (tokens, tokens), 1)
    unit = jnp.where(row == column, 1.0, 0.0).astype(BF16)
    out_ref[:, :width] = rows_ref[...]
    out_ref[:, width:] = contract(unit, table.astype(BF16), 1, 1).astype(BF16)


def route(placement, rows, scores, expert_ids, slots):
    tokens, width = rows.shape
    vmem = pl.BlockSpec(memory_space=pltpu.VMEM)
    return pl.pallas_call(
        functools.partial(route_kernel, experts=placement.shape[0], slots=slots),
        in_specs=[pl.BlockSpec(memory_space=pltpu.SMEM), vmem, vmem, vmem],
        out_specs=vmem,
        out_shape=jax.ShapeDtypeStruct((tokens, width + LANES), BF16),
        compiler_params=pltpu.CompilerParams(vmem_limit_bytes=4 << 20),
        name="route",
    )(*(pltpu.with_memory_space_constraint(x, pltpu.HBM) for x in (placement.T, rows, scores.T, expert_ids.T)))


def experts_kernel(*refs, parts, tile):
    rows_refs = refs[:parts]
    gate_ref, up_ref, down_ref, chip_ref = refs[parts : parts + 4]
    out_refs = refs[parts + 4 : 2 * parts + 4]
    rows_s, act_s = refs[-2:]
    slots, width, hidden = gate_ref.shape
    start = 0
    for ref in rows_refs:
        rows_s[start : start + ref.shape[0], :] = ref[...]
        start += ref.shape[0]
    table = rows_s[:, width:].astype(F32)
    lane = lax.broadcasted_iota(jnp.int32, table.shape, 1)
    for s in range(slots):
        slot = chip_ref[0] * slots + s
        weight = jnp.sum(jnp.where(lane == slot, table, 0.0), axis=1, keepdims=True)
        rows = rows_s[:, :width]
        gate = jnp.dot(rows, gate_ref[s], preferred_element_type=F32)
        up = jnp.dot(rows, up_ref[s], preferred_element_type=F32)
        act = gate / (1.0 + jnp.exp(-gate)) * up
        act_s[:, s * hidden : (s + 1) * hidden] = (weight * act).astype(BF16)

    def project(i, carry):
        columns = pl.ds(pl.multiple_of(i * tile, tile), tile)
        total = jnp.dot(act_s[:, :hidden], down_ref[0, :, columns], preferred_element_type=F32)
        for s in range(1, slots):
            total = total + jnp.dot(
                act_s[:, s * hidden : (s + 1) * hidden],
                down_ref[s, :, columns],
                preferred_element_type=F32,
            )
        start = 0
        for ref in out_refs:
            ref[:, columns] = total[start : start + ref.shape[0]].astype(ref.dtype)
            start += ref.shape[0]
        return carry

    lax.fori_loop(0, width // tile, project, 0)


def experts(parts, gate, up, down, chip):
    slots, width, hidden = gate.shape
    count = sum(p.shape[0] for p in parts)
    vmem = pl.BlockSpec(memory_space=pltpu.VMEM)
    return pl.pallas_call(
        functools.partial(experts_kernel, parts=len(parts), tile=512),
        in_specs=[vmem] * (len(parts) + 3) + [pl.BlockSpec(memory_space=pltpu.SMEM)],
        out_specs=[vmem] * len(parts),
        out_shape=[
            jax.ShapeDtypeStruct((p.shape[0], width), kind) for p, kind in zip(parts, (F32, BF16))
        ],
        scratch_shapes=[
            pltpu.VMEM((count, parts[0].shape[1]), BF16),
            pltpu.VMEM((count, slots * hidden), BF16),
        ],
        compiler_params=pltpu.CompilerParams(vmem_limit_bytes=16 << 20),
        cost_estimate=pl.CostEstimate(
            flops=1 << 20, bytes_accessed=1 << 16, transcendentals=0
        ),
        name="experts",
    )(*parts, gate, up, down, chip)


def halving_masks(ep):
    bits = []
    bit = ep // 2
    while bit:
        bits.append(bit)
        bit //= 2
    other = bits[:-2] + bits[-2:][::-1]
    return bits, other


def hop(x, ep, sub, masks, turn):
    pairs = [
        (e * sub + s, (e ^ masks[s % 2][turn]) * sub + s) for e in range(ep) for s in range(sub)
    ]
    return lax.ppermute(x, ("ep", "sub"), pairs)


def swap(x):
    return lax.ppermute(x, "sub", [(0, 1), (1, 0)])


def add(*terms):
    total = terms[0].astype(F32)
    for t in terms[1:]:
        total = total + t.astype(F32)
    return total


def on_device(
    queries,
    latent_cache,
    new_latent,
    lengths,
    moe_input,
    gate_scores,
    expert_ids,
    placement,
    w_gate,
    w_up,
    w_down,
):
    ep, sub = lax.axis_size("ep"), lax.axis_size("sub")
    masks = halving_masks(ep)
    turns = len(masks[0])
    tokens = moe_input.shape[0]
    requests = queries.shape[0]
    inputs = [queries.transpose(0, 1, 3, 2), latent_cache.transpose(0, 2, 1), new_latent]
    chip = lax.axis_index("ep").astype(jnp.int32)[None]
    slots = ep * w_gate.shape[0]
    barrier = lax.optimization_barrier
    chip, gate_scores, lengths = barrier((chip, gate_scores, lengths))

    out = None
    weights = []
    done = 0
    loads = [[w_gate, w_up], [w_down]] + [[]] * turns
    share = [1, 1] + [2] * turns

    def attend(window, tie):
        nonlocal out, inputs, done, weights
        count = min(share[window], requests - done)
        if window == 1 + turns:
            count = requests - done
        if count == 0:
            return tie
        out, inputs, loaded = attention(lengths, inputs, done, count, loads[window], out)
        weights = weights + loaded
        done += count
        tie, out, inputs, weights = barrier((tie, out, inputs, weights))
        return tie

    rows = route(placement, moe_input, gate_scores, expert_ids, slots)
    for turn in range(turns - 1):
        got = hop(rows, ep, sub, masks, turn)
        if turn < 2:
            rows, inputs, weights = barrier((rows, inputs, weights))
            got = attend(turn, got)
        rows = jnp.concatenate([rows, got], axis=0)

    far = hop(rows, ep, sub, masks, turns - 1)
    near_own, near_other = experts([rows, swap(rows)], *weights, chip)
    far, near_own, inputs, weights = barrier((far, near_own, inputs, weights))
    far_own, far_other = experts([far, swap(far)], *weights, chip)
    total = add(near_own, swap(near_other))
    sent = add(far_own, swap(far_other)).astype(BF16)
    for turn in range(turns - 1, -1, -1):
        got = hop(sent, ep, sub, masks, turn)
        sent, inputs = barrier((sent, inputs))
        got = attend(turns + 1 - turn, got)
        total = add(total, got)
        if turn:
            half = total.shape[0] // 2
            sent = total[half:].astype(BF16)
            total = total[:half]
    return out, total.astype(BF16)


def solution(mesh):
    split = ("groups", "ep", "sub")
    return jax.shard_map(
        on_device,
        mesh=mesh,
        in_specs=(
            P(split, None, None, None),
            P(split, None, None),
            P(split, None, None),
            P(split),
            P(split, None),
            P(split, None),
            P(split, None),
            P("groups", None),
            P(("groups", "ep"), None, "sub"),
            P(("groups", "ep"), None, "sub"),
            P(("groups", "ep"), "sub", None),
        ),
        out_specs=(P(split, None, None, None), P(split, None)),
        check_vma=False,
    )
```

```python
import functools

import jax
import jax.numpy as jnp
from jax import lax
from jax.experimental import pallas as pl
from jax.experimental.pallas import tpu as pltpu
from jax.sharding import PartitionSpec as P

LATENT_RANK = 512
SCORE_SCALE = 192.0 ** (-0.5)
ROUTE_SCALE = 2.5
LANES = 128
F32 = jnp.float32
BF16 = jnp.bfloat16
SMALL_COST = pl.CostEstimate(flops=1 << 20, bytes_accessed=1 << 16, transcendentals=0)


def contract(a, b, dim_a, dim_b):
    return lax.dot_general(
        a, b, (((dim_a,), (dim_b,)), ((), ())), preferred_element_type=F32
    )


def attend_request(q_steps, cached, fresh, length):
    heads, context, steps = q_steps[0].shape[1], cached.shape[1], fresh.shape[0]
    q = jnp.concatenate(q_steps, axis=1)
    padded = jnp.concatenate(
        [fresh, jnp.zeros((-steps % 16, fresh.shape[1]), fresh.dtype)], axis=0
    )
    scores = jnp.concatenate([contract(cached, q, 0, 0), contract(padded, q, 1, 0)], axis=0)
    scores = scores * SCORE_SCALE
    key = lax.broadcasted_iota(jnp.int32, scores.shape, 0)
    column = lax.broadcasted_iota(jnp.int32, scores.shape, 1)
    step = key - context
    is_new = jnp.logical_and(step >= 0, jnp.logical_and(step < steps, step * heads <= column))
    is_old = jnp.logical_and(key < context, key < length)
    scores = jnp.where(jnp.logical_or(is_old, is_new), scores, -jnp.inf)
    weights = jnp.exp(scores - jnp.max(scores, axis=0, keepdims=True))
    total = jnp.sum(weights, axis=0, keepdims=True)
    probs = (weights / total).astype(BF16)
    blended = contract(probs[:context], cached[:LATENT_RANK], 0, 1)
    blended = blended + contract(probs[context:], padded[:, :LATENT_RANK], 0, 0)
    return blended.reshape(len(q_steps), heads, LATENT_RANK).astype(BF16)


def attention_kernel(*refs, base, first, count, loads, opening, following):
    length_ref, refs = refs[0], refs[1:]
    sources, refs = refs[:3], refs[3:]
    load_refs, refs = refs[:loads], refs[loads:]
    if following:
        refs = refs[1:]
    out_ref, refs = refs[0], refs[1:]
    if opening:
        resident, refs = refs[:3], refs[3:]
    else:
        resident = sources
    loaded, (result, out_sems, load_sems, in_sems) = refs[:loads], refs[loads:]
    held = resident[0].shape[0]

    needed, copies = [], []
    if opening:
        for lo, hi, group in ((0, first - base + count, 0), (first - base + count, held, 1)):
            if hi == lo:
                continue
            for i in range(3):
                copy = pltpu.make_async_copy(
                    sources[i].at[base + lo : base + hi],
                    resident[i].at[lo:hi],
                    in_sems.at[i, group],
                )
                copy.start()
                (copies if group else needed).append(copy)
    for i, (source, target) in enumerate(zip(load_refs, loaded)):
        copy = pltpu.make_async_copy(source, target, load_sems.at[i])
        copy.start()
        copies.append(copy)
    for copy in needed:
        copy.wait()
    query_ref, cache_ref, new_ref = resident
    steps = query_ref.shape[1]
    for b in range(count):
        r = first - base + b
        result[b] = attend_request(
            [query_ref[r, s] for s in range(steps)], cache_ref[r], new_ref[r], length_ref[first + b]
        )
        copy = pltpu.make_async_copy(result.at[b], out_ref.at[first + b], out_sems.at[b])
        copy.start()
        copies.append(copy)
    for copy in copies:
        copy.wait()


def attention(lengths, inputs, base, first, count, held=0, loads=(), previous=None):
    opening, following = held > 0, previous is not None
    _, steps, latent, heads = inputs[0].shape
    requests = lengths.shape[0]
    vmem = pl.BlockSpec(memory_space=pltpu.VMEM)
    hbm = pl.BlockSpec(memory_space=pl.ANY)
    in_specs = [pl.BlockSpec(memory_space=pltpu.SMEM)]
    in_specs += [hbm if opening else vmem] * 3 + [hbm] * len(loads)
    place = pltpu.HBM if opening else pltpu.VMEM
    operands = [pltpu.with_memory_space_constraint(lengths, pltpu.HBM)]
    operands += [pltpu.with_memory_space_constraint(x, place) for x in inputs]
    operands += [pltpu.with_memory_space_constraint(x, pltpu.HBM) for x in loads]
    aliases = {}
    if following:
        in_specs.append(hbm)
        aliases = {len(operands): 0}
        operands.append(pltpu.with_memory_space_constraint(previous, pltpu.HBM))
    kept = [((held,) + x.shape[1:], x.dtype) for x in inputs] if opening else []
    kept += [(x.shape, x.dtype) for x in loads]
    outs = pl.pallas_call(
        functools.partial(
            attention_kernel,
            base=base,
            first=first,
            count=count,
            loads=len(loads),
            opening=opening,
            following=following,
        ),
        in_specs=in_specs,
        out_specs=[hbm] + [vmem] * len(kept),
        out_shape=[pltpu.HBM((requests, steps, heads, LATENT_RANK), BF16)]
        + [pltpu.VMEM(shape, kind) for shape, kind in kept],
        scratch_shapes=[
            pltpu.VMEM((count, steps, heads, LATENT_RANK), BF16),
            pltpu.SemaphoreType.DMA((count,)),
            pltpu.SemaphoreType.DMA((max(len(loads), 1),)),
            pltpu.SemaphoreType.DMA((3, 2)),
        ],
        input_output_aliases=aliases,
        compiler_params=pltpu.CompilerParams(vmem_limit_bytes=12 << 20),
        cost_estimate=SMALL_COST,
        name="attention",
    )(*operands)
    kept = list(outs[1:])
    if opening:
        return outs[0], kept[:3], kept[3:]
    return outs[0], list(inputs), kept


def route_kernel(place_ref, rows_ref, score_ref, expert_ref, out_ref, *, experts, slots):
    tokens, width = rows_ref.shape
    sigmoid = jax.nn.sigmoid(score_ref[...])
    weights = ROUTE_SCALE * sigmoid / jnp.sum(sigmoid, axis=0, keepdims=True)
    weights = weights.astype(BF16).astype(F32)
    named = expert_ref[...]
    even = lax.broadcasted_iota(jnp.int32, named.shape, 1) % 2 == 0
    slot = jnp.zeros_like(named)
    for e in range(experts):
        slot = jnp.where(
            named == e, jnp.where(even, place_ref[0, e], place_ref[1, e]), slot
        )
    index = lax.broadcasted_iota(jnp.int32, (LANES, tokens), 0)
    table = jnp.zeros((LANES, tokens), F32)
    for k in range(named.shape[0]):
        table = table + jnp.where(index == slot[k : k + 1], weights[k : k + 1], 0.0)
    row = lax.broadcasted_iota(jnp.int32, (tokens, tokens), 0)
    column = lax.broadcasted_iota(jnp.int32, (tokens, tokens), 1)
    unit = jnp.where(row == column, 1.0, 0.0).astype(BF16)
    out_ref[:, :width] = rows_ref[...]
    out_ref[:, width:] = contract(unit, table.astype(BF16), 1, 1).astype(BF16)


def route(placement, rows, scores, expert_ids, slots):
    tokens, width = rows.shape
    vmem = pl.BlockSpec(memory_space=pltpu.VMEM)
    return pl.pallas_call(
        functools.partial(route_kernel, experts=placement.shape[0], slots=slots),
        in_specs=[pl.BlockSpec(memory_space=pltpu.SMEM), vmem, vmem, vmem],
        out_specs=vmem,
        out_shape=jax.ShapeDtypeStruct((tokens, width + LANES), BF16),
        compiler_params=pltpu.CompilerParams(vmem_limit_bytes=4 << 20),
        name="route",
    )(*(pltpu.with_memory_space_constraint(x, pltpu.HBM) for x in (placement.T, rows, scores.T, expert_ids.T)))


def project(act_s, down_ref, own_ref, other_ref, own, first, tile):
    slots, hidden, _ = down_ref.shape

    def step(i, carry):
        source = pl.ds(pl.multiple_of(first + i * tile, LANES), tile)
        target = pl.ds(pl.multiple_of(i * tile, LANES), tile)
        total = contract(act_s[:, :hidden], down_ref[0, :, source], 1, 0)
        for s in range(1, slots):
            total = total + contract(
                act_s[:, s * hidden : (s + 1) * hidden], down_ref[s, :, source], 1, 0
            )
        own_ref[:, target] = total[:own]
        other_ref[:, target] = total[own:].astype(BF16)
        return carry

    lax.fori_loop(0, own_ref.shape[1] // tile, step, 0)


def experts_kernel(*refs, parts, tile, load):
    rows_refs = refs[:parts]
    gate_ref, up_ref, down_ref, chip_ref, own_ref, other_ref, act_s = refs[parts : parts + 7]
    rows_s = refs[-2]
    if load:
        copy = pltpu.make_async_copy(down_ref, refs[parts + 7], refs[-1].at[0])
        copy.start()
        down_ref = refs[parts + 7]
    slots, width, hidden = gate_ref.shape
    start = 0
    for ref in rows_refs:
        rows_s[start : start + ref.shape[0], :] = ref[...]
        start += ref.shape[0]
    table = rows_s[:, width:].astype(F32)
    lane = lax.broadcasted_iota(jnp.int32, table.shape, 1)
    for s in range(slots):
        slot = chip_ref[0] * slots + s
        weight = jnp.sum(jnp.where(lane == slot, table, 0.0), axis=1, keepdims=True)
        rows = rows_s[:, :width]
        gate = contract(rows, gate_ref[s], 1, 0)
        up = contract(rows, up_ref[s], 1, 0)
        act = gate / (1.0 + jnp.exp(-gate)) * up
        act_s[:, s * hidden : (s + 1) * hidden] = (weight * act).astype(BF16)
    if load:
        copy.wait()
    project(act_s, down_ref, own_ref, other_ref, own_ref.shape[0], 0, tile)


def down_kernel(act_ref, down_ref, own_ref, other_ref, *, first, tile):
    project(act_ref, down_ref, own_ref, other_ref, own_ref.shape[0], first, tile)


def experts(parts, gate, up, down, chip, columns, load):
    slots, width, hidden = gate.shape
    count = sum(p.shape[0] for p in parts)
    vmem = pl.BlockSpec(memory_space=pltpu.VMEM)
    down_spec = vmem
    if load:
        down_spec = pl.BlockSpec(memory_space=pl.ANY)
        down = pltpu.with_memory_space_constraint(down, pltpu.HBM)
    return pl.pallas_call(
        functools.partial(experts_kernel, parts=len(parts), tile=width // 4, load=load),
        in_specs=[vmem] * (len(parts) + 2) + [down_spec, pl.BlockSpec(memory_space=pltpu.SMEM)],
        out_specs=[vmem] * (4 if load else 3),
        out_shape=[
            jax.ShapeDtypeStruct((count // 2, columns), F32),
            jax.ShapeDtypeStruct((count // 2, columns), BF16),
            jax.ShapeDtypeStruct((count, slots * hidden), BF16),
        ]
        + ([pltpu.VMEM(down.shape, down.dtype)] if load else []),
        scratch_shapes=[
            pltpu.VMEM((count, parts[0].shape[1]), BF16),
            pltpu.SemaphoreType.DMA((1,)),
        ],
        compiler_params=pltpu.CompilerParams(vmem_limit_bytes=16 << 20),
        cost_estimate=SMALL_COST,
        name="experts",
    )(*parts, gate, up, down, chip)


def down_rest(act, down, first):
    count = act.shape[0]
    width = down.shape[2]
    vmem = pl.BlockSpec(memory_space=pltpu.VMEM)
    return pl.pallas_call(
        functools.partial(down_kernel, first=first, tile=width // 4),
        in_specs=[vmem] * 2,
        out_specs=[vmem] * 2,
        out_shape=[
            jax.ShapeDtypeStruct((count // 2, width - first), F32),
            jax.ShapeDtypeStruct((count // 2, width - first), BF16),
        ],
        compiler_params=pltpu.CompilerParams(vmem_limit_bytes=8 << 20),
        cost_estimate=SMALL_COST,
        name="down",
    )(act, down)


def halving_masks(ep):
    bits = []
    bit = ep // 2
    while bit:
        bits.append(bit)
        bit //= 2
    other = bits[:-2] + bits[-2:][::-1]
    return bits, other


def hop(x, ep, sub, masks, turn):
    pairs = [
        (e * sub + s, (e ^ masks[s % 2][turn]) * sub + s) for e in range(ep) for s in range(sub)
    ]
    return lax.ppermute(x, ("ep", "sub"), pairs)


def swap(x):
    return lax.ppermute(x, "sub", [(0, 1), (1, 0)])


def add(*terms):
    total = terms[0].astype(F32)
    for t in terms[1:]:
        total = total + t.astype(F32)
    return total


def on_device(
    queries,
    latent_cache,
    new_latent,
    lengths,
    moe_input,
    gate_scores,
    expert_ids,
    placement,
    w_gate,
    w_up,
    w_down,
):
    ep, sub = lax.axis_size("ep"), lax.axis_size("sub")
    masks = halving_masks(ep)
    turns = len(masks[0])
    width = moe_input.shape[1]
    requests, width = queries.shape[0], moe_input.shape[1]
    inputs = [queries.transpose(0, 1, 3, 2), latent_cache.transpose(0, 2, 1), new_latent]
    chip = lax.axis_index("ep").astype(jnp.int32)[None]
    slots = ep * w_gate.shape[0]
    barrier = lax.optimization_barrier
    chip, gate_scores, lengths = barrier((chip, gate_scores, lengths))

    requests = queries.shape[0]
    half = width // 2

    base = route(placement, moe_input, gate_scores, expert_ids, slots)
    for turn in range(turns - 2):
        got = hop(base, ep, sub, masks, turn)
        if turn == 0:
            base, inputs = barrier((base, inputs))
            out, _, (gate, up) = attention(lengths, inputs, 0, 0, 2, held=2, loads=(w_gate, w_up))
            got, out, inputs = barrier((got, out, inputs))
        base = jnp.concatenate([base, got], axis=0)

    second = hop(base, ep, sub, masks, turns - 2)
    early = hop(base, ep, sub, masks, turns - 1)
    base, inputs = barrier((base, inputs))
    out, inputs, _ = attention(lengths, inputs, 2, 2, 1, held=requests - 2, previous=out)
    done = 3
    second, out, inputs = barrier((second, out, inputs))
    late = hop(second, ep, sub, masks, turns - 1)
    near_rows = [base, second, swap(base), swap(second)]
    near_rows, early = barrier((near_rows, early))
    early_swap = swap(early)
    near_own, near_other, _, down = experts(near_rows, gate, up, w_down, chip, width, True)
    late, early_swap, near_own, near_other = barrier((late, early_swap, near_own, near_other))
    near_back = swap(near_other)
    own_a, other_a, act = experts(
        [early, late, early_swap, swap(late)], gate, up, down, chip, half, False
    )
    sent_a = add(own_a, swap(other_a)).astype(BF16)
    sent_a, act = barrier((sent_a, act))
    own_b, other_b = down_rest(act, down, half)
    totals = [
        barrier(add(near_own[:, :half], near_back[:, :half])),
        barrier(add(near_own[:, half:], near_back[:, half:])),
    ]
    sent = [sent_a, add(own_b, swap(other_b)).astype(BF16)]
    shares = {turns - 1: 3, 0: requests}
    for turn in range(turns - 1, -1, -1):
        got = [hop(x, ep, sub, masks, turn) for x in sent]
        if turn in shares and done < requests:
            sent, inputs = barrier((sent, inputs))
            count = min(shares[turn], requests - done)
            out, inputs, _ = attention(lengths, inputs, 2, done, count, previous=out)
            done += count
            got[0], out, inputs = barrier((got[0], out, inputs))
        totals = [add(t, g) for t, g in zip(totals, got)]
        if turn:
            keep = totals[0].shape[0] // 2
            sent = [barrier(t[keep:].astype(BF16)) for t in totals]
            totals = [barrier(t[:keep]) for t in totals]
    return out, jnp.concatenate(totals, axis=1).astype(BF16)


def solution(mesh):
    split = ("groups", "ep", "sub")
    return jax.shard_map(
        on_device,
        mesh=mesh,
        in_specs=(
            P(split, None, None, None),
            P(split, None, None),
            P(split, None, None),
            P(split),
            P(split, None),
            P(split, None),
            P(split, None),
            P("groups", None),
            P(("groups", "ep"), None, "sub"),
            P(("groups", "ep"), None, "sub"),
            P(("groups", "ep"), "sub", None),
        ),
        out_specs=(P(split, None, None, None), P(split, None)),
        check_vma=False,
    )
```

```python
import functools

import jax
import jax.numpy as jnp
from jax import lax
from jax.experimental import pallas as pl
from jax.experimental.pallas import tpu as pltpu
from jax.sharding import PartitionSpec as P

LATENT_RANK = 512
SCORE_SCALE = 192.0 ** (-0.5)
ROUTE_SCALE = 2.5
LANES = 128
F32 = jnp.float32
BF16 = jnp.bfloat16
SMALL_COST = pl.CostEstimate(flops=1 << 20, bytes_accessed=1 << 16, transcendentals=0)


def contract(a, b, dim_a, dim_b):
    return lax.dot_general(
        a, b, (((dim_a,), (dim_b,)), ((), ())), preferred_element_type=F32
    )


def attend_request(q_steps, cached, fresh, length):
    heads, context, steps = q_steps[0].shape[1], cached.shape[1], fresh.shape[0]
    q = jnp.concatenate(q_steps, axis=1)
    padded = jnp.concatenate(
        [fresh, jnp.zeros((-steps % 16, fresh.shape[1]), fresh.dtype)], axis=0
    )
    scores = jnp.concatenate([contract(cached, q, 0, 0), contract(padded, q, 1, 0)], axis=0)
    scores = scores * SCORE_SCALE
    key = lax.broadcasted_iota(jnp.int32, scores.shape, 0)
    column = lax.broadcasted_iota(jnp.int32, scores.shape, 1)
    step = key - context
    is_new = jnp.logical_and(step >= 0, jnp.logical_and(step < steps, step * heads <= column))
    is_old = jnp.logical_and(key < context, key < length)
    scores = jnp.where(jnp.logical_or(is_old, is_new), scores, -jnp.inf)
    weights = jnp.exp(scores - jnp.max(scores, axis=0, keepdims=True))
    total = jnp.sum(weights, axis=0, keepdims=True)
    probs = (weights / total).astype(BF16)
    blended = contract(probs[:context], cached[:LATENT_RANK], 0, 1)
    blended = blended + contract(probs[context:], padded[:, :LATENT_RANK], 0, 0)
    return blended.reshape(len(q_steps), heads, LATENT_RANK).astype(BF16)


def attention_kernel(*refs, base, first, count, loads, opening, following):
    length_ref, refs = refs[0], refs[1:]
    sources, refs = refs[:3], refs[3:]
    load_refs, refs = refs[:loads], refs[loads:]
    if following:
        refs = refs[1:]
    out_ref, refs = refs[0], refs[1:]
    if opening:
        resident, refs = refs[:3], refs[3:]
    else:
        resident = sources
    loaded, (result, out_sems, load_sems, in_sems) = refs[:loads], refs[loads:]
    held = resident[0].shape[0]

    needed, copies = [], []
    if opening:
        for lo, hi, group in ((0, first - base + count, 0), (first - base + count, held, 1)):
            if hi == lo:
                continue
            for i in range(3):
                copy = pltpu.make_async_copy(
                    sources[i].at[base + lo : base + hi],
                    resident[i].at[lo:hi],
                    in_sems.at[i, group],
                )
                copy.start()
                (copies if group else needed).append(copy)
    for i, (source, target) in enumerate(zip(load_refs, loaded)):
        copy = pltpu.make_async_copy(source, target, load_sems.at[i])
        copy.start()
        copies.append(copy)
    for copy in needed:
        copy.wait()
    query_ref, cache_ref, new_ref = resident
    steps = query_ref.shape[1]
    for b in range(count):
        r = first - base + b
        result[b] = attend_request(
            [query_ref[r, s] for s in range(steps)], cache_ref[r], new_ref[r], length_ref[first + b]
        )
        copy = pltpu.make_async_copy(result.at[b], out_ref.at[first + b], out_sems.at[b])
        copy.start()
        copies.append(copy)
    for copy in copies:
        copy.wait()


def attention(lengths, inputs, base, first, count, held=0, loads=(), previous=None):
    opening, following = held > 0, previous is not None
    _, steps, latent, heads = inputs[0].shape
    requests = lengths.shape[0]
    vmem = pl.BlockSpec(memory_space=pltpu.VMEM)
    hbm = pl.BlockSpec(memory_space=pl.ANY)
    in_specs = [pl.BlockSpec(memory_space=pltpu.SMEM)]
    in_specs += [hbm if opening else vmem] * 3 + [hbm] * len(loads)
    place = pltpu.HBM if opening else pltpu.VMEM
    operands = [pltpu.with_memory_space_constraint(lengths, pltpu.HBM)]
    operands += [pltpu.with_memory_space_constraint(x, place) for x in inputs]
    operands += [pltpu.with_memory_space_constraint(x, pltpu.HBM) for x in loads]
    aliases = {}
    if following:
        in_specs.append(hbm)
        aliases = {len(operands): 0}
        operands.append(pltpu.with_memory_space_constraint(previous, pltpu.HBM))
    kept = [((held,) + x.shape[1:], x.dtype) for x in inputs] if opening else []
    kept += [(x.shape, x.dtype) for x in loads]
    outs = pl.pallas_call(
        functools.partial(
            attention_kernel,
            base=base,
            first=first,
            count=count,
            loads=len(loads),
            opening=opening,
            following=following,
        ),
        in_specs=in_specs,
        out_specs=[hbm] + [vmem] * len(kept),
        out_shape=[pltpu.HBM((requests, steps, heads, LATENT_RANK), BF16)]
        + [pltpu.VMEM(shape, kind) for shape, kind in kept],
        scratch_shapes=[
            pltpu.VMEM((count, steps, heads, LATENT_RANK), BF16),
            pltpu.SemaphoreType.DMA((count,)),
            pltpu.SemaphoreType.DMA((max(len(loads), 1),)),
            pltpu.SemaphoreType.DMA((3, 2)),
        ],
        input_output_aliases=aliases,
        compiler_params=pltpu.CompilerParams(vmem_limit_bytes=12 << 20),
        cost_estimate=pl.CostEstimate(flops=1 << 32, bytes_accessed=1 << 23, transcendentals=0)
        if opening
        else SMALL_COST,
        name="attention",
    )(*operands)
    kept = list(outs[1:])
    if opening:
        return outs[0], kept[:3], kept[3:]
    return outs[0], list(inputs), kept


def route_kernel(place_ref, rows_ref, score_ref, expert_ref, out_ref, *, experts, slots):
    tokens, width = rows_ref.shape
    sigmoid = jax.nn.sigmoid(score_ref[...])
    weights = ROUTE_SCALE * sigmoid / jnp.sum(sigmoid, axis=0, keepdims=True)
    weights = weights.astype(BF16).astype(F32)
    named = expert_ref[...]
    even = lax.broadcasted_iota(jnp.int32, named.shape, 1) % 2 == 0
    slot = jnp.zeros_like(named)
    for e in range(experts):
        slot = jnp.where(
            named == e, jnp.where(even, place_ref[0, e], place_ref[1, e]), slot
        )
    index = lax.broadcasted_iota(jnp.int32, (LANES, tokens), 0)
    table = jnp.zeros((LANES, tokens), F32)
    for k in range(named.shape[0]):
        table = table + jnp.where(index == slot[k : k + 1], weights[k : k + 1], 0.0)
    row = lax.broadcasted_iota(jnp.int32, (tokens, tokens), 0)
    column = lax.broadcasted_iota(jnp.int32, (tokens, tokens), 1)
    unit = jnp.where(row == column, 1.0, 0.0).astype(BF16)
    out_ref[:, :width] = rows_ref[...]
    out_ref[:, width:] = contract(unit, table.astype(BF16), 1, 1).astype(BF16)


def route(placement, rows, scores, expert_ids, slots):
    tokens, width = rows.shape
    vmem = pl.BlockSpec(memory_space=pltpu.VMEM)
    return pl.pallas_call(
        functools.partial(route_kernel, experts=placement.shape[0], slots=slots),
        in_specs=[pl.BlockSpec(memory_space=pltpu.SMEM), vmem, vmem, vmem],
        out_specs=vmem,
        out_shape=jax.ShapeDtypeStruct((tokens, width + LANES), BF16),
        compiler_params=pltpu.CompilerParams(vmem_limit_bytes=4 << 20),
        name="route",
    )(*(pltpu.with_memory_space_constraint(x, pltpu.HBM) for x in (placement.T, rows, scores.T, expert_ids.T)))


def project(act_s, down_ref, own_ref, other_ref, first, tile):
    slots, hidden, _ = down_ref.shape
    own = own_ref.shape[0]

    def step(i, carry):
        source = pl.ds(pl.multiple_of(first + i * tile, LANES), tile)
        target = pl.ds(pl.multiple_of(i * tile, LANES), tile)
        total = contract(act_s[:, :hidden], down_ref[0, :, source], 1, 0)
        for s in range(1, slots):
            total = total + contract(
                act_s[:, s * hidden : (s + 1) * hidden], down_ref[s, :, source], 1, 0
            )
        own_ref[:, target] = total[:own]
        other_ref[:, target] = total[own:].astype(BF16)
        return carry

    lax.fori_loop(0, own_ref.shape[1] // tile, step, 0)


def experts_kernel(*refs, parts, cuts, tile):
    rows_refs, refs = refs[:parts], refs[parts:]
    (gate_ref, up_ref, down_ref, chip_ref), refs = refs[:4], refs[4:]
    own_refs, other_refs, (rows_s, act_s) = refs[:cuts], refs[cuts : 2 * cuts], refs[2 * cuts :]
    slots, width, hidden = gate_ref.shape
    start = 0
    for ref in rows_refs:
        rows_s[start : start + ref.shape[0], :] = ref[...]
        start += ref.shape[0]
    table = rows_s[:, width:].astype(F32)
    lane = lax.broadcasted_iota(jnp.int32, table.shape, 1)
    for s in range(slots):
        slot = chip_ref[0] * slots + s
        weight = jnp.sum(jnp.where(lane == slot, table, 0.0), axis=1, keepdims=True)
        rows = rows_s[:, :width]
        gate = contract(rows, gate_ref[s], 1, 0)
        up = contract(rows, up_ref[s], 1, 0)
        act = gate / (1.0 + jnp.exp(-gate)) * up
        act_s[:, s * hidden : (s + 1) * hidden] = (weight * act).astype(BF16)
    for i, (own_ref, other_ref) in enumerate(zip(own_refs, other_refs)):
        project(act_s, down_ref, own_ref, other_ref, i * own_ref.shape[1], tile)


def experts(parts, gate, up, down, chip, cuts):
    slots, width, hidden = gate.shape
    count = sum(p.shape[0] for p in parts)
    vmem = pl.BlockSpec(memory_space=pltpu.VMEM)
    shape = (count // 2, width // cuts)
    outs = pl.pallas_call(
        functools.partial(experts_kernel, parts=len(parts), cuts=cuts, tile=width // 4),
        in_specs=[vmem] * (len(parts) + 3) + [pl.BlockSpec(memory_space=pltpu.SMEM)],
        out_specs=[vmem] * (2 * cuts),
        out_shape=[jax.ShapeDtypeStruct(shape, F32)] * cuts
        + [jax.ShapeDtypeStruct(shape, BF16)] * cuts,
        scratch_shapes=[
            pltpu.VMEM((count, parts[0].shape[1]), BF16),
            pltpu.VMEM((count, slots * hidden), BF16),
        ],
        compiler_params=pltpu.CompilerParams(vmem_limit_bytes=16 << 20),
        cost_estimate=SMALL_COST,
        name="experts",
    )(*parts, gate, up, down, chip)
    return outs[:cuts], outs[cuts:]


def halving_masks(ep):
    bits = []
    bit = ep // 2
    while bit:
        bits.append(bit)
        bit //= 2
    other = bits[:-2] + bits[-2:][::-1]
    return bits, other


def hop(x, ep, sub, masks, turn):
    pairs = [
        (e * sub + s, (e ^ masks[s % 2][turn]) * sub + s) for e in range(ep) for s in range(sub)
    ]
    return lax.ppermute(x, ("ep", "sub"), pairs)


def swap(x):
    return lax.ppermute(x, "sub", [(0, 1), (1, 0)])


def add(*terms):
    total = terms[0].astype(F32)
    for t in terms[1:]:
        total = total + t.astype(F32)
    return total


def on_device(
    queries,
    latent_cache,
    new_latent,
    lengths,
    moe_input,
    gate_scores,
    expert_ids,
    placement,
    w_gate,
    w_up,
    w_down,
):
    ep, sub = lax.axis_size("ep"), lax.axis_size("sub")
    masks = halving_masks(ep)
    turns = len(masks[0])
    width = moe_input.shape[1]
    requests, width = queries.shape[0], moe_input.shape[1]
    inputs = [queries.transpose(0, 1, 3, 2), latent_cache.transpose(0, 2, 1), new_latent]
    chip = lax.axis_index("ep").astype(jnp.int32)[None]
    slots = ep * w_gate.shape[0]
    barrier = lax.optimization_barrier
    chip, gate_scores, lengths = barrier((chip, gate_scores, lengths))

    requests = queries.shape[0]
    half = width // 2
    gate, up, down = [pltpu.with_memory_space_constraint(w, pltpu.VMEM) for w in (w_gate, w_up, w_down)]

    base = route(placement, moe_input, gate_scores, expert_ids, slots)
    for turn in range(turns - 2):
        got = hop(base, ep, sub, masks, turn)
        if turn == 0:
            base, inputs = barrier((base, inputs))
            out, _, _ = attention(lengths, inputs, 0, 0, 2, held=2, loads=())
            got, out, inputs = barrier((got, out, inputs))
        base = jnp.concatenate([base, got], axis=0)

    second = hop(base, ep, sub, masks, turns - 2)
    base, inputs = barrier((base, inputs))
    out, inputs, _ = attention(lengths, inputs, 2, 2, 1, held=requests - 2, previous=out)
    done = 3
    base_late, out = barrier((base, out))
    early = hop(base_late, ep, sub, masks, turns - 1)
    second, out, inputs = barrier((second, out, inputs))
    late = hop(second, ep, sub, masks, turns - 1)
    near_rows = [base, second, swap(base), swap(second)]
    near_rows, early = barrier((near_rows, early))
    early_swap = swap(early)
    near_own, (near_other,) = experts(near_rows, gate, up, down, chip, 1)
    late, early_swap, near_own, near_other = barrier((late, early_swap, near_own, near_other))
    near_back = swap(near_other)
    own, other = experts([early, late, early_swap, swap(late)], gate, up, down, chip, 2)
    sent = [add(x, swap(y)).astype(BF16) for x, y in zip(own, other)]
    totals = [
        barrier(add(near_own[0][:, :half], near_back[:, :half])),
        barrier(add(near_own[0][:, half:], near_back[:, half:])),
    ]
    shares = {turns - 1: 3, 0: requests}
    for turn in range(turns - 1, -1, -1):
        got = [hop(x, ep, sub, masks, turn) for x in sent]
        if turn in shares and done < requests:
            sent, inputs = barrier((sent, inputs))
            count = min(shares[turn], requests - done)
            out, inputs, _ = attention(lengths, inputs, 2, done, count, previous=out)
            done += count
            got[0], out, inputs = barrier((got[0], out, inputs))
        totals = [add(t, g) for t, g in zip(totals, got)]
        if turn:
            keep = totals[0].shape[0] // 2
            sent = [barrier(t[keep:].astype(BF16)) for t in totals]
            totals = [barrier(t[:keep]) for t in totals]
    return out, jnp.concatenate(totals, axis=1).astype(BF16)


def solution(mesh):
    split = ("groups", "ep", "sub")
    return jax.shard_map(
        on_device,
        mesh=mesh,
        in_specs=(
            P(split, None, None, None),
            P(split, None, None),
            P(split, None, None),
            P(split),
            P(split, None),
            P(split, None),
            P(split, None),
            P("groups", None),
            P(("groups", "ep"), None, "sub"),
            P(("groups", "ep"), None, "sub"),
            P(("groups", "ep"), "sub", None),
        ),
        out_specs=(P(split, None, None, None), P(split, None)),
        check_vma=False,
    )
```

```python
import functools

import jax
import jax.numpy as jnp
from jax import lax
from jax.experimental import pallas as pl
from jax.experimental.pallas import tpu as pltpu
from jax.sharding import PartitionSpec as P

LATENT_RANK = 512
SCORE_SCALE = 192.0 ** (-0.5)
ROUTE_SCALE = 2.5
LANES = 128
F32 = jnp.float32
BF16 = jnp.bfloat16
SMALL_COST = pl.CostEstimate(flops=1 << 20, bytes_accessed=1 << 16, transcendentals=0)


def contract(a, b, dim_a, dim_b):
    return lax.dot_general(
        a, b, (((dim_a,), (dim_b,)), ((), ())), preferred_element_type=F32
    )


def attend_request(q_steps, cached, fresh, length):
    heads, context, steps = q_steps[0].shape[1], cached.shape[1], fresh.shape[0]
    q = jnp.concatenate(q_steps, axis=1)
    padded = jnp.concatenate(
        [fresh, jnp.zeros((-steps % 16, fresh.shape[1]), fresh.dtype)], axis=0
    )
    scores = jnp.concatenate([contract(cached, q, 0, 0), contract(padded, q, 1, 0)], axis=0)
    scores = scores * SCORE_SCALE
    key = lax.broadcasted_iota(jnp.int32, scores.shape, 0)
    column = lax.broadcasted_iota(jnp.int32, scores.shape, 1)
    step = key - context
    is_new = jnp.logical_and(step >= 0, jnp.logical_and(step < steps, step * heads <= column))
    is_old = jnp.logical_and(key < context, key < length)
    scores = jnp.where(jnp.logical_or(is_old, is_new), scores, -jnp.inf)
    weights = jnp.exp(scores - jnp.max(scores, axis=0, keepdims=True))
    total = jnp.sum(weights, axis=0, keepdims=True)
    probs = (weights / total).astype(BF16)
    blended = contract(probs[:context], cached[:LATENT_RANK], 0, 1)
    blended = blended + contract(probs[context:], padded[:, :LATENT_RANK], 0, 0)
    return blended.reshape(len(q_steps), heads, LATENT_RANK).astype(BF16)


def attention_kernel(*refs, base, first, count, loads, opening, following):
    length_ref, refs = refs[0], refs[1:]
    sources, refs = refs[:3], refs[3:]
    load_refs, refs = refs[:loads], refs[loads:]
    if following:
        refs = refs[1:]
    out_ref, refs = refs[0], refs[1:]
    if opening:
        resident, refs = refs[:3], refs[3:]
    else:
        resident = sources
    loaded, (result, out_sems, load_sems, in_sems) = refs[:loads], refs[loads:]
    held = resident[0].shape[0]

    needed, copies = [], []
    if opening:
        for lo, hi, group in ((0, first - base + count, 0), (first - base + count, held, 1)):
            if hi == lo:
                continue
            for i in range(3):
                copy = pltpu.make_async_copy(
                    sources[i].at[base + lo : base + hi],
                    resident[i].at[lo:hi],
                    in_sems.at[i, group],
                )
                copy.start()
                (copies if group else needed).append(copy)
    for i, (source, target) in enumerate(zip(load_refs, loaded)):
        copy = pltpu.make_async_copy(source, target, load_sems.at[i])
        copy.start()
        copies.append(copy)
    for copy in needed:
        copy.wait()
    query_ref, cache_ref, new_ref = resident
    steps = query_ref.shape[1]
    for b in range(count):
        r = first - base + b
        result[b] = attend_request(
            [query_ref[r, s] for s in range(steps)], cache_ref[r], new_ref[r], length_ref[first + b]
        )
        copy = pltpu.make_async_copy(result.at[b], out_ref.at[first + b], out_sems.at[b])
        copy.start()
        copies.append(copy)
    for copy in copies:
        copy.wait()


def attention(lengths, inputs, base, first, count, held=0, loads=(), previous=None):
    opening, following = held > 0, previous is not None
    _, steps, latent, heads = inputs[0].shape
    requests = lengths.shape[0]
    vmem = pl.BlockSpec(memory_space=pltpu.VMEM)
    hbm = pl.BlockSpec(memory_space=pl.ANY)
    in_specs = [pl.BlockSpec(memory_space=pltpu.SMEM)]
    in_specs += [hbm if opening else vmem] * 3 + [hbm] * len(loads)
    place = pltpu.HBM if opening else pltpu.VMEM
    operands = [pltpu.with_memory_space_constraint(lengths, pltpu.HBM)]
    operands += [pltpu.with_memory_space_constraint(x, place) for x in inputs]
    operands += [pltpu.with_memory_space_constraint(x, pltpu.HBM) for x in loads]
    aliases = {}
    if following:
        in_specs.append(hbm)
        aliases = {len(operands): 0}
        operands.append(pltpu.with_memory_space_constraint(previous, pltpu.HBM))
    kept = [((held,) + x.shape[1:], x.dtype) for x in inputs] if opening else []
    kept += [(x.shape, x.dtype) for x in loads]
    outs = pl.pallas_call(
        functools.partial(
            attention_kernel,
            base=base,
            first=first,
            count=count,
            loads=len(loads),
            opening=opening,
            following=following,
        ),
        in_specs=in_specs,
        out_specs=[hbm] + [vmem] * len(kept),
        out_shape=[pltpu.HBM((requests, steps, heads, LATENT_RANK), BF16)]
        + [pltpu.VMEM(shape, kind) for shape, kind in kept],
        scratch_shapes=[
            pltpu.VMEM((count, steps, heads, LATENT_RANK), BF16),
            pltpu.SemaphoreType.DMA((count,)),
            pltpu.SemaphoreType.DMA((max(len(loads), 1),)),
            pltpu.SemaphoreType.DMA((3, 2)),
        ],
        input_output_aliases=aliases,
        compiler_params=pltpu.CompilerParams(vmem_limit_bytes=12 << 20),
        cost_estimate=pl.CostEstimate(flops=1 << 32, bytes_accessed=1 << 23, transcendentals=0)
        if opening
        else SMALL_COST,
        name="attention",
    )(*operands)
    kept = list(outs[1:])
    if opening:
        return outs[0], kept[:3], kept[3:]
    return outs[0], list(inputs), kept


def route_kernel(place_ref, rows_ref, score_ref, expert_ref, out_ref, *, experts, slots):
    tokens, width = rows_ref.shape
    sigmoid = jax.nn.sigmoid(score_ref[...])
    weights = ROUTE_SCALE * sigmoid / jnp.sum(sigmoid, axis=0, keepdims=True)
    weights = weights.astype(BF16).astype(F32)
    named = expert_ref[...]
    even = lax.broadcasted_iota(jnp.int32, named.shape, 1) % 2 == 0
    slot = jnp.zeros_like(named)
    for e in range(experts):
        slot = jnp.where(
            named == e, jnp.where(even, place_ref[0, e], place_ref[1, e]), slot
        )
    index = lax.broadcasted_iota(jnp.int32, (LANES, tokens), 0)
    table = jnp.zeros((LANES, tokens), F32)
    for k in range(named.shape[0]):
        table = table + jnp.where(index == slot[k : k + 1], weights[k : k + 1], 0.0)
    row = lax.broadcasted_iota(jnp.int32, (tokens, tokens), 0)
    column = lax.broadcasted_iota(jnp.int32, (tokens, tokens), 1)
    unit = jnp.where(row == column, 1.0, 0.0).astype(BF16)
    out_ref[:, :width] = rows_ref[...]
    out_ref[:, width:] = contract(unit, table.astype(BF16), 1, 1).astype(BF16)


def route(placement, rows, scores, expert_ids, slots):
    tokens, width = rows.shape
    vmem = pl.BlockSpec(memory_space=pltpu.VMEM)
    return pl.pallas_call(
        functools.partial(route_kernel, experts=placement.shape[0], slots=slots),
        in_specs=[pl.BlockSpec(memory_space=pltpu.SMEM), vmem, vmem, vmem],
        out_specs=vmem,
        out_shape=jax.ShapeDtypeStruct((tokens, width + LANES), BF16),
        compiler_params=pltpu.CompilerParams(vmem_limit_bytes=4 << 20),
        name="route",
    )(*(pltpu.with_memory_space_constraint(x, pltpu.HBM) for x in (placement.T, rows, scores.T, expert_ids.T)))


def project(act_s, down_ref, own_ref, other_ref, first, tile):
    slots, hidden, _ = down_ref.shape
    own = own_ref.shape[0]

    def step(i, carry):
        source = pl.ds(pl.multiple_of(first + i * tile, LANES), tile)
        target = pl.ds(pl.multiple_of(i * tile, LANES), tile)
        total = contract(act_s[:, :hidden], down_ref[0, :, source], 1, 0)
        for s in range(1, slots):
            total = total + contract(
                act_s[:, s * hidden : (s + 1) * hidden], down_ref[s, :, source], 1, 0
            )
        own_ref[:, target] = total[:own]
        other_ref[:, target] = total[own:].astype(BF16)
        return carry

    lax.fori_loop(0, own_ref.shape[1] // tile, step, 0)


def experts_kernel(*refs, parts, cuts, tile):
    rows_refs, refs = refs[:parts], refs[parts:]
    (gate_ref, up_ref, down_ref, chip_ref), refs = refs[:4], refs[4:]
    own_refs, other_refs, (rows_s, act_s) = refs[:cuts], refs[cuts : 2 * cuts], refs[2 * cuts :]
    slots, width, hidden = gate_ref.shape
    start = 0
    for ref in rows_refs:
        rows_s[start : start + ref.shape[0], :] = ref[...]
        start += ref.shape[0]
    table = rows_s[:, width:].astype(F32)
    lane = lax.broadcasted_iota(jnp.int32, table.shape, 1)
    for s in range(slots):
        slot = chip_ref[0] * slots + s
        weight = jnp.sum(jnp.where(lane == slot, table, 0.0), axis=1, keepdims=True)
        rows = rows_s[:, :width]
        gate = contract(rows, gate_ref[s], 1, 0)
        up = contract(rows, up_ref[s], 1, 0)
        act = gate / (1.0 + jnp.exp(-gate)) * up
        act_s[:, s * hidden : (s + 1) * hidden] = (weight * act).astype(BF16)
    for i, (own_ref, other_ref) in enumerate(zip(own_refs, other_refs)):
        project(act_s, down_ref, own_ref, other_ref, i * own_ref.shape[1], tile)


def experts(parts, gate, up, down, chip, cuts):
    slots, width, hidden = gate.shape
    count = sum(p.shape[0] for p in parts)
    vmem = pl.BlockSpec(memory_space=pltpu.VMEM)
    shape = (count // 2, width // cuts)
    outs = pl.pallas_call(
        functools.partial(experts_kernel, parts=len(parts), cuts=cuts, tile=width // 4),
        in_specs=[vmem] * (len(parts) + 3) + [pl.BlockSpec(memory_space=pltpu.SMEM)],
        out_specs=[vmem] * (2 * cuts),
        out_shape=[jax.ShapeDtypeStruct(shape, F32)] * cuts
        + [jax.ShapeDtypeStruct(shape, BF16)] * cuts,
        scratch_shapes=[
            pltpu.VMEM((count, parts[0].shape[1]), BF16),
            pltpu.VMEM((count, slots * hidden), BF16),
        ],
        compiler_params=pltpu.CompilerParams(vmem_limit_bytes=16 << 20),
        cost_estimate=SMALL_COST,
        name="experts",
    )(*parts, gate, up, down, chip)
    return outs[:cuts], outs[cuts:]


def halving_masks(ep):
    bits = []
    bit = ep // 2
    while bit:
        bits.append(bit)
        bit //= 2
    other = bits[:-2] + bits[-2:][::-1]
    return bits, other


def hop(x, ep, sub, masks, turn):
    pairs = [
        (e * sub + s, (e ^ masks[s % 2][turn]) * sub + s) for e in range(ep) for s in range(sub)
    ]
    return lax.ppermute(x, ("ep", "sub"), pairs)


def swap(x):
    return lax.ppermute(x, "sub", [(0, 1), (1, 0)])


def add(*terms):
    total = terms[0].astype(F32)
    for t in terms[1:]:
        total = total + t.astype(F32)
    return total


def on_device(
    queries,
    latent_cache,
    new_latent,
    lengths,
    moe_input,
    gate_scores,
    expert_ids,
    placement,
    w_gate,
    w_up,
    w_down,
):
    ep, sub = lax.axis_size("ep"), lax.axis_size("sub")
    masks = halving_masks(ep)
    turns = len(masks[0])
    width = moe_input.shape[1]
    requests, width = queries.shape[0], moe_input.shape[1]
    inputs = [queries.transpose(0, 1, 3, 2), latent_cache.transpose(0, 2, 1), new_latent]
    chip = lax.axis_index("ep").astype(jnp.int32)[None]
    slots = ep * w_gate.shape[0]
    barrier = lax.optimization_barrier
    chip, gate_scores, lengths = barrier((chip, gate_scores, lengths))

    requests = queries.shape[0]
    half = width // 2
    gate, up, down = [pltpu.with_memory_space_constraint(w, pltpu.VMEM) for w in (w_gate, w_up, w_down)]

    own = route(placement, moe_input, gate_scores, expert_ids, slots)
    own, inputs = barrier((own, inputs))
    whole = [pltpu.with_memory_space_constraint(x, pltpu.VMEM) for x in inputs]
    for turn in range(turns - 3):
        own = jnp.concatenate([own, hop(own, ep, sub, masks, turn)], axis=0)
    hop_a, hop_b, hop_c = (
        functools.partial(hop, ep=ep, sub=sub, masks=masks, turn=turn)
        for turn in range(turns - 3, turns)
    )
    a, b, c = hop_a(own), hop_b(own), hop_c(own)
    out, _, _ = attention(lengths, inputs, 0, 0, 1, held=1)
    a, b, c, out, inputs = barrier((a, b, c, out, inputs))
    ab, ac, bc = hop_b(a), hop_c(a), hop_c(b)
    out, _, _ = attention(lengths, inputs, 1, 1, 1, held=1, previous=out)
    ab, out, inputs = barrier((ab, out, inputs))
    abc = hop_c(ab)
    done = 2
    base = jnp.concatenate([own, a], axis=0)
    second = jnp.concatenate([b, ab], axis=0)
    early = jnp.concatenate([c, ac], axis=0)
    near_rows = [base, second, swap(base), swap(second)]
    near_rows, c = barrier((near_rows, c))
    late_swap = swap(bc)
    early_swap = swap(early)
    near_own, (near_other,) = experts(near_rows, gate, up, down, chip, 1)
    abc, early_swap, late_swap, near_own, near_other = barrier(
        (abc, early_swap, late_swap, near_own, near_other)
    )
    near_back = swap(near_other)
    far_rows = [early, bc, abc, early_swap, late_swap, swap(abc)]
    far_own, far_other = experts(far_rows, gate, up, down, chip, 2)
    sent = [add(x, swap(y)).astype(BF16) for x, y in zip(far_own, far_other)]
    totals = [
        barrier(add(near_own[0][:, :half], near_back[:, :half])),
        barrier(add(near_own[0][:, half:], near_back[:, half:])),
    ]
    shares = {turns - 1: 3, 0: requests}
    for turn in range(turns - 1, -1, -1):
        got = [hop(x, ep, sub, masks, turn) for x in sent]
        if turn in shares and done < requests:
            sent, whole = barrier((sent, whole))
            count = min(shares[turn], requests - done)
            out, _, _ = attention(lengths, whole, 0, done, count, previous=out)
            done += count
            got[0], out, whole = barrier((got[0], out, whole))
        totals = [add(t, g) for t, g in zip(totals, got)]
        if turn:
            keep = totals[0].shape[0] // 2
            sent = [barrier(t[keep:].astype(BF16)) for t in totals]
            totals = [barrier(t[:keep]) for t in totals]
    return out, jnp.concatenate(totals, axis=1).astype(BF16)


def solution(mesh):
    split = ("groups", "ep", "sub")
    return jax.shard_map(
        on_device,
        mesh=mesh,
        in_specs=(
            P(split, None, None, None),
            P(split, None, None),
            P(split, None, None),
            P(split),
            P(split, None),
            P(split, None),
            P(split, None),
            P("groups", None),
            P(("groups", "ep"), None, "sub"),
            P(("groups", "ep"), None, "sub"),
            P(("groups", "ep"), "sub", None),
        ),
        out_specs=(P(split, None, None, None), P(split, None)),
        check_vma=False,
    )
```

```python
import functools

import jax
import jax.numpy as jnp
from jax import lax
from jax.experimental import pallas as pl
from jax.experimental.pallas import tpu as pltpu
from jax.sharding import PartitionSpec as P

LATENT_RANK = 512
SCORE_SCALE = 192.0 ** (-0.5)
ROUTE_SCALE = 2.5
LANES = 128
F32 = jnp.float32
BF16 = jnp.bfloat16
SMALL_COST = pl.CostEstimate(flops=1 << 20, bytes_accessed=1 << 16, transcendentals=0)


def contract(a, b, dim_a, dim_b):
    return lax.dot_general(
        a, b, (((dim_a,), (dim_b,)), ((), ())), preferred_element_type=F32
    )


def attend_request(q_steps, cached, fresh, length):
    heads, context, steps = q_steps[0].shape[1], cached.shape[1], fresh.shape[0]
    q = jnp.concatenate(q_steps, axis=1)
    padded = jnp.concatenate(
        [fresh, jnp.zeros((-steps % 16, fresh.shape[1]), fresh.dtype)], axis=0
    )
    scores = jnp.concatenate([contract(cached, q, 0, 0), contract(padded, q, 1, 0)], axis=0)
    scores = scores * SCORE_SCALE
    key = lax.broadcasted_iota(jnp.int32, scores.shape, 0)
    column = lax.broadcasted_iota(jnp.int32, scores.shape, 1)
    step = key - context
    is_new = jnp.logical_and(step >= 0, jnp.logical_and(step < steps, step * heads <= column))
    is_old = jnp.logical_and(key < context, key < length)
    scores = jnp.where(jnp.logical_or(is_old, is_new), scores, -jnp.inf)
    weights = jnp.exp(scores - jnp.max(scores, axis=0, keepdims=True))
    total = jnp.sum(weights, axis=0, keepdims=True)
    probs = (weights / total).astype(BF16)
    blended = contract(probs[:context], cached[:LATENT_RANK], 0, 1)
    blended = blended + contract(probs[context:], padded[:, :LATENT_RANK], 0, 0)
    return blended.reshape(len(q_steps), heads, LATENT_RANK).astype(BF16)


def attention_kernel(length_ref, query_ref, cache_ref, new_ref, *refs, first, count):
    out_ref, result, sems = refs[-3:]
    steps = query_ref.shape[1]
    copies = []
    for b in range(count):
        r = first + b
        result[b] = attend_request(
            [query_ref[r, s] for s in range(steps)], cache_ref[r], new_ref[r], length_ref[r]
        )
        copy = pltpu.make_async_copy(result.at[b], out_ref.at[r], sems.at[b])
        copy.start()
        copies.append(copy)
    for copy in copies:
        copy.wait()


def attention(lengths, inputs, first, count, previous):
    requests, steps, latent, heads = inputs[0].shape
    vmem = pl.BlockSpec(memory_space=pltpu.VMEM)
    hbm = pl.BlockSpec(memory_space=pl.ANY)
    in_specs = [pl.BlockSpec(memory_space=pltpu.SMEM), vmem, vmem, vmem]
    operands = [pltpu.with_memory_space_constraint(lengths, pltpu.HBM)]
    operands += [pltpu.with_memory_space_constraint(x, pltpu.VMEM) for x in inputs]
    aliases = {}
    if previous is not None:
        in_specs.append(hbm)
        aliases = {len(operands): 0}
        operands.append(pltpu.with_memory_space_constraint(previous, pltpu.HBM))
    return pl.pallas_call(
        functools.partial(attention_kernel, first=first, count=count),
        in_specs=in_specs,
        out_specs=hbm,
        out_shape=pltpu.HBM((requests, steps, heads, LATENT_RANK), BF16),
        scratch_shapes=[
            pltpu.VMEM((count, steps, heads, LATENT_RANK), BF16),
            pltpu.SemaphoreType.DMA((count,)),
        ],
        input_output_aliases=aliases,
        compiler_params=pltpu.CompilerParams(vmem_limit_bytes=12 << 20),
        cost_estimate=SMALL_COST,
        name="attention",
    )(*operands)


def route_kernel(place_ref, rows_ref, score_ref, expert_ref, out_ref, *, experts, slots):
    tokens, width = rows_ref.shape
    sigmoid = jax.nn.sigmoid(score_ref[...])
    weights = ROUTE_SCALE * sigmoid / jnp.sum(sigmoid, axis=0, keepdims=True)
    weights = weights.astype(BF16).astype(F32)
    named = expert_ref[...]
    even = lax.broadcasted_iota(jnp.int32, named.shape, 1) % 2 == 0
    slot = jnp.zeros_like(named)
    for e in range(experts):
        slot = jnp.where(
            named == e, jnp.where(even, place_ref[0, e], place_ref[1, e]), slot
        )
    index = lax.broadcasted_iota(jnp.int32, (LANES, tokens), 0)
    table = jnp.zeros((LANES, tokens), F32)
    for k in range(named.shape[0]):
        table = table + jnp.where(index == slot[k : k + 1], weights[k : k + 1], 0.0)
    row = lax.broadcasted_iota(jnp.int32, (tokens, tokens), 0)
    column = lax.broadcasted_iota(jnp.int32, (tokens, tokens), 1)
    unit = jnp.where(row == column, 1.0, 0.0).astype(BF16)
    out_ref[:, :width] = rows_ref[...]
    out_ref[:, width:] = contract(unit, table.astype(BF16), 1, 1).astype(BF16)


def route(placement, rows, scores, expert_ids, slots):
    tokens, width = rows.shape
    vmem = pl.BlockSpec(memory_space=pltpu.VMEM)
    return pl.pallas_call(
        functools.partial(route_kernel, experts=placement.shape[0], slots=slots),
        in_specs=[pl.BlockSpec(memory_space=pltpu.SMEM), vmem, vmem, vmem],
        out_specs=vmem,
        out_shape=jax.ShapeDtypeStruct((tokens, width + LANES), BF16),
        compiler_params=pltpu.CompilerParams(vmem_limit_bytes=4 << 20),
        cost_estimate=pl.CostEstimate(flops=1 << 34, bytes_accessed=1 << 25, transcendentals=0),
        name="route",
    )(*(pltpu.with_memory_space_constraint(x, pltpu.HBM) for x in (placement.T, rows, scores.T, expert_ids.T)))


def experts_kernel(*refs, parts, groups, tile):
    rows_refs, refs = refs[:parts], refs[parts:]
    (gate_ref, up_ref, down_ref, chip_ref), refs = refs[:4], refs[4:]
    out_refs, (rows_s, act_s) = refs[: 2 * groups], refs[2 * groups :]
    slots, width, hidden = gate_ref.shape
    start = 0
    for ref in rows_refs:
        rows_s[start : start + ref.shape[0], :] = ref[...]
        start += ref.shape[0]
    table = rows_s[:, width:].astype(F32)
    lane = lax.broadcasted_iota(jnp.int32, table.shape, 1)
    for s in range(slots):
        slot = chip_ref[0] * slots + s
        weight = jnp.sum(jnp.where(lane == slot, table, 0.0), axis=1, keepdims=True)
        rows = rows_s[:, :width]
        gate = contract(rows, gate_ref[s], 1, 0)
        up = contract(rows, up_ref[s], 1, 0)
        act = gate / (1.0 + jnp.exp(-gate)) * up
        act_s[:, s * hidden : (s + 1) * hidden] = (weight * act).astype(BF16)

    def step(i, carry):
        columns = pl.ds(pl.multiple_of(i * tile, LANES), tile)
        total = contract(act_s[:, :hidden], down_ref[0, :, columns], 1, 0)
        for s in range(1, slots):
            total = total + contract(
                act_s[:, s * hidden : (s + 1) * hidden], down_ref[s, :, columns], 1, 0
            )
        start = 0
        for ref in out_refs:
            ref[:, columns] = total[start : start + ref.shape[0]].astype(ref.dtype)
            start += ref.shape[0]
        return carry

    lax.fori_loop(0, width // tile, step, 0)


def experts(parts, gate, up, down, chip, groups):
    slots, width, hidden = gate.shape
    count = 2 * sum(groups)
    vmem = pl.BlockSpec(memory_space=pltpu.VMEM)
    outs = pl.pallas_call(
        functools.partial(experts_kernel, parts=len(parts), groups=len(groups), tile=width // 4),
        in_specs=[vmem] * (len(parts) + 3) + [pl.BlockSpec(memory_space=pltpu.SMEM)],
        out_specs=[vmem] * (2 * len(groups)),
        out_shape=[
            jax.ShapeDtypeStruct((n, width), kind) for kind in (F32, BF16) for n in groups
        ],
        scratch_shapes=[
            pltpu.VMEM((count, parts[0].shape[1]), BF16),
            pltpu.VMEM((count, slots * hidden), BF16),
        ],
        compiler_params=pltpu.CompilerParams(vmem_limit_bytes=16 << 20),
        cost_estimate=SMALL_COST,
        name="experts",
    )(*parts, gate, up, down, chip)
    return outs[: len(groups)], outs[len(groups) :]


def halving_masks(ep):
    bits = []
    bit = ep // 2
    while bit:
        bits.append(bit)
        bit //= 2
    other = bits[:-2] + bits[-2:][::-1]
    return bits, other


def hop(x, ep, sub, masks, turn):
    pairs = [
        (e * sub + s, (e ^ masks[s % 2][turn]) * sub + s) for e in range(ep) for s in range(sub)
    ]
    return lax.ppermute(x, ("ep", "sub"), pairs)


def swap(x):
    return lax.ppermute(x, "sub", [(0, 1), (1, 0)])


def add(*terms):
    total = terms[0].astype(F32)
    for t in terms[1:]:
        total = total + t.astype(F32)
    return total


def on_device(
    queries,
    latent_cache,
    new_latent,
    lengths,
    moe_input,
    gate_scores,
    expert_ids,
    placement,
    w_gate,
    w_up,
    w_down,
):
    ep, sub = lax.axis_size("ep"), lax.axis_size("sub")
    masks = halving_masks(ep)
    turns = len(masks[0])
    width = moe_input.shape[1]
    requests, width = queries.shape[0], moe_input.shape[1]
    inputs = [queries.transpose(0, 1, 3, 2), latent_cache.transpose(0, 2, 1), new_latent]
    chip = lax.axis_index("ep").astype(jnp.int32)[None]
    slots = ep * w_gate.shape[0]
    barrier = lax.optimization_barrier
    chip, gate_scores, lengths = barrier((chip, gate_scores, lengths))

    requests = queries.shape[0]
    gate, up, down = [pltpu.with_memory_space_constraint(w, pltpu.VMEM) for w in (w_gate, w_up, w_down)]
    inputs = [pltpu.with_memory_space_constraint(x, pltpu.VMEM) for x in inputs]

    out = None
    done = 0

    def attend(count, tie):
        nonlocal out, inputs, done
        count = min(count, requests - done)
        if count == 0:
            return tie
        out = attention(lengths, inputs, done, count, out)
        done += count
        tie, out, inputs = barrier((tie, out, inputs))
        return tie

    own = route(placement, moe_input, gate_scores, expert_ids, slots)
    for turn in range(turns - 3):
        own = jnp.concatenate([own, hop(own, ep, sub, masks, turn)], axis=0)
    hop_a, hop_b, hop_c = (
        functools.partial(hop, ep=ep, sub=sub, masks=masks, turn=turn)
        for turn in range(turns - 3, turns)
    )
    n = own.shape[0]
    own, inputs = barrier((own, inputs))
    a, b, c = attend(2, (hop_a(own), hop_b(own), hop_c(own)))
    ab, ac, bc = hop_b(a), hop_c(a), hop_c(b)
    a, inputs = barrier((a, inputs))
    ab = attend(1, ab)
    abc = hop_c(ab)
    base = jnp.concatenate([own, a], axis=0)
    second = jnp.concatenate([b, ab], axis=0)
    early = jnp.concatenate([c, ac], axis=0)
    near_rows = [base, second, swap(base), swap(second)]
    near_rows, c = barrier((near_rows, c))
    late_swap = swap(bc)
    early_swap = swap(early)
    near_own, near_other = experts(near_rows, gate, up, down, chip, [4 * n])
    abc, early_swap, late_swap, near_own, near_other = barrier(
        (abc, early_swap, late_swap, near_own, near_other)
    )
    near_back = swap(near_other[0])
    far_rows = [early, bc, abc, early_swap, late_swap, swap(abc)]
    far_own, far_other = experts(far_rows, gate, up, down, chip, [3 * n, n])
    near = barrier(add(near_own[0], near_back))

    sent = add(far_own[1], swap(far_other[1])).astype(BF16)
    rest = add(far_own[0], swap(far_other[0])).astype(BF16)
    got_ab = hop_c(sent)
    got = hop_c(rest)
    rest, inputs = barrier((rest, inputs))
    got_ab = attend(2, got_ab)
    sent = add(near[3 * n :], got_ab).astype(BF16)
    got_a = hop_b(sent)
    sent, inputs = barrier((sent, inputs))
    got_a = attend(1, got_a)
    back_b = hop_b(add(near[2 * n : 3 * n], got[2 * n :]).astype(BF16))
    sent = add(near[n : 2 * n], got[n : 2 * n], got_a).astype(BF16)
    back_a = hop_a(sent)
    sent, inputs = barrier((sent, inputs))
    back_a = attend(requests, back_a)
    total = add(near[:n], got[:n], back_b, back_a)
    for turn in range(turns - 4, -1, -1):
        half = total.shape[0] // 2
        total = add(total[:half], hop(total[half:].astype(BF16), ep, sub, masks, turn))
    return out, total.astype(BF16)


def solution(mesh):
    split = ("groups", "ep", "sub")
    return jax.shard_map(
        on_device,
        mesh=mesh,
        in_specs=(
            P(split, None, None, None),
            P(split, None, None),
            P(split, None, None),
            P(split),
            P(split, None),
            P(split, None),
            P(split, None),
            P("groups", None),
            P(("groups", "ep"), None, "sub"),
            P(("groups", "ep"), None, "sub"),
            P(("groups", "ep"), "sub", None),
        ),
        out_specs=(P(split, None, None, None), P(split, None)),
        check_vma=False,
    )
```

```python
import functools

import jax
import jax.numpy as jnp
from jax import lax
from jax.experimental import pallas as pl
from jax.experimental.pallas import tpu as pltpu
from jax.sharding import PartitionSpec as P

LATENT_RANK = 512
SCORE_SCALE = 192.0 ** (-0.5)
ROUTE_SCALE = 2.5
LANES = 128
F32 = jnp.float32
BF16 = jnp.bfloat16
SMALL_COST = pl.CostEstimate(flops=1 << 20, bytes_accessed=1 << 16, transcendentals=0)


def contract(a, b, dim_a, dim_b):
    return lax.dot_general(
        a, b, (((dim_a,), (dim_b,)), ((), ())), preferred_element_type=F32
    )


def attend_request(q_steps, cached, fresh, length):
    heads, context, steps = q_steps[0].shape[1], cached.shape[1], fresh.shape[0]
    q = jnp.concatenate(q_steps, axis=1)
    padded = jnp.concatenate(
        [fresh, jnp.zeros((-steps % 16, fresh.shape[1]), fresh.dtype)], axis=0
    )
    scores = jnp.concatenate([contract(cached, q, 0, 0), contract(padded, q, 1, 0)], axis=0)
    scores = scores * SCORE_SCALE
    key = lax.broadcasted_iota(jnp.int32, scores.shape, 0)
    column = lax.broadcasted_iota(jnp.int32, scores.shape, 1)
    step = key - context
    is_new = jnp.logical_and(step >= 0, jnp.logical_and(step < steps, step * heads <= column))
    is_old = jnp.logical_and(key < context, key < length)
    scores = jnp.where(jnp.logical_or(is_old, is_new), scores, -jnp.inf)
    weights = jnp.exp(scores - jnp.max(scores, axis=0, keepdims=True))
    total = jnp.sum(weights, axis=0, keepdims=True)
    probs = (weights / total).astype(BF16)
    blended = contract(probs[:context], cached[:LATENT_RANK], 0, 1)
    blended = blended + contract(probs[context:], padded[:, :LATENT_RANK], 0, 0)
    return blended.reshape(len(q_steps), heads, LATENT_RANK).astype(BF16)


def attention_kernel(length_ref, query_ref, cache_ref, new_ref, *refs, first, count):
    out_ref, result, sems = refs[-3:]
    steps = query_ref.shape[1]
    copies = []
    for b in range(count):
        r = first + b
        result[b] = attend_request(
            [query_ref[r, s] for s in range(steps)], cache_ref[r], new_ref[r], length_ref[r]
        )
        copy = pltpu.make_async_copy(result.at[b], out_ref.at[r], sems.at[b])
        copy.start()
        copies.append(copy)
    for copy in copies:
        copy.wait()


def attention(lengths, inputs, first, count, previous):
    requests, steps, latent, heads = inputs[0].shape
    vmem = pl.BlockSpec(memory_space=pltpu.VMEM)
    hbm = pl.BlockSpec(memory_space=pl.ANY)
    in_specs = [pl.BlockSpec(memory_space=pltpu.SMEM), vmem, vmem, vmem]
    operands = [pltpu.with_memory_space_constraint(lengths, pltpu.HBM)]
    operands += [pltpu.with_memory_space_constraint(x, pltpu.VMEM) for x in inputs]
    aliases = {}
    if previous is not None:
        in_specs.append(hbm)
        aliases = {len(operands): 0}
        operands.append(pltpu.with_memory_space_constraint(previous, pltpu.HBM))
    return pl.pallas_call(
        functools.partial(attention_kernel, first=first, count=count),
        in_specs=in_specs,
        out_specs=hbm,
        out_shape=pltpu.HBM((requests, steps, heads, LATENT_RANK), BF16),
        scratch_shapes=[
            pltpu.VMEM((count, steps, heads, LATENT_RANK), BF16),
            pltpu.SemaphoreType.DMA((count,)),
        ],
        input_output_aliases=aliases,
        compiler_params=pltpu.CompilerParams(vmem_limit_bytes=12 << 20),
        cost_estimate=SMALL_COST,
        name="attention",
    )(*operands)


def route_kernel(place_ref, rows_ref, score_ref, expert_ref, out_ref, *, experts, slots):
    tokens, width = rows_ref.shape
    sigmoid = jax.nn.sigmoid(score_ref[...])
    weights = ROUTE_SCALE * sigmoid / jnp.sum(sigmoid, axis=0, keepdims=True)
    weights = weights.astype(BF16).astype(F32)
    named = expert_ref[...]
    even = lax.broadcasted_iota(jnp.int32, named.shape, 1) % 2 == 0
    slot = jnp.zeros_like(named)
    for e in range(experts):
        slot = jnp.where(
            named == e, jnp.where(even, place_ref[0, e], place_ref[1, e]), slot
        )
    index = lax.broadcasted_iota(jnp.int32, (LANES, tokens), 0)
    table = jnp.zeros((LANES, tokens), F32)
    for k in range(named.shape[0]):
        table = table + jnp.where(index == slot[k : k + 1], weights[k : k + 1], 0.0)
    row = lax.broadcasted_iota(jnp.int32, (tokens, tokens), 0)
    column = lax.broadcasted_iota(jnp.int32, (tokens, tokens), 1)
    unit = jnp.where(row == column, 1.0, 0.0).astype(BF16)
    out_ref[:, :width] = rows_ref[...]
    out_ref[:, width:] = contract(unit, table.astype(BF16), 1, 1).astype(BF16)


def route(placement, rows, scores, expert_ids, slots):
    tokens, width = rows.shape
    vmem = pl.BlockSpec(memory_space=pltpu.VMEM)
    return pl.pallas_call(
        functools.partial(route_kernel, experts=placement.shape[0], slots=slots),
        in_specs=[pl.BlockSpec(memory_space=pltpu.SMEM), vmem, vmem, vmem],
        out_specs=vmem,
        out_shape=jax.ShapeDtypeStruct((tokens, width + LANES), BF16),
        compiler_params=pltpu.CompilerParams(vmem_limit_bytes=4 << 20),
        cost_estimate=pl.CostEstimate(flops=1 << 34, bytes_accessed=1 << 25, transcendentals=0),
        name="route",
    )(*(pltpu.with_memory_space_constraint(x, pltpu.HBM) for x in (placement.T, rows, scores.T, expert_ids.T)))


def experts_kernel(*refs, parts, groups, tile):
    rows_refs, refs = refs[:parts], refs[parts:]
    (gate_ref, up_ref, down_ref, chip_ref), refs = refs[:4], refs[4:]
    out_refs, (rows_s, act_s) = refs[: 2 * groups], refs[2 * groups :]
    slots, width, hidden = gate_ref.shape
    start = 0
    for ref in rows_refs:
        rows_s[start : start + ref.shape[0], :] = ref[...]
        start += ref.shape[0]
    table = rows_s[:, width:].astype(F32)
    lane = lax.broadcasted_iota(jnp.int32, table.shape, 1)
    for s in range(slots):
        slot = chip_ref[0] * slots + s
        weight = jnp.sum(jnp.where(lane == slot, table, 0.0), axis=1, keepdims=True)
        rows = rows_s[:, :width]
        gate = contract(rows, gate_ref[s], 1, 0)
        up = contract(rows, up_ref[s], 1, 0)
        act = gate / (1.0 + jnp.exp(-gate)) * up
        act_s[:, s * hidden : (s + 1) * hidden] = (weight * act).astype(BF16)

    def step(i, carry):
        columns = pl.ds(pl.multiple_of(i * tile, LANES), tile)
        total = contract(act_s[:, :hidden], down_ref[0, :, columns], 1, 0)
        for s in range(1, slots):
            total = total + contract(
                act_s[:, s * hidden : (s + 1) * hidden], down_ref[s, :, columns], 1, 0
            )
        start = 0
        for ref in out_refs:
            ref[:, columns] = total[start : start + ref.shape[0]].astype(ref.dtype)
            start += ref.shape[0]
        return carry

    lax.fori_loop(0, width // tile, step, 0)


def experts(parts, gate, up, down, chip, groups):
    slots, width, hidden = gate.shape
    count = 2 * sum(groups)
    vmem = pl.BlockSpec(memory_space=pltpu.VMEM)
    outs = pl.pallas_call(
        functools.partial(experts_kernel, parts=len(parts), groups=len(groups), tile=width // 4),
        in_specs=[vmem] * (len(parts) + 3) + [pl.BlockSpec(memory_space=pltpu.SMEM)],
        out_specs=[vmem] * (2 * len(groups)),
        out_shape=[
            jax.ShapeDtypeStruct((n, width), kind) for kind in (F32, BF16) for n in groups
        ],
        scratch_shapes=[
            pltpu.VMEM((count, parts[0].shape[1]), BF16),
            pltpu.VMEM((count, slots * hidden), BF16),
        ],
        compiler_params=pltpu.CompilerParams(vmem_limit_bytes=16 << 20),
        cost_estimate=SMALL_COST,
        name="experts",
    )(*parts, gate, up, down, chip)
    return outs[: len(groups)], outs[len(groups) :]


def halving_masks(ep):
    bits = []
    bit = ep // 2
    while bit:
        bits.append(bit)
        bit //= 2
    other = bits[:-2] + bits[-2:][::-1]
    return bits, other


def hop(x, ep, sub, masks, turn):
    pairs = [
        (e * sub + s, (e ^ masks[s % 2][turn]) * sub + s) for e in range(ep) for s in range(sub)
    ]
    return lax.ppermute(x, ("ep", "sub"), pairs)


def swap(x):
    return lax.ppermute(x, "sub", [(0, 1), (1, 0)])


def add(*terms):
    total = terms[0].astype(F32)
    for t in terms[1:]:
        total = total + t.astype(F32)
    return total


def on_device(
    queries,
    latent_cache,
    new_latent,
    lengths,
    moe_input,
    gate_scores,
    expert_ids,
    placement,
    w_gate,
    w_up,
    w_down,
):
    ep, sub = lax.axis_size("ep"), lax.axis_size("sub")
    masks = halving_masks(ep)
    turns = len(masks[0])
    width = moe_input.shape[1]
    requests, width = queries.shape[0], moe_input.shape[1]
    inputs = [queries.transpose(0, 1, 3, 2), latent_cache.transpose(0, 2, 1), new_latent]
    chip = lax.axis_index("ep").astype(jnp.int32)[None]
    slots = ep * w_gate.shape[0]
    barrier = lax.optimization_barrier
    chip, gate_scores, lengths = barrier((chip, gate_scores, lengths))

    requests = queries.shape[0]
    gate, up, down = [pltpu.with_memory_space_constraint(w, pltpu.VMEM) for w in (w_gate, w_up, w_down)]
    inputs = [pltpu.with_memory_space_constraint(x, pltpu.VMEM) for x in inputs]

    out = None
    done = 0

    def attend(count, tie):
        nonlocal out, inputs, done
        count = min(count, requests - done)
        if count == 0:
            return tie
        out = attention(lengths, inputs, done, count, out)
        done += count
        tie, out, inputs = barrier((tie, out, inputs))
        return tie

    own = route(placement, moe_input, gate_scores, expert_ids, slots)
    for turn in range(turns - 3):
        own = jnp.concatenate([own, hop(own, ep, sub, masks, turn)], axis=0)
    hop_a, hop_b, hop_c = (
        functools.partial(hop, ep=ep, sub=sub, masks=masks, turn=turn)
        for turn in range(turns - 3, turns)
    )
    n = own.shape[0]
    own, inputs = barrier((own, inputs))
    c, b, a = attend(3, (hop_c(own), hop_b(own), hop_a(own)))
    bc, ac, ab = hop_c(b), hop_c(a), hop_b(a)
    near_rows = [jnp.concatenate(x, axis=0) for x in ((own, a), (b, c))]
    near_rows += [swap(x) for x in near_rows]
    near_own, near_other = experts(near_rows, gate, up, down, chip, [4 * n])
    bc, ac, ab, near_own, near_other = barrier((bc, ac, ab, near_own, near_other))
    abc = hop_c(ab)
    ab, inputs = barrier((ab, inputs))
    abc = attend(2, abc)
    near = barrier(add(near_own[0], swap(near_other[0])))
    got_c = hop_c(near[3 * n :].astype(BF16))
    early = jnp.concatenate([ab, ac], axis=0)
    early_swap, late_swap = swap(early), swap(bc)
    abc, early_swap, late_swap, near = barrier((abc, early_swap, late_swap, near))
    far_rows = [early, bc, abc, early_swap, late_swap, swap(abc)]
    far_own, far_other = experts(far_rows, gate, up, down, chip, [3 * n, n])
    far_own, far_other, got_c = barrier((far_own, far_other, got_c))

    sent = add(far_own[1], swap(far_other[1])).astype(BF16)
    far = add(far_own[0], swap(far_other[0]))
    rest = far[n:].astype(BF16)
    got_ab = hop_c(sent)
    got = hop_c(rest)
    rest, inputs = barrier((rest, inputs))
    got_ab = attend(1, got_ab)
    sent = add(far[:n], got_ab).astype(BF16)
    got_a = hop_b(sent)
    got, got_a = barrier((got, got_a))
    sent = add(near[n : 2 * n], got[:n], got_a).astype(BF16)
    sent, got = barrier((sent, got))
    back_a = hop_a(sent)
    back_b = hop_b(add(near[2 * n : 3 * n], got[n:]).astype(BF16))
    sent, inputs = barrier((sent, inputs))
    back_a = attend(requests, back_a)
    total = add(near[:n], got_c, back_b, back_a)
    for turn in range(turns - 4, -1, -1):
        half = total.shape[0] // 2
        total = add(total[:half], hop(total[half:].astype(BF16), ep, sub, masks, turn))
    return out, total.astype(BF16)


def solution(mesh):
    split = ("groups", "ep", "sub")
    return jax.shard_map(
        on_device,
        mesh=mesh,
        in_specs=(
            P(split, None, None, None),
            P(split, None, None),
            P(split, None, None),
            P(split),
            P(split, None),
            P(split, None),
            P(split, None),
            P("groups", None),
            P(("groups", "ep"), None, "sub"),
            P(("groups", "ep"), None, "sub"),
            P(("groups", "ep"), "sub", None),
        ),
        out_specs=(P(split, None, None, None), P(split, None)),
        check_vma=False,
    )
```

```python
import functools

import jax
import jax.numpy as jnp
from jax import lax
from jax.experimental import pallas as pl
from jax.experimental.pallas import tpu as pltpu
from jax.sharding import PartitionSpec as P

LATENT_RANK = 512
SCORE_SCALE = 192.0 ** (-0.5)
ROUTE_SCALE = 2.5
LANES = 128
F32 = jnp.float32
BF16 = jnp.bfloat16
SMALL_COST = pl.CostEstimate(flops=1 << 20, bytes_accessed=1 << 16, transcendentals=0)


def contract(a, b, dim_a, dim_b):
    return lax.dot_general(
        a, b, (((dim_a,), (dim_b,)), ((), ())), preferred_element_type=F32
    )


def attend_request(q_steps, cached, fresh, length):
    heads, context, steps = q_steps[0].shape[1], cached.shape[1], fresh.shape[0]
    q = jnp.concatenate(q_steps, axis=1)
    padded = jnp.concatenate(
        [fresh, jnp.zeros((-steps % 16, fresh.shape[1]), fresh.dtype)], axis=0
    )
    scores = jnp.concatenate([contract(cached, q, 0, 0), contract(padded, q, 1, 0)], axis=0)
    scores = scores * SCORE_SCALE
    key = lax.broadcasted_iota(jnp.int32, scores.shape, 0)
    column = lax.broadcasted_iota(jnp.int32, scores.shape, 1)
    step = key - context
    is_new = jnp.logical_and(step >= 0, jnp.logical_and(step < steps, step * heads <= column))
    is_old = jnp.logical_and(key < context, key < length)
    scores = jnp.where(jnp.logical_or(is_old, is_new), scores, -jnp.inf)
    weights = jnp.exp(scores - jnp.max(scores, axis=0, keepdims=True))
    total = jnp.sum(weights, axis=0, keepdims=True)
    probs = (weights / total).astype(BF16)
    blended = contract(probs[:context], cached[:LATENT_RANK], 0, 1)
    blended = blended + contract(probs[context:], padded[:, :LATENT_RANK], 0, 0)
    return blended.reshape(len(q_steps), heads, LATENT_RANK).astype(BF16)


def attention_kernel(length_ref, query_ref, cache_ref, new_ref, *refs, first, count):
    out_ref, result, sems = refs[-3:]
    steps = query_ref.shape[1]
    copies = []
    for b in range(count):
        r = first + b
        result[b] = attend_request(
            [query_ref[r, s] for s in range(steps)], cache_ref[r], new_ref[r], length_ref[r]
        )
        copy = pltpu.make_async_copy(result.at[b], out_ref.at[r], sems.at[b])
        copy.start()
        copies.append(copy)
    for copy in copies:
        copy.wait()


def attention(lengths, inputs, first, count, previous):
    requests, steps, latent, heads = inputs[0].shape
    vmem = pl.BlockSpec(memory_space=pltpu.VMEM)
    hbm = pl.BlockSpec(memory_space=pl.ANY)
    in_specs = [pl.BlockSpec(memory_space=pltpu.SMEM), vmem, vmem, vmem]
    operands = [pltpu.with_memory_space_constraint(lengths, pltpu.HBM)]
    operands += [pltpu.with_memory_space_constraint(x, pltpu.VMEM) for x in inputs]
    aliases = {}
    if previous is not None:
        in_specs.append(hbm)
        aliases = {len(operands): 0}
        operands.append(pltpu.with_memory_space_constraint(previous, pltpu.HBM))
    return pl.pallas_call(
        functools.partial(attention_kernel, first=first, count=count),
        in_specs=in_specs,
        out_specs=hbm,
        out_shape=pltpu.HBM((requests, steps, heads, LATENT_RANK), BF16),
        scratch_shapes=[
            pltpu.VMEM((count, steps, heads, LATENT_RANK), BF16),
            pltpu.SemaphoreType.DMA((count,)),
        ],
        input_output_aliases=aliases,
        compiler_params=pltpu.CompilerParams(vmem_limit_bytes=12 << 20),
        cost_estimate=SMALL_COST,
        name="attention",
    )(*operands)


def route_kernel(place_ref, rows_ref, score_ref, expert_ref, out_ref, *, experts, slots):
    tokens, width = rows_ref.shape
    sigmoid = jax.nn.sigmoid(score_ref[...])
    weights = ROUTE_SCALE * sigmoid / jnp.sum(sigmoid, axis=0, keepdims=True)
    weights = weights.astype(BF16).astype(F32)
    named = expert_ref[...]
    even = lax.broadcasted_iota(jnp.int32, named.shape, 1) % 2 == 0
    slot = jnp.zeros_like(named)
    for e in range(experts):
        slot = jnp.where(
            named == e, jnp.where(even, place_ref[0, e], place_ref[1, e]), slot
        )
    index = lax.broadcasted_iota(jnp.int32, (LANES, tokens), 0)
    table = jnp.zeros((LANES, tokens), F32)
    for k in range(named.shape[0]):
        table = table + jnp.where(index == slot[k : k + 1], weights[k : k + 1], 0.0)
    row = lax.broadcasted_iota(jnp.int32, (tokens, tokens), 0)
    column = lax.broadcasted_iota(jnp.int32, (tokens, tokens), 1)
    unit = jnp.where(row == column, 1.0, 0.0).astype(BF16)
    out_ref[:, :width] = rows_ref[...]
    out_ref[:, width:] = contract(unit, table.astype(BF16), 1, 1).astype(BF16)


def route(placement, rows, scores, expert_ids, slots):
    tokens, width = rows.shape
    vmem = pl.BlockSpec(memory_space=pltpu.VMEM)
    return pl.pallas_call(
        functools.partial(route_kernel, experts=placement.shape[0], slots=slots),
        in_specs=[pl.BlockSpec(memory_space=pltpu.SMEM), vmem, vmem, vmem],
        out_specs=vmem,
        out_shape=jax.ShapeDtypeStruct((tokens, width + LANES), BF16),
        compiler_params=pltpu.CompilerParams(vmem_limit_bytes=4 << 20),
        cost_estimate=pl.CostEstimate(flops=1 << 34, bytes_accessed=1 << 25, transcendentals=0),
        name="route",
    )(*(pltpu.with_memory_space_constraint(x, pltpu.HBM) for x in (placement.T, rows, scores.T, expert_ids.T)))


def experts_kernel(*refs, parts, groups, tile):
    rows_refs, refs = refs[:parts], refs[parts:]
    (gate_ref, up_ref, down_ref, chip_ref), refs = refs[:4], refs[4:]
    out_refs, (rows_s, act_s) = refs[: 2 * groups], refs[2 * groups :]
    slots, width, hidden = gate_ref.shape
    start = 0
    for ref in rows_refs:
        rows_s[start : start + ref.shape[0], :] = ref[...]
        start += ref.shape[0]
    table = rows_s[:, width:].astype(F32)
    lane = lax.broadcasted_iota(jnp.int32, table.shape, 1)
    for s in range(slots):
        slot = chip_ref[0] * slots + s
        weight = jnp.sum(jnp.where(lane == slot, table, 0.0), axis=1, keepdims=True)
        rows = rows_s[:, :width]
        gate = contract(rows, gate_ref[s], 1, 0)
        up = contract(rows, up_ref[s], 1, 0)
        act = gate / (1.0 + jnp.exp(-gate)) * up
        act_s[:, s * hidden : (s + 1) * hidden] = (weight * act).astype(BF16)

    def step(i, carry):
        columns = pl.ds(pl.multiple_of(i * tile, LANES), tile)
        total = contract(act_s[:, :hidden], down_ref[0, :, columns], 1, 0)
        for s in range(1, slots):
            total = total + contract(
                act_s[:, s * hidden : (s + 1) * hidden], down_ref[s, :, columns], 1, 0
            )
        start = 0
        for ref in out_refs:
            ref[:, columns] = total[start : start + ref.shape[0]].astype(ref.dtype)
            start += ref.shape[0]
        return carry

    lax.fori_loop(0, width // tile, step, 0)


def experts(parts, gate, up, down, chip, groups):
    slots, width, hidden = gate.shape
    count = 2 * sum(groups)
    vmem = pl.BlockSpec(memory_space=pltpu.VMEM)
    outs = pl.pallas_call(
        functools.partial(experts_kernel, parts=len(parts), groups=len(groups), tile=width // 4),
        in_specs=[vmem] * (len(parts) + 3) + [pl.BlockSpec(memory_space=pltpu.SMEM)],
        out_specs=[vmem] * (2 * len(groups)),
        out_shape=[
            jax.ShapeDtypeStruct((n, width), kind) for kind in (F32, BF16) for n in groups
        ],
        scratch_shapes=[
            pltpu.VMEM((count, parts[0].shape[1]), BF16),
            pltpu.VMEM((count, slots * hidden), BF16),
        ],
        compiler_params=pltpu.CompilerParams(vmem_limit_bytes=16 << 20),
        cost_estimate=SMALL_COST,
        name="experts",
    )(*parts, gate, up, down, chip)
    return outs[: len(groups)], outs[len(groups) :]


def halving_masks(ep):
    bits = []
    bit = ep // 2
    while bit:
        bits.append(bit)
        bit //= 2
    other = bits[:-2] + bits[-2:][::-1]
    return bits, other


def hop(x, ep, sub, masks, turn):
    pairs = [
        (e * sub + s, (e ^ masks[s % 2][turn]) * sub + s) for e in range(ep) for s in range(sub)
    ]
    return lax.ppermute(x, ("ep", "sub"), pairs)


def swap(x):
    return lax.ppermute(x, "sub", [(0, 1), (1, 0)])


def add(*terms):
    total = terms[0].astype(F32)
    for t in terms[1:]:
        total = total + t.astype(F32)
    return total


def on_device(
    queries,
    latent_cache,
    new_latent,
    lengths,
    moe_input,
    gate_scores,
    expert_ids,
    placement,
    w_gate,
    w_up,
    w_down,
):
    ep, sub = lax.axis_size("ep"), lax.axis_size("sub")
    masks = halving_masks(ep)
    turns = len(masks[0])
    width = moe_input.shape[1]
    requests, width = queries.shape[0], moe_input.shape[1]
    inputs = [queries.transpose(0, 1, 3, 2), latent_cache.transpose(0, 2, 1), new_latent]
    chip = lax.axis_index("ep").astype(jnp.int32)[None]
    slots = ep * w_gate.shape[0]
    barrier = lax.optimization_barrier
    chip, gate_scores, lengths = barrier((chip, gate_scores, lengths))

    requests = queries.shape[0]
    gate, up, down = [pltpu.with_memory_space_constraint(w, pltpu.VMEM) for w in (w_gate, w_up, w_down)]
    inputs = [pltpu.with_memory_space_constraint(x, pltpu.VMEM) for x in inputs]

    out = None
    done = 0

    def attend(count, tie):
        nonlocal out, inputs, done
        count = min(count, requests - done)
        if count == 0:
            return tie
        out = attention(lengths, inputs, done, count, out)
        done += count
        tie, out, inputs = barrier((tie, out, inputs))
        return tie

    own = route(placement, moe_input, gate_scores, expert_ids, slots)
    for turn in range(turns - 3):
        own = jnp.concatenate([own, hop(own, ep, sub, masks, turn)], axis=0)
    hop_a, hop_b, hop_c = (
        functools.partial(hop, ep=ep, sub=sub, masks=masks, turn=turn)
        for turn in range(turns - 3, turns)
    )
    n = own.shape[0]
    own, inputs = barrier((own, inputs))
    c, b, a = attend(3, (hop_c(own), hop_b(own), hop_a(own)))
    bc, ac, ab = hop_c(b), hop_c(a), hop_b(a)
    near_rows = [jnp.concatenate(x, axis=0) for x in ((own, a), (b, c))]
    near_rows += [swap(x) for x in near_rows]
    near_rows, inputs = barrier((near_rows, inputs))
    ab = attend(1, ab)
    abc = hop_c(ab)
    near_rows, ab_swap, bc, ac = barrier((near_rows, swap(ab), bc, ac))
    ac_swap, bc_swap = swap(ac), swap(bc)
    near_own, near_other = experts(near_rows, gate, up, down, chip, [4 * n])
    abc, ac_swap, bc_swap, near_own, near_other = barrier(
        (abc, ac_swap, bc_swap, near_own, near_other)
    )
    far_rows = [ab, ac, bc, abc, ab_swap, ac_swap, bc_swap, swap(abc)]
    far_own, far_other = experts(far_rows, gate, up, down, chip, [3 * n, n])
    near_other, far_other = barrier((near_other, far_other))

    sent = add(far_own[1], swap(far_other[1])).astype(BF16)
    far = add(far_own[0], swap(far_other[0]))
    rest = far[n:].astype(BF16)
    got_ab = hop_c(sent)
    got = hop_c(rest)
    rest, inputs = barrier((rest, inputs))
    near = add(near_own[0], swap(near_other[0]))
    got_ab, near = attend(1, (got_ab, near))
    sent = add(far[:n], got_ab).astype(BF16)
    got_a = hop_b(sent)
    got, near = barrier((got, near))
    got_c = hop_c(near[3 * n :].astype(BF16))
    got, got_a = barrier((got, got_a))
    sent = add(near[n : 2 * n], got[:n], got_a).astype(BF16)
    sent, got = barrier((sent, got))
    back_a = hop_a(sent)
    back_b = hop_b(add(near[2 * n : 3 * n], got[n:]).astype(BF16))
    sent, inputs = barrier((sent, inputs))
    back_a = attend(requests, back_a)
    total = add(near[:n], got_c, back_b, back_a)
    for turn in range(turns - 4, -1, -1):
        half = total.shape[0] // 2
        total = add(total[:half], hop(total[half:].astype(BF16), ep, sub, masks, turn))
    return out, total.astype(BF16)


def solution(mesh):
    split = ("groups", "ep", "sub")
    return jax.shard_map(
        on_device,
        mesh=mesh,
        in_specs=(
            P(split, None, None, None),
            P(split, None, None),
            P(split, None, None),
            P(split),
            P(split, None),
            P(split, None),
            P(split, None),
            P("groups", None),
            P(("groups", "ep"), None, "sub"),
            P(("groups", "ep"), None, "sub"),
            P(("groups", "ep"), "sub", None),
        ),
        out_specs=(P(split, None, None, None), P(split, None)),
        check_vma=False,
    )
```

```python
import functools

import jax
import jax.numpy as jnp
from jax import lax
from jax.experimental import pallas as pl
from jax.experimental.pallas import tpu as pltpu
from jax.sharding import PartitionSpec as P

LATENT_RANK = 512
SCORE_SCALE = 192.0 ** (-0.5)
ROUTE_SCALE = 2.5
LANES = 128
F32 = jnp.float32
BF16 = jnp.bfloat16
SMALL_COST = pl.CostEstimate(flops=1 << 20, bytes_accessed=1 << 16, transcendentals=0)


def contract(a, b, dim_a, dim_b):
    return lax.dot_general(
        a, b, (((dim_a,), (dim_b,)), ((), ())), preferred_element_type=F32
    )


def attend_request(q_steps, cached, fresh, length):
    heads, context, steps = q_steps[0].shape[1], cached.shape[1], fresh.shape[0]
    q = jnp.concatenate(q_steps, axis=1)
    padded = jnp.concatenate(
        [fresh, jnp.zeros((-steps % 16, fresh.shape[1]), fresh.dtype)], axis=0
    )
    scores = jnp.concatenate([contract(cached, q, 0, 0), contract(padded, q, 1, 0)], axis=0)
    scores = scores * SCORE_SCALE
    key = lax.broadcasted_iota(jnp.int32, scores.shape, 0)
    column = lax.broadcasted_iota(jnp.int32, scores.shape, 1)
    step = key - context
    is_new = jnp.logical_and(step >= 0, jnp.logical_and(step < steps, step * heads <= column))
    is_old = jnp.logical_and(key < context, key < length)
    scores = jnp.where(jnp.logical_or(is_old, is_new), scores, -jnp.inf)
    weights = jnp.exp(scores - jnp.max(scores, axis=0, keepdims=True))
    total = jnp.sum(weights, axis=0, keepdims=True)
    probs = (weights / total).astype(BF16)
    blended = contract(probs[:context], cached[:LATENT_RANK], 0, 1)
    blended = blended + contract(probs[context:], padded[:, :LATENT_RANK], 0, 0)
    return blended.reshape(len(q_steps), heads, LATENT_RANK).astype(BF16)


def attention_kernel(length_ref, query_ref, cache_ref, new_ref, *refs, first, count):
    out_ref, result, sems = refs[-3:]
    steps = query_ref.shape[1]
    copies = []
    for b in range(count):
        r = first + b
        result[b] = attend_request(
            [query_ref[r, s] for s in range(steps)], cache_ref[r], new_ref[r], length_ref[r]
        )
        copy = pltpu.make_async_copy(result.at[b], out_ref.at[r], sems.at[b])
        copy.start()
        copies.append(copy)
    for copy in copies:
        copy.wait()


def attention(lengths, inputs, first, count, previous):
    requests, steps, latent, heads = inputs[0].shape
    vmem = pl.BlockSpec(memory_space=pltpu.VMEM)
    hbm = pl.BlockSpec(memory_space=pl.ANY)
    in_specs = [pl.BlockSpec(memory_space=pltpu.SMEM), vmem, vmem, vmem]
    operands = [pltpu.with_memory_space_constraint(lengths, pltpu.HBM)]
    operands += [pltpu.with_memory_space_constraint(x, pltpu.VMEM) for x in inputs]
    aliases = {}
    if previous is not None:
        in_specs.append(hbm)
        aliases = {len(operands): 0}
        operands.append(pltpu.with_memory_space_constraint(previous, pltpu.HBM))
    return pl.pallas_call(
        functools.partial(attention_kernel, first=first, count=count),
        in_specs=in_specs,
        out_specs=hbm,
        out_shape=pltpu.HBM((requests, steps, heads, LATENT_RANK), BF16),
        scratch_shapes=[
            pltpu.VMEM((count, steps, heads, LATENT_RANK), BF16),
            pltpu.SemaphoreType.DMA((count,)),
        ],
        input_output_aliases=aliases,
        compiler_params=pltpu.CompilerParams(vmem_limit_bytes=12 << 20),
        cost_estimate=SMALL_COST,
        name="attention",
    )(*operands)


def route_kernel(place_ref, rows_ref, score_ref, expert_ref, out_ref, *, experts, slots):
    tokens, width = rows_ref.shape
    sigmoid = jax.nn.sigmoid(score_ref[...])
    weights = ROUTE_SCALE * sigmoid / jnp.sum(sigmoid, axis=0, keepdims=True)
    weights = weights.astype(BF16).astype(F32)
    named = expert_ref[...]
    even = lax.broadcasted_iota(jnp.int32, named.shape, 1) % 2 == 0
    slot = jnp.zeros_like(named)
    for e in range(experts):
        slot = jnp.where(
            named == e, jnp.where(even, place_ref[0, e], place_ref[1, e]), slot
        )
    index = lax.broadcasted_iota(jnp.int32, (LANES, tokens), 0)
    table = jnp.zeros((LANES, tokens), F32)
    for k in range(named.shape[0]):
        table = table + jnp.where(index == slot[k : k + 1], weights[k : k + 1], 0.0)
    row = lax.broadcasted_iota(jnp.int32, (tokens, tokens), 0)
    column = lax.broadcasted_iota(jnp.int32, (tokens, tokens), 1)
    unit = jnp.where(row == column, 1.0, 0.0).astype(BF16)
    out_ref[:, :width] = rows_ref[...]
    out_ref[:, width:] = contract(unit, table.astype(BF16), 1, 1).astype(BF16)


def route(placement, rows, scores, expert_ids, slots):
    tokens, width = rows.shape
    vmem = pl.BlockSpec(memory_space=pltpu.VMEM)
    return pl.pallas_call(
        functools.partial(route_kernel, experts=placement.shape[0], slots=slots),
        in_specs=[pl.BlockSpec(memory_space=pltpu.SMEM), vmem, vmem, vmem],
        out_specs=vmem,
        out_shape=jax.ShapeDtypeStruct((tokens, width + LANES), BF16),
        compiler_params=pltpu.CompilerParams(vmem_limit_bytes=4 << 20),
        cost_estimate=pl.CostEstimate(flops=1 << 34, bytes_accessed=1 << 25, transcendentals=0),
        name="route",
    )(*(pltpu.with_memory_space_constraint(x, pltpu.HBM) for x in (placement.T, rows, scores.T, expert_ids.T)))


def experts_kernel(*refs, parts, groups):
    rows_refs, refs = refs[:parts], refs[parts:]
    (gate_ref, up_ref, down_ref, chip_ref), refs = refs[:4], refs[4:]
    out_refs, (rows_s, act_s) = refs[: 2 * groups], refs[2 * groups :]
    slots, width, hidden = gate_ref.shape
    start = 0
    for ref in rows_refs:
        rows_s[start : start + ref.shape[0], :] = ref[...]
        start += ref.shape[0]
    table = rows_s[:, width:].astype(F32)
    lane = lax.broadcasted_iota(jnp.int32, table.shape, 1)
    for s in range(slots):
        slot = chip_ref[0] * slots + s
        weight = jnp.sum(jnp.where(lane == slot, table, 0.0), axis=1, keepdims=True)
        rows = rows_s[:, :width]
        gate = contract(rows, gate_ref[s], 1, 0)
        up = contract(rows, up_ref[s], 1, 0)
        act = gate / (1.0 + jnp.exp(-gate)) * up
        act_s[:, s * hidden : (s + 1) * hidden] = (weight * act).astype(BF16)

    total = contract(act_s[:, :hidden], down_ref[0], 1, 0)
    for s in range(1, slots):
        total = total + contract(act_s[:, s * hidden : (s + 1) * hidden], down_ref[s], 1, 0)
    start = 0
    for ref in out_refs:
        ref[...] = total[start : start + ref.shape[0]].astype(ref.dtype)
        start += ref.shape[0]


def experts(parts, gate, up, down, chip, groups):
    slots, width, hidden = gate.shape
    count = 2 * sum(groups)
    vmem = pl.BlockSpec(memory_space=pltpu.VMEM)
    outs = pl.pallas_call(
        functools.partial(experts_kernel, parts=len(parts), groups=len(groups)),
        in_specs=[vmem] * (len(parts) + 3) + [pl.BlockSpec(memory_space=pltpu.SMEM)],
        out_specs=[vmem] * (2 * len(groups)),
        out_shape=[
            jax.ShapeDtypeStruct((n, width), kind) for kind in (F32, BF16) for n in groups
        ],
        scratch_shapes=[
            pltpu.VMEM((count, parts[0].shape[1]), BF16),
            pltpu.VMEM((count, slots * hidden), BF16),
        ],
        compiler_params=pltpu.CompilerParams(vmem_limit_bytes=16 << 20),
        cost_estimate=SMALL_COST,
        name="experts",
    )(*parts, gate, up, down, chip)
    return outs[: len(groups)], outs[len(groups) :]


def halving_masks(ep):
    bits = []
    bit = ep // 2
    while bit:
        bits.append(bit)
        bit //= 2
    other = bits[:-2] + bits[-2:][::-1]
    return bits, other


def hop(x, ep, sub, masks, turn):
    pairs = [
        (e * sub + s, (e ^ masks[s % 2][turn]) * sub + s) for e in range(ep) for s in range(sub)
    ]
    return lax.ppermute(x, ("ep", "sub"), pairs)


def swap(x):
    return lax.ppermute(x, "sub", [(0, 1), (1, 0)])


def add(*terms):
    total = terms[0].astype(F32)
    for t in terms[1:]:
        total = total + t.astype(F32)
    return total


def on_device(
    queries,
    latent_cache,
    new_latent,
    lengths,
    moe_input,
    gate_scores,
    expert_ids,
    placement,
    w_gate,
    w_up,
    w_down,
):
    ep, sub = lax.axis_size("ep"), lax.axis_size("sub")
    masks = halving_masks(ep)
    turns = len(masks[0])
    width = moe_input.shape[1]
    requests, width = queries.shape[0], moe_input.shape[1]
    inputs = [queries.transpose(0, 1, 3, 2), latent_cache.transpose(0, 2, 1), new_latent]
    chip = lax.axis_index("ep").astype(jnp.int32)[None]
    slots = ep * w_gate.shape[0]
    barrier = lax.optimization_barrier
    chip, gate_scores, lengths = barrier((chip, gate_scores, lengths))

    requests = queries.shape[0]
    gate, up, down = [pltpu.with_memory_space_constraint(w, pltpu.VMEM) for w in (w_gate, w_up, w_down)]
    inputs = [pltpu.with_memory_space_constraint(x, pltpu.VMEM) for x in inputs]

    out = None
    done = 0

    def attend(count, tie):
        nonlocal out, inputs, done
        count = min(count, requests - done)
        if count == 0:
            return tie
        out = attention(lengths, inputs, done, count, out)
        done += count
        tie, out, inputs = barrier((tie, out, inputs))
        return tie

    own = route(placement, moe_input, gate_scores, expert_ids, slots)
    for turn in range(turns - 3):
        own = jnp.concatenate([own, hop(own, ep, sub, masks, turn)], axis=0)
    hop_a, hop_b, hop_c = (
        functools.partial(hop, ep=ep, sub=sub, masks=masks, turn=turn)
        for turn in range(turns - 3, turns)
    )
    n = own.shape[0]
    own, inputs = barrier((own, inputs))
    c, b, a = attend(3, (hop_c(own), hop_b(own), hop_a(own)))
    bc, ac, ab = hop_c(b), hop_c(a), hop_b(a)
    near_rows = [jnp.concatenate(x, axis=0) for x in ((own, a), (b, c))]
    near_rows += [swap(x) for x in near_rows]
    near_own, near_other = experts(near_rows, gate, up, down, chip, [4 * n])
    bc, ac, ab, near_own, near_other = barrier((bc, ac, ab, near_own, near_other))
    abc = hop_c(ab)
    ab, inputs = barrier((ab, inputs))
    abc = attend(2, abc)
    near = barrier(add(near_own[0], swap(near_other[0])))
    got_c = hop_c(near[3 * n :].astype(BF16))
    early = jnp.concatenate([ab, ac], axis=0)
    early_swap, late_swap = swap(early), swap(bc)
    abc, early_swap, late_swap, near = barrier((abc, early_swap, late_swap, near))
    far_rows = [early, bc, abc, early_swap, late_swap, swap(abc)]
    far_own, far_other = experts(far_rows, gate, up, down, chip, [3 * n, n])
    far_own, far_other, got_c = barrier((far_own, far_other, got_c))

    sent = add(far_own[1], swap(far_other[1])).astype(BF16)
    far = add(far_own[0], swap(far_other[0]))
    rest = far[n:].astype(BF16)
    got_ab = hop_c(sent)
    got = hop_c(rest)
    rest, inputs = barrier((rest, inputs))
    got_ab = attend(1, got_ab)
    sent = add(far[:n], got_ab).astype(BF16)
    got_a = hop_b(sent)
    got, got_a = barrier((got, got_a))
    sent = add(near[n : 2 * n], got[:n], got_a).astype(BF16)
    sent, got = barrier((sent, got))
    back_a = hop_a(sent)
    back_b = hop_b(add(near[2 * n : 3 * n], got[n:]).astype(BF16))
    sent, inputs = barrier((sent, inputs))
    back_a = attend(requests, back_a)
    total = add(near[:n], got_c, back_b, back_a)
    for turn in range(turns - 4, -1, -1):
        half = total.shape[0] // 2
        total = add(total[:half], hop(total[half:].astype(BF16), ep, sub, masks, turn))
    return out, total.astype(BF16)


def solution(mesh):
    split = ("groups", "ep", "sub")
    return jax.shard_map(
        on_device,
        mesh=mesh,
        in_specs=(
            P(split, None, None, None),
            P(split, None, None),
            P(split, None, None),
            P(split),
            P(split, None),
            P(split, None),
            P(split, None),
            P("groups", None),
            P(("groups", "ep"), None, "sub"),
            P(("groups", "ep"), None, "sub"),
            P(("groups", "ep"), "sub", None),
        ),
        out_specs=(P(split, None, None, None), P(split, None)),
        check_vma=False,
    )
```

```python
import functools

import jax
import jax.numpy as jnp
from jax import lax
from jax.experimental import pallas as pl
from jax.experimental.pallas import tpu as pltpu
from jax.sharding import PartitionSpec as P

LATENT_RANK = 512
SCORE_SCALE = 192.0 ** (-0.5)
ROUTE_SCALE = 2.5
LANES = 128
F32 = jnp.float32
BF16 = jnp.bfloat16
SMALL_COST = pl.CostEstimate(flops=1 << 20, bytes_accessed=1 << 16, transcendentals=0)


def contract(a, b, dim_a, dim_b):
    return lax.dot_general(
        a, b, (((dim_a,), (dim_b,)), ((), ())), preferred_element_type=F32
    )


def attend_request(q_steps, cached, fresh, length):
    heads, context, steps = q_steps[0].shape[1], cached.shape[1], fresh.shape[0]
    q = jnp.concatenate(q_steps, axis=1)
    padded = jnp.concatenate(
        [fresh, jnp.zeros((-steps % 16, fresh.shape[1]), fresh.dtype)], axis=0
    )
    scores = jnp.concatenate([contract(cached, q, 0, 0), contract(padded, q, 1, 0)], axis=0)
    scores = scores * SCORE_SCALE
    key = lax.broadcasted_iota(jnp.int32, scores.shape, 0)
    column = lax.broadcasted_iota(jnp.int32, scores.shape, 1)
    step = key - context
    is_new = jnp.logical_and(step >= 0, jnp.logical_and(step < steps, step * heads <= column))
    is_old = jnp.logical_and(key < context, key < length)
    scores = jnp.where(jnp.logical_or(is_old, is_new), scores, -jnp.inf)
    weights = jnp.exp(scores - jnp.max(scores, axis=0, keepdims=True))
    total = jnp.sum(weights, axis=0, keepdims=True)
    probs = (weights / total).astype(BF16)
    blended = contract(probs[:context], cached[:LATENT_RANK], 0, 1)
    blended = blended + contract(probs[context:], padded[:, :LATENT_RANK], 0, 0)
    return blended.reshape(len(q_steps), heads, LATENT_RANK).astype(BF16)


def attention_kernel(length_ref, query_ref, cache_ref, new_ref, *refs, first, count):
    out_ref, result, sems = refs[-3:]
    steps = query_ref.shape[1]
    copies = []
    for b in range(count):
        r = first + b
        result[b] = attend_request(
            [query_ref[r, s] for s in range(steps)], cache_ref[r], new_ref[r], length_ref[r]
        )
        copy = pltpu.make_async_copy(result.at[b], out_ref.at[r], sems.at[b])
        copy.start()
        copies.append(copy)
    for copy in copies:
        copy.wait()


def attention(lengths, inputs, first, count, previous):
    requests, steps, latent, heads = inputs[0].shape
    vmem = pl.BlockSpec(memory_space=pltpu.VMEM)
    hbm = pl.BlockSpec(memory_space=pl.ANY)
    in_specs = [pl.BlockSpec(memory_space=pltpu.SMEM), vmem, vmem, vmem]
    operands = [pltpu.with_memory_space_constraint(lengths, pltpu.HBM)]
    operands += [pltpu.with_memory_space_constraint(x, pltpu.VMEM) for x in inputs]
    aliases = {}
    if previous is not None:
        in_specs.append(hbm)
        aliases = {len(operands): 0}
        operands.append(pltpu.with_memory_space_constraint(previous, pltpu.HBM))
    return pl.pallas_call(
        functools.partial(attention_kernel, first=first, count=count),
        in_specs=in_specs,
        out_specs=hbm,
        out_shape=pltpu.HBM((requests, steps, heads, LATENT_RANK), BF16),
        scratch_shapes=[
            pltpu.VMEM((count, steps, heads, LATENT_RANK), BF16),
            pltpu.SemaphoreType.DMA((count,)),
        ],
        input_output_aliases=aliases,
        compiler_params=pltpu.CompilerParams(vmem_limit_bytes=12 << 20),
        cost_estimate=SMALL_COST,
        name="attention",
    )(*operands)


def route_kernel(place_ref, rows_ref, score_ref, expert_ref, out_ref, table_ref, *, experts):
    tokens, width = rows_ref.shape
    sigmoid = jax.nn.sigmoid(score_ref[...])
    weights = ROUTE_SCALE * sigmoid / jnp.sum(sigmoid, axis=0, keepdims=True)
    weights = weights.astype(BF16).astype(F32)
    named = expert_ref[...]
    even = lax.broadcasted_iota(jnp.int32, named.shape, 1) % 2 == 0
    slot = jnp.zeros_like(named)
    for e in range(experts):
        slot = jnp.where(
            named == e, jnp.where(even, place_ref[0, e], place_ref[1, e]), slot
        )
    index = lax.broadcasted_iota(jnp.int32, (LANES, tokens), 0)
    table = jnp.zeros((LANES, tokens), F32)
    for k in range(named.shape[0]):
        table = table + jnp.where(index == slot[k : k + 1], weights[k : k + 1], 0.0)
    row = lax.broadcasted_iota(jnp.int32, (tokens, tokens), 0)
    column = lax.broadcasted_iota(jnp.int32, (tokens, tokens), 1)
    unit = jnp.where(row == column, 1.0, 0.0).astype(BF16)
    table = contract(unit, table.astype(BF16), 1, 1).astype(BF16)
    out_ref[:, :width] = rows_ref[...]
    out_ref[:, width:] = table
    table_ref[...] = table


def route(placement, rows, scores, expert_ids):
    tokens, width = rows.shape
    vmem = pl.BlockSpec(memory_space=pltpu.VMEM)
    return pl.pallas_call(
        functools.partial(route_kernel, experts=placement.shape[0]),
        in_specs=[pl.BlockSpec(memory_space=pltpu.SMEM), vmem, vmem, vmem],
        out_specs=[vmem] * 2,
        out_shape=[jax.ShapeDtypeStruct((tokens, n), BF16) for n in (width + LANES, LANES)],
        compiler_params=pltpu.CompilerParams(vmem_limit_bytes=4 << 20),
        cost_estimate=pl.CostEstimate(flops=1 << 34, bytes_accessed=1 << 25, transcendentals=0),
        name="route",
    )(*(pltpu.with_memory_space_constraint(x, pltpu.HBM) for x in (placement.T, rows, scores.T, expert_ids.T)))


def experts_kernel(*refs, parts, groups):
    rows_refs, refs = refs[:parts], refs[parts:]
    (gate_ref, up_ref, down_ref, chip_ref), refs = refs[:4], refs[4:]
    out_refs, (rows_s, act_s) = refs[: 2 * groups], refs[2 * groups :]
    slots, width, hidden = gate_ref.shape
    start = 0
    for ref in rows_refs:
        rows_s[start : start + ref.shape[0], :] = ref[...]
        start += ref.shape[0]
    table = rows_s[:, width:].astype(F32)
    lane = lax.broadcasted_iota(jnp.int32, table.shape, 1)
    for s in range(slots):
        slot = chip_ref[0] * slots + s
        weight = jnp.sum(jnp.where(lane == slot, table, 0.0), axis=1, keepdims=True)
        rows = rows_s[:, :width]
        gate = contract(rows, gate_ref[s], 1, 0)
        up = contract(rows, up_ref[s], 1, 0)
        act = gate / (1.0 + jnp.exp(-gate)) * up
        act_s[:, s * hidden : (s + 1) * hidden] = (weight * act).astype(BF16)

    total = contract(act_s[:, :hidden], down_ref[0], 1, 0)
    for s in range(1, slots):
        total = total + contract(act_s[:, s * hidden : (s + 1) * hidden], down_ref[s], 1, 0)
    start = 0
    for ref in out_refs:
        ref[...] = total[start : start + ref.shape[0]].astype(ref.dtype)
        start += ref.shape[0]


def experts(parts, gate, up, down, chip, groups):
    slots, width, hidden = gate.shape
    count = 2 * sum(groups)
    vmem = pl.BlockSpec(memory_space=pltpu.VMEM)
    outs = pl.pallas_call(
        functools.partial(experts_kernel, parts=len(parts), groups=len(groups)),
        in_specs=[vmem] * (len(parts) + 3) + [pl.BlockSpec(memory_space=pltpu.SMEM)],
        out_specs=[vmem] * (2 * len(groups)),
        out_shape=[
            jax.ShapeDtypeStruct((n, width), kind) for kind in (F32, BF16) for n in groups
        ],
        scratch_shapes=[
            pltpu.VMEM((count, parts[0].shape[1]), BF16),
            pltpu.VMEM((count, slots * hidden), BF16),
        ],
        compiler_params=pltpu.CompilerParams(vmem_limit_bytes=16 << 20),
        cost_estimate=SMALL_COST,
        name="experts",
    )(*parts, gate, up, down, chip)
    return outs[: len(groups)], outs[len(groups) :]


def halving_masks(ep):
    bits = []
    bit = ep // 2
    while bit:
        bits.append(bit)
        bit //= 2
    other = bits[:-2] + bits[-2:][::-1]
    return bits, other


def hop(x, ep, sub, masks, turn):
    pairs = [
        (e * sub + s, (e ^ masks[s % 2][turn]) * sub + s) for e in range(ep) for s in range(sub)
    ]
    return lax.ppermute(x, ("ep", "sub"), pairs)


def swap(x):
    return lax.ppermute(x, "sub", [(0, 1), (1, 0)])


def add(*terms):
    total = terms[0].astype(F32)
    for t in terms[1:]:
        total = total + t.astype(F32)
    return total


def on_device(
    queries,
    latent_cache,
    new_latent,
    lengths,
    moe_input,
    gate_scores,
    expert_ids,
    placement,
    w_gate,
    w_up,
    w_down,
):
    ep, sub = lax.axis_size("ep"), lax.axis_size("sub")
    masks = halving_masks(ep)
    turns = len(masks[0])
    width = moe_input.shape[1]
    requests, width = queries.shape[0], moe_input.shape[1]
    inputs = [queries.transpose(0, 1, 3, 2), latent_cache.transpose(0, 2, 1), new_latent]
    chip = lax.axis_index("ep").astype(jnp.int32)[None]
    barrier = lax.optimization_barrier
    chip, gate_scores, lengths = barrier((chip, gate_scores, lengths))

    requests = queries.shape[0]
    gate, up, down = [pltpu.with_memory_space_constraint(w, pltpu.VMEM) for w in (w_gate, w_up, w_down)]
    inputs = [pltpu.with_memory_space_constraint(x, pltpu.VMEM) for x in inputs]

    out = None
    done = 0

    def attend(count, tie):
        nonlocal out, inputs, done
        count = min(count, requests - done)
        if count == 0:
            return tie
        out = attention(lengths, inputs, done, count, out)
        done += count
        tie, out, inputs = barrier((tie, out, inputs))
        return tie

    own, table = route(placement, moe_input, gate_scores, expert_ids)
    a = jnp.concatenate([hop(x, ep, sub, masks, 0) for x in (moe_input, table)], axis=1)
    hop_a, hop_b, hop_c = (
        functools.partial(hop, ep=ep, sub=sub, masks=masks, turn=turn)
        for turn in range(turns - 3, turns)
    )
    if turns > 3:
        own = jnp.concatenate([own, a], axis=0)
        for turn in range(1, turns - 3):
            own = jnp.concatenate([own, hop(own, ep, sub, masks, turn)], axis=0)
        a = hop_a(own)
    n = own.shape[0]
    own, inputs = barrier((own, inputs))
    c = hop_c(own)
    b, a = attend(2, (hop_b(own), a))
    ab, bc, ac = hop_b(a), hop_c(b), hop_c(a)
    near_rows = [jnp.concatenate(x, axis=0) for x in ((own, a), (b, c))]
    near_rows += [swap(x) for x in near_rows]
    near_own, near_other = experts(near_rows, gate, up, down, chip, [4 * n])
    ab, bc, ac, near_own, near_other = barrier((ab, bc, ac, near_own, near_other))
    abc = hop_c(ab)
    ab, inputs = barrier((ab, inputs))
    abc = attend(2, abc)
    near = barrier(add(near_own[0], swap(near_other[0])))
    got_c = hop_c(near[3 * n :].astype(BF16))
    early = jnp.concatenate([ab, ac], axis=0)
    early_swap, late_swap = swap(early), swap(bc)
    abc, early_swap, late_swap, near = barrier((abc, early_swap, late_swap, near))
    far_rows = [early, bc, abc, early_swap, late_swap, swap(abc)]
    far_own, far_other = experts(far_rows, gate, up, down, chip, [3 * n, n])

    sent = add(far_own[1], swap(far_other[1])).astype(BF16)
    far = add(far_own[0], swap(far_other[0]))
    rest = far[n:].astype(BF16)
    got_ab = hop_c(sent)
    got = hop_c(rest)
    rest, inputs = barrier((rest, inputs))
    got_ab = attend(1, got_ab)
    sent = add(far[:n], got_ab).astype(BF16)
    got_a = hop_b(sent)
    got, got_a = barrier((got, got_a))
    sent = add(near[n : 2 * n], got[:n], got_a).astype(BF16)
    sent, got = barrier((sent, got))
    back_a = hop_a(sent)
    back_b = hop_b(add(near[2 * n : 3 * n], got[n:]).astype(BF16))
    sent, inputs = barrier((sent, inputs))
    back_a = attend(requests, back_a)
    total = add(near[:n], got_c, back_b, back_a)
    for turn in range(turns - 4, -1, -1):
        half = total.shape[0] // 2
        total = add(total[:half], hop(total[half:].astype(BF16), ep, sub, masks, turn))
    return out, total.astype(BF16)


def solution(mesh):
    split = ("groups", "ep", "sub")
    return jax.shard_map(
        on_device,
        mesh=mesh,
        in_specs=(
            P(split, None, None, None),
            P(split, None, None),
            P(split, None, None),
            P(split),
            P(split, None),
            P(split, None),
            P(split, None),
            P("groups", None),
            P(("groups", "ep"), None, "sub"),
            P(("groups", "ep"), None, "sub"),
            P(("groups", "ep"), "sub", None),
        ),
        out_specs=(P(split, None, None, None), P(split, None)),
        check_vma=False,
    )
```

```python
import functools

import jax
import jax.numpy as jnp
from jax import lax
from jax.experimental import pallas as pl
from jax.experimental.pallas import tpu as pltpu
from jax.sharding import PartitionSpec as P

LATENT_RANK = 512
SCORE_SCALE = 192.0 ** (-0.5)
ROUTE_SCALE = 2.5
LANES = 128
F32 = jnp.float32
BF16 = jnp.bfloat16
SMALL_COST = pl.CostEstimate(flops=1 << 20, bytes_accessed=1 << 16, transcendentals=0)


def contract(a, b, dim_a, dim_b):
    return lax.dot_general(
        a, b, (((dim_a,), (dim_b,)), ((), ())), preferred_element_type=F32
    )


def attend_request(q_steps, cached, fresh, length):
    heads, context, steps = q_steps[0].shape[1], cached.shape[1], fresh.shape[0]
    q = jnp.concatenate(q_steps, axis=1)
    padded = jnp.concatenate(
        [fresh, jnp.zeros((-steps % 16, fresh.shape[1]), fresh.dtype)], axis=0
    )
    scores = jnp.concatenate([contract(cached, q, 0, 0), contract(padded, q, 1, 0)], axis=0)
    scores = scores * SCORE_SCALE
    key = lax.broadcasted_iota(jnp.int32, scores.shape, 0)
    column = lax.broadcasted_iota(jnp.int32, scores.shape, 1)
    step = key - context
    is_new = jnp.logical_and(step >= 0, jnp.logical_and(step < steps, step * heads <= column))
    is_old = jnp.logical_and(key < context, key < length)
    scores = jnp.where(jnp.logical_or(is_old, is_new), scores, -jnp.inf)
    weights = jnp.exp(scores - jnp.max(scores, axis=0, keepdims=True))
    total = jnp.sum(weights, axis=0, keepdims=True)
    probs = (weights / total).astype(BF16)
    blended = contract(probs[:context], cached[:LATENT_RANK], 0, 1)
    blended = blended + contract(probs[context:], padded[:, :LATENT_RANK], 0, 0)
    return blended.reshape(len(q_steps), heads, LATENT_RANK).astype(BF16)


def attention_kernel(length_ref, query_ref, cache_ref, new_ref, *refs, first, count):
    out_ref, result, sems = refs[-3:]
    steps = query_ref.shape[1]
    copies = []
    for b in range(count):
        r = first + b
        result[b] = attend_request(
            [query_ref[r, s] for s in range(steps)], cache_ref[r], new_ref[r], length_ref[r]
        )
        copy = pltpu.make_async_copy(result.at[b], out_ref.at[r], sems.at[b])
        copy.start()
        copies.append(copy)
    for copy in copies:
        copy.wait()


def attention(lengths, inputs, first, count, previous):
    requests, steps, latent, heads = inputs[0].shape
    vmem = pl.BlockSpec(memory_space=pltpu.VMEM)
    hbm = pl.BlockSpec(memory_space=pl.ANY)
    in_specs = [pl.BlockSpec(memory_space=pltpu.SMEM), vmem, vmem, vmem]
    operands = [pltpu.with_memory_space_constraint(lengths, pltpu.HBM)]
    operands += [pltpu.with_memory_space_constraint(x, pltpu.VMEM) for x in inputs]
    aliases = {}
    if previous is not None:
        in_specs.append(hbm)
        aliases = {len(operands): 0}
        operands.append(pltpu.with_memory_space_constraint(previous, pltpu.HBM))
    return pl.pallas_call(
        functools.partial(attention_kernel, first=first, count=count),
        in_specs=in_specs,
        out_specs=hbm,
        out_shape=pltpu.HBM((requests, steps, heads, LATENT_RANK), BF16),
        scratch_shapes=[
            pltpu.VMEM((count, steps, heads, LATENT_RANK), BF16),
            pltpu.SemaphoreType.DMA((count,)),
        ],
        input_output_aliases=aliases,
        compiler_params=pltpu.CompilerParams(vmem_limit_bytes=12 << 20),
        cost_estimate=SMALL_COST,
        name="attention",
    )(*operands)


def route_kernel(place_ref, rows_ref, score_ref, expert_ref, out_ref, table_ref, *, experts):
    tokens, width = rows_ref.shape
    sigmoid = jax.nn.sigmoid(score_ref[...])
    weights = ROUTE_SCALE * sigmoid / jnp.sum(sigmoid, axis=0, keepdims=True)
    weights = weights.astype(BF16).astype(F32)
    named = expert_ref[...]
    even = lax.broadcasted_iota(jnp.int32, named.shape, 1) % 2 == 0
    slot = jnp.zeros_like(named)
    for e in range(experts):
        slot = jnp.where(
            named == e, jnp.where(even, place_ref[0, e], place_ref[1, e]), slot
        )
    index = lax.broadcasted_iota(jnp.int32, (LANES, tokens), 0)
    table = jnp.zeros((LANES, tokens), F32)
    for k in range(named.shape[0]):
        table = table + jnp.where(index == slot[k : k + 1], weights[k : k + 1], 0.0)
    row = lax.broadcasted_iota(jnp.int32, (tokens, tokens), 0)
    column = lax.broadcasted_iota(jnp.int32, (tokens, tokens), 1)
    unit = jnp.where(row == column, 1.0, 0.0).astype(BF16)
    table = contract(unit, table.astype(BF16), 1, 1).astype(BF16)
    out_ref[:, :width] = rows_ref[...]
    out_ref[:, width:] = table
    table_ref[...] = table


def route(placement, rows, scores, expert_ids):
    tokens, width = rows.shape
    vmem = pl.BlockSpec(memory_space=pltpu.VMEM)
    return pl.pallas_call(
        functools.partial(route_kernel, experts=placement.shape[0]),
        in_specs=[pl.BlockSpec(memory_space=pltpu.SMEM), vmem, vmem, vmem],
        out_specs=[vmem] * 2,
        out_shape=[jax.ShapeDtypeStruct((tokens, n), BF16) for n in (width + LANES, LANES)],
        compiler_params=pltpu.CompilerParams(vmem_limit_bytes=4 << 20),
        cost_estimate=pl.CostEstimate(flops=1 << 34, bytes_accessed=1 << 25, transcendentals=0),
        name="route",
    )(*(pltpu.with_memory_space_constraint(x, pltpu.HBM) for x in (placement.T, rows, scores.T, expert_ids.T)))


def experts_kernel(*refs, parts, groups):
    rows_refs, refs = refs[:parts], refs[parts:]
    (gate_ref, up_ref, down_ref, chip_ref), refs = refs[:4], refs[4:]
    out_refs, (rows_s, act_s) = refs[: 2 * groups], refs[2 * groups :]
    slots, width, hidden = gate_ref.shape
    start = 0
    for ref in rows_refs:
        rows_s[start : start + ref.shape[0], :] = ref[...]
        start += ref.shape[0]
    table = rows_s[:, width:].astype(F32)
    lane = lax.broadcasted_iota(jnp.int32, table.shape, 1)
    for s in range(slots):
        slot = chip_ref[0] * slots + s
        weight = jnp.sum(jnp.where(lane == slot, table, 0.0), axis=1, keepdims=True)
        rows = rows_s[:, :width]
        gate = contract(rows, gate_ref[s], 1, 0)
        up = contract(rows, up_ref[s], 1, 0)
        act = gate / (1.0 + jnp.exp(-gate)) * up
        act_s[:, s * hidden : (s + 1) * hidden] = (weight * act).astype(BF16)

    total = contract(act_s[:, :hidden], down_ref[0], 1, 0)
    for s in range(1, slots):
        total = total + contract(act_s[:, s * hidden : (s + 1) * hidden], down_ref[s], 1, 0)
    start = 0
    for ref in out_refs:
        ref[...] = total[start : start + ref.shape[0]].astype(ref.dtype)
        start += ref.shape[0]


def experts(parts, gate, up, down, chip, groups):
    slots, width, hidden = gate.shape
    count = 2 * sum(groups)
    vmem = pl.BlockSpec(memory_space=pltpu.VMEM)
    outs = pl.pallas_call(
        functools.partial(experts_kernel, parts=len(parts), groups=len(groups)),
        in_specs=[vmem] * (len(parts) + 3) + [pl.BlockSpec(memory_space=pltpu.SMEM)],
        out_specs=[vmem] * (2 * len(groups)),
        out_shape=[
            jax.ShapeDtypeStruct((n, width), kind) for kind in (F32, BF16) for n in groups
        ],
        scratch_shapes=[
            pltpu.VMEM((count, parts[0].shape[1]), BF16),
            pltpu.VMEM((count, slots * hidden), BF16),
        ],
        compiler_params=pltpu.CompilerParams(vmem_limit_bytes=16 << 20),
        cost_estimate=SMALL_COST,
        name="experts",
    )(*parts, gate, up, down, chip)
    return outs[: len(groups)], outs[len(groups) :]


def halving_masks(ep):
    bits = []
    bit = ep // 2
    while bit:
        bits.append(bit)
        bit //= 2
    other = bits[:-2] + bits[-2:][::-1]
    return bits, other


def hop(x, ep, sub, masks, turn):
    pairs = [
        (e * sub + s, (e ^ masks[s % 2][turn]) * sub + s) for e in range(ep) for s in range(sub)
    ]
    return lax.ppermute(x, ("ep", "sub"), pairs)


def swap(x):
    return lax.ppermute(x, "sub", [(0, 1), (1, 0)])


def add(*terms):
    total = terms[0].astype(F32)
    for t in terms[1:]:
        total = total + t.astype(F32)
    return total


def on_device(
    queries,
    latent_cache,
    new_latent,
    lengths,
    moe_input,
    gate_scores,
    expert_ids,
    placement,
    w_gate,
    w_up,
    w_down,
):
    ep, sub = lax.axis_size("ep"), lax.axis_size("sub")
    masks = halving_masks(ep)
    turns = len(masks[0])
    width = moe_input.shape[1]
    requests, width = queries.shape[0], moe_input.shape[1]
    inputs = [queries.transpose(0, 1, 3, 2), latent_cache.transpose(0, 2, 1), new_latent]
    chip = lax.axis_index("ep").astype(jnp.int32)[None]
    barrier = lax.optimization_barrier
    chip, gate_scores, lengths = barrier((chip, gate_scores, lengths))

    requests = queries.shape[0]
    gate, up, down = [pltpu.with_memory_space_constraint(w, pltpu.VMEM) for w in (w_gate, w_up, w_down)]
    inputs = [pltpu.with_memory_space_constraint(x, pltpu.VMEM) for x in inputs]

    out = None
    done = 0

    def attend(count, tie):
        nonlocal out, inputs, done
        count = min(count, requests - done)
        if count == 0:
            return tie
        out = attention(lengths, inputs, done, count, out)
        done += count
        tie, out, inputs = barrier((tie, out, inputs))
        return tie

    own, table = route(placement, moe_input, gate_scores, expert_ids)
    first = [moe_input, table]
    for turn in range(turns - 3):
        got = [hop(x, ep, sub, masks, turn) for x in first]
        first = [jnp.concatenate(x, axis=0) for x in zip(first, got)]
    hop_a, hop_b, hop_c = (
        functools.partial(hop, ep=ep, sub=sub, masks=masks, turn=turn)
        for turn in range(turns - 3, turns)
    )
    if turns > 3:
        own = jnp.concatenate(first, axis=1)
    n = own.shape[0]
    own, inputs = barrier((own, inputs))
    a, b = [[h(x) for x in first] for h in (hop_a, hop_b)]
    c = hop_c(own)
    a, b = attend(2, (a, b))
    a, b = [jnp.concatenate(x, axis=1) for x in (a, b)]
    ab, bc, ac = hop_b(a), hop_c(b), hop_c(a)
    near_rows = [jnp.concatenate(x, axis=0) for x in ((own, a), (b, c))]
    near_rows += [swap(x) for x in near_rows]
    near_own, near_other = experts(near_rows, gate, up, down, chip, [4 * n])
    ab, bc, ac, near_own, near_other = barrier((ab, bc, ac, near_own, near_other))
    abc = hop_c(ab)
    ab, inputs = barrier((ab, inputs))
    abc = attend(2, abc)
    near = barrier(add(near_own[0], swap(near_other[0])))
    got_c = hop_c(near[3 * n :].astype(BF16))
    early = jnp.concatenate([ab, ac], axis=0)
    early_swap, late_swap = swap(early), swap(bc)
    abc, early_swap, late_swap, near = barrier((abc, early_swap, late_swap, near))
    far_rows = [early, bc, abc, early_swap, late_swap, swap(abc)]
    far_own, far_other = experts(far_rows, gate, up, down, chip, [3 * n, n])

    sent = add(far_own[1], swap(far_other[1])).astype(BF16)
    far = add(far_own[0], swap(far_other[0]))
    rest = far[n:].astype(BF16)
    got_ab = hop_c(sent)
    got = hop_c(rest)
    rest, inputs = barrier((rest, inputs))
    got_ab = attend(1, got_ab)
    sent = add(far[:n], got_ab).astype(BF16)
    got_a = hop_b(sent)
    got, got_a = barrier((got, got_a))
    sent = add(near[n : 2 * n], got[:n], got_a).astype(BF16)
    sent, got = barrier((sent, got))
    back_a = hop_a(sent)
    back_b = hop_b(add(near[2 * n : 3 * n], got[n:]).astype(BF16))
    sent, inputs = barrier((sent, inputs))
    back_a = attend(requests, back_a)
    total = add(near[:n], got_c, back_b, back_a)
    for turn in range(turns - 4, -1, -1):
        half = total.shape[0] // 2
        total = add(total[:half], hop(total[half:].astype(BF16), ep, sub, masks, turn))
    return out, total.astype(BF16)


def solution(mesh):
    split = ("groups", "ep", "sub")
    return jax.shard_map(
        on_device,
        mesh=mesh,
        in_specs=(
            P(split, None, None, None),
            P(split, None, None),
            P(split, None, None),
            P(split),
            P(split, None),
            P(split, None),
            P(split, None),
            P("groups", None),
            P(("groups", "ep"), None, "sub"),
            P(("groups", "ep"), None, "sub"),
            P(("groups", "ep"), "sub", None),
        ),
        out_specs=(P(split, None, None, None), P(split, None)),
        check_vma=False,
    )
```

```python
import functools

import jax
import jax.numpy as jnp
from jax import lax
from jax.experimental import pallas as pl
from jax.experimental.pallas import tpu as pltpu
from jax.sharding import PartitionSpec as P

LATENT_RANK = 512
SCORE_SCALE = 192.0 ** (-0.5)
ROUTE_SCALE = 2.5
LANES = 128
F32 = jnp.float32
BF16 = jnp.bfloat16
SMALL_COST = pl.CostEstimate(flops=1 << 20, bytes_accessed=1 << 16, transcendentals=0)


def contract(a, b, dim_a, dim_b):
    return lax.dot_general(
        a, b, (((dim_a,), (dim_b,)), ((), ())), preferred_element_type=F32
    )


def attend_request(q_steps, cached, fresh, length):
    heads, context, steps = q_steps[0].shape[1], cached.shape[1], fresh.shape[0]
    q = jnp.concatenate(q_steps, axis=1)
    padded = jnp.concatenate(
        [fresh, jnp.zeros((-steps % 16, fresh.shape[1]), fresh.dtype)], axis=0
    )
    scores = jnp.concatenate([contract(cached, q, 0, 0), contract(padded, q, 1, 0)], axis=0)
    scores = scores * SCORE_SCALE
    key = lax.broadcasted_iota(jnp.int32, scores.shape, 0)
    column = lax.broadcasted_iota(jnp.int32, scores.shape, 1)
    step = key - context
    is_new = jnp.logical_and(step >= 0, jnp.logical_and(step < steps, step * heads <= column))
    is_old = jnp.logical_and(key < context, key < length)
    scores = jnp.where(jnp.logical_or(is_old, is_new), scores, -jnp.inf)
    weights = jnp.exp(scores - jnp.max(scores, axis=0, keepdims=True))
    total = jnp.sum(weights, axis=0, keepdims=True)
    probs = (weights / total).astype(BF16)
    blended = contract(probs[:context], cached[:LATENT_RANK], 0, 1)
    blended = blended + contract(probs[context:], padded[:, :LATENT_RANK], 0, 0)
    return blended.reshape(len(q_steps), heads, LATENT_RANK).astype(BF16)


def attention_kernel(length_ref, query_ref, cache_ref, new_ref, *refs, first, count):
    out_ref, result, sems = refs[-3:]
    steps = query_ref.shape[1]
    copies = []
    for b in range(count):
        r = first + b
        result[b] = attend_request(
            [query_ref[r, s] for s in range(steps)], cache_ref[r], new_ref[r], length_ref[r]
        )
        copy = pltpu.make_async_copy(result.at[b], out_ref.at[r], sems.at[b])
        copy.start()
        copies.append(copy)
    for copy in copies:
        copy.wait()


def attention(lengths, inputs, first, count, previous):
    requests, steps, latent, heads = inputs[0].shape
    vmem = pl.BlockSpec(memory_space=pltpu.VMEM)
    hbm = pl.BlockSpec(memory_space=pl.ANY)
    in_specs = [pl.BlockSpec(memory_space=pltpu.SMEM), vmem, vmem, vmem]
    operands = [pltpu.with_memory_space_constraint(lengths, pltpu.HBM)]
    operands += [pltpu.with_memory_space_constraint(x, pltpu.VMEM) for x in inputs]
    aliases = {}
    if previous is not None:
        in_specs.append(hbm)
        aliases = {len(operands): 0}
        operands.append(pltpu.with_memory_space_constraint(previous, pltpu.HBM))
    return pl.pallas_call(
        functools.partial(attention_kernel, first=first, count=count),
        in_specs=in_specs,
        out_specs=hbm,
        out_shape=pltpu.HBM((requests, steps, heads, LATENT_RANK), BF16),
        scratch_shapes=[
            pltpu.VMEM((count, steps, heads, LATENT_RANK), BF16),
            pltpu.SemaphoreType.DMA((count,)),
        ],
        input_output_aliases=aliases,
        compiler_params=pltpu.CompilerParams(vmem_limit_bytes=12 << 20),
        cost_estimate=SMALL_COST,
        name="attention",
    )(*operands)


def route_kernel(place_ref, rows_ref, score_ref, expert_ref, out_ref, table_ref, *, experts):
    tokens, width = rows_ref.shape
    sigmoid = jax.nn.sigmoid(score_ref[...])
    weights = ROUTE_SCALE * sigmoid / jnp.sum(sigmoid, axis=0, keepdims=True)
    weights = weights.astype(BF16).astype(F32)
    named = expert_ref[...]
    even = lax.broadcasted_iota(jnp.int32, named.shape, 1) % 2 == 0
    slot = jnp.zeros_like(named)
    for e in range(experts):
        slot = jnp.where(
            named == e, jnp.where(even, place_ref[0, e], place_ref[1, e]), slot
        )
    index = lax.broadcasted_iota(jnp.int32, (LANES, tokens), 0)
    table = jnp.zeros((LANES, tokens), F32)
    for k in range(named.shape[0]):
        table = table + jnp.where(index == slot[k : k + 1], weights[k : k + 1], 0.0)
    row = lax.broadcasted_iota(jnp.int32, (tokens, tokens), 0)
    column = lax.broadcasted_iota(jnp.int32, (tokens, tokens), 1)
    unit = jnp.where(row == column, 1.0, 0.0).astype(BF16)
    table = contract(unit, table.astype(BF16), 1, 1).astype(BF16)
    out_ref[:, :width] = rows_ref[...]
    out_ref[:, width:] = table
    table_ref[...] = table


def route(placement, rows, scores, expert_ids):
    tokens, width = rows.shape
    vmem = pl.BlockSpec(memory_space=pltpu.VMEM)
    return pl.pallas_call(
        functools.partial(route_kernel, experts=placement.shape[0]),
        in_specs=[pl.BlockSpec(memory_space=pltpu.SMEM), vmem, vmem, vmem],
        out_specs=[vmem] * 2,
        out_shape=[jax.ShapeDtypeStruct((tokens, n), BF16) for n in (width + LANES, LANES)],
        compiler_params=pltpu.CompilerParams(vmem_limit_bytes=4 << 20),
        cost_estimate=pl.CostEstimate(flops=1 << 34, bytes_accessed=1 << 25, transcendentals=0),
        name="route",
    )(*(pltpu.with_memory_space_constraint(x, pltpu.HBM) for x in (placement.T, rows, scores.T, expert_ids.T)))


def experts_kernel(*refs, parts, groups):
    rows_refs, refs = refs[:parts], refs[parts:]
    (gate_ref, up_ref, down_ref, chip_ref), refs = refs[:4], refs[4:]
    out_refs, (rows_s, act_s) = refs[: 2 * groups], refs[2 * groups :]
    slots, width, hidden = gate_ref.shape
    start = 0
    for ref in rows_refs:
        rows_s[start : start + ref.shape[0], :] = ref[...]
        start += ref.shape[0]
    table = rows_s[:, width:].astype(F32)
    lane = lax.broadcasted_iota(jnp.int32, table.shape, 1)
    for s in range(slots):
        slot = chip_ref[0] * slots + s
        weight = jnp.sum(jnp.where(lane == slot, table, 0.0), axis=1, keepdims=True)
        rows = rows_s[:, :width]
        gate = contract(rows, gate_ref[s], 1, 0)
        up = contract(rows, up_ref[s], 1, 0)
        act = gate / (1.0 + jnp.exp(-gate)) * up
        act_s[:, s * hidden : (s + 1) * hidden] = (weight * act).astype(BF16)

    total = contract(act_s[:, :hidden], down_ref[0], 1, 0)
    for s in range(1, slots):
        total = total + contract(act_s[:, s * hidden : (s + 1) * hidden], down_ref[s], 1, 0)
    start = 0
    for ref in out_refs:
        ref[...] = total[start : start + ref.shape[0]].astype(ref.dtype)
        start += ref.shape[0]


def experts(parts, gate, up, down, chip, groups):
    slots, width, hidden = gate.shape
    count = 2 * sum(groups)
    vmem = pl.BlockSpec(memory_space=pltpu.VMEM)
    outs = pl.pallas_call(
        functools.partial(experts_kernel, parts=len(parts), groups=len(groups)),
        in_specs=[vmem] * (len(parts) + 3) + [pl.BlockSpec(memory_space=pltpu.SMEM)],
        out_specs=[vmem] * (2 * len(groups)),
        out_shape=[
            jax.ShapeDtypeStruct((n, width), kind) for kind in (F32, BF16) for n in groups
        ],
        scratch_shapes=[
            pltpu.VMEM((count, parts[0].shape[1]), BF16),
            pltpu.VMEM((count, slots * hidden), BF16),
        ],
        compiler_params=pltpu.CompilerParams(vmem_limit_bytes=16 << 20),
        cost_estimate=SMALL_COST,
        name="experts",
    )(*parts, gate, up, down, chip)
    return outs[: len(groups)], outs[len(groups) :]


def halving_masks(ep):
    bits = []
    bit = ep // 2
    while bit:
        bits.append(bit)
        bit //= 2
    other = bits[:-2] + bits[-2:][::-1]
    return bits, other


def hop(x, ep, sub, masks, turn):
    pairs = [
        (e * sub + s, (e ^ masks[s % 2][turn]) * sub + s) for e in range(ep) for s in range(sub)
    ]
    return lax.ppermute(x, ("ep", "sub"), pairs)


def swap(x):
    return lax.ppermute(x, "sub", [(0, 1), (1, 0)])


def add(*terms):
    total = terms[0].astype(F32)
    for t in terms[1:]:
        total = total + t.astype(F32)
    return total


def on_device(
    queries,
    latent_cache,
    new_latent,
    lengths,
    moe_input,
    gate_scores,
    expert_ids,
    placement,
    w_gate,
    w_up,
    w_down,
):
    ep, sub = lax.axis_size("ep"), lax.axis_size("sub")
    masks = halving_masks(ep)
    turns = len(masks[0])
    width = moe_input.shape[1]
    requests, width = queries.shape[0], moe_input.shape[1]
    inputs = [queries.transpose(0, 1, 3, 2), latent_cache.transpose(0, 2, 1), new_latent]
    chip = lax.axis_index("ep").astype(jnp.int32)[None]
    barrier = lax.optimization_barrier
    chip, gate_scores, lengths = barrier((chip, gate_scores, lengths))

    requests = queries.shape[0]
    gate, up, down = [pltpu.with_memory_space_constraint(w, pltpu.VMEM) for w in (w_gate, w_up, w_down)]
    inputs = [pltpu.with_memory_space_constraint(x, pltpu.VMEM) for x in inputs]

    out = None
    done = 0

    def attend(count, tie):
        nonlocal out, inputs, done
        count = min(count, requests - done)
        if count == 0:
            return tie
        out = attention(lengths, inputs, done, count, out)
        done += count
        tie, out, inputs = barrier((tie, out, inputs))
        return tie

    own, table = route(placement, moe_input, gate_scores, expert_ids)
    a = jnp.concatenate([hop(x, ep, sub, masks, 0) for x in (moe_input, table)], axis=1)
    hop_a, hop_b, hop_c = (
        functools.partial(hop, ep=ep, sub=sub, masks=masks, turn=turn)
        for turn in range(turns - 3, turns)
    )
    if turns > 3:
        own = jnp.concatenate([own, a], axis=0)
        for turn in range(1, turns - 3):
            own = jnp.concatenate([own, hop(own, ep, sub, masks, turn)], axis=0)
        a = hop_a(own)
    n = own.shape[0]
    own, inputs = barrier((own, inputs))
    c = hop_c(own)
    b, a = attend(3, (hop_b(own), a))
    ab, bc, ac = hop_b(a), hop_c(b), hop_c(a)
    near_rows = [jnp.concatenate(x, axis=0) for x in ((own, a), (b, c))]
    near_rows += [swap(x) for x in near_rows]
    near_own, near_other = experts(near_rows, gate, up, down, chip, [4 * n])
    ab, bc, ac, near_own, near_other = barrier((ab, bc, ac, near_own, near_other))
    abc = hop_c(ab)
    ab, inputs = barrier((ab, inputs))
    abc = attend(2, abc)
    near = barrier(add(near_own[0], swap(near_other[0])))
    got_c = hop_c(near[3 * n :].astype(BF16))
    early = jnp.concatenate([ab, ac], axis=0)
    early_swap, late_swap = swap(early), swap(bc)
    abc, early_swap, late_swap, near = barrier((abc, early_swap, late_swap, near))
    far_rows = [early, bc, abc, early_swap, late_swap, swap(abc)]
    far_own, far_other = experts(far_rows, gate, up, down, chip, [3 * n, n])

    sent = add(far_own[1], swap(far_other[1])).astype(BF16)
    far = add(far_own[0], swap(far_other[0]))
    rest = far[n:].astype(BF16)
    got_ab = hop_c(sent)
    got = hop_c(rest)
    sent = add(far[:n], got_ab).astype(BF16)
    got_a = hop_b(sent)
    sent, inputs = barrier((sent, inputs))
    got_a = attend(1, got_a)
    got, got_a = barrier((got, got_a))
    sent = add(near[n : 2 * n], got[:n], got_a).astype(BF16)
    sent, got = barrier((sent, got))
    back_a = hop_a(sent)
    back_b = hop_b(add(near[2 * n : 3 * n], got[n:]).astype(BF16))
    sent, inputs = barrier((sent, inputs))
    back_a = attend(requests, back_a)
    total = add(near[:n], got_c, back_b, back_a)
    for turn in range(turns - 4, -1, -1):
        half = total.shape[0] // 2
        total = add(total[:half], hop(total[half:].astype(BF16), ep, sub, masks, turn))
    return out, total.astype(BF16)


def solution(mesh):
    split = ("groups", "ep", "sub")
    return jax.shard_map(
        on_device,
        mesh=mesh,
        in_specs=(
            P(split, None, None, None),
            P(split, None, None),
            P(split, None, None),
            P(split),
            P(split, None),
            P(split, None),
            P(split, None),
            P("groups", None),
            P(("groups", "ep"), None, "sub"),
            P(("groups", "ep"), None, "sub"),
            P(("groups", "ep"), "sub", None),
        ),
        out_specs=(P(split, None, None, None), P(split, None)),
        check_vma=False,
    )
```

```python
import functools

import jax
import jax.numpy as jnp
from jax import lax
from jax.experimental import pallas as pl
from jax.experimental.pallas import tpu as pltpu
from jax.sharding import PartitionSpec as P

LATENT_RANK = 512
SCORE_SCALE = 192.0 ** (-0.5)
ROUTE_SCALE = 2.5
LANES = 128
F32 = jnp.float32
BF16 = jnp.bfloat16
SMALL_COST = pl.CostEstimate(flops=1 << 20, bytes_accessed=1 << 16, transcendentals=0)


def contract(a, b, dim_a, dim_b):
    return lax.dot_general(
        a, b, (((dim_a,), (dim_b,)), ((), ())), preferred_element_type=F32
    )


def attend_request(q_steps, cached, fresh, length):
    heads, context, steps = q_steps[0].shape[1], cached.shape[1], fresh.shape[0]
    q = jnp.concatenate(q_steps, axis=1)
    padded = jnp.concatenate(
        [fresh, jnp.zeros((-steps % 16, fresh.shape[1]), fresh.dtype)], axis=0
    )
    scores = jnp.concatenate([contract(cached, q, 0, 0), contract(padded, q, 1, 0)], axis=0)
    scores = scores * SCORE_SCALE
    key = lax.broadcasted_iota(jnp.int32, scores.shape, 0)
    column = lax.broadcasted_iota(jnp.int32, scores.shape, 1)
    step = key - context
    is_new = jnp.logical_and(step >= 0, jnp.logical_and(step < steps, step * heads <= column))
    is_old = jnp.logical_and(key < context, key < length)
    scores = jnp.where(jnp.logical_or(is_old, is_new), scores, -jnp.inf)
    weights = jnp.exp(scores - jnp.max(scores, axis=0, keepdims=True))
    total = jnp.sum(weights, axis=0, keepdims=True)
    probs = (weights / total).astype(BF16)
    blended = contract(probs[:context], cached[:LATENT_RANK], 0, 1)
    blended = blended + contract(probs[context:], padded[:, :LATENT_RANK], 0, 0)
    return blended.reshape(len(q_steps), heads, LATENT_RANK).astype(BF16)


def attention_kernel(length_ref, query_ref, cache_ref, new_ref, *refs, first, count):
    out_ref, result, sems = refs[-3:]
    steps = query_ref.shape[1]
    copies = []
    for b in range(count):
        r = first + b
        result[b] = attend_request(
            [query_ref[r, s] for s in range(steps)], cache_ref[r], new_ref[r], length_ref[r]
        )
        copy = pltpu.make_async_copy(result.at[b], out_ref.at[r], sems.at[b])
        copy.start()
        copies.append(copy)
    for copy in copies:
        copy.wait()


def attention(lengths, inputs, first, count, previous):
    requests, steps, latent, heads = inputs[0].shape
    vmem = pl.BlockSpec(memory_space=pltpu.VMEM)
    hbm = pl.BlockSpec(memory_space=pl.ANY)
    in_specs = [pl.BlockSpec(memory_space=pltpu.SMEM), vmem, vmem, vmem]
    operands = [pltpu.with_memory_space_constraint(lengths, pltpu.HBM)]
    operands += [pltpu.with_memory_space_constraint(x, pltpu.VMEM) for x in inputs]
    aliases = {}
    if previous is not None:
        in_specs.append(hbm)
        aliases = {len(operands): 0}
        operands.append(pltpu.with_memory_space_constraint(previous, pltpu.HBM))
    return pl.pallas_call(
        functools.partial(attention_kernel, first=first, count=count),
        in_specs=in_specs,
        out_specs=hbm,
        out_shape=pltpu.HBM((requests, steps, heads, LATENT_RANK), BF16),
        scratch_shapes=[
            pltpu.VMEM((count, steps, heads, LATENT_RANK), BF16),
            pltpu.SemaphoreType.DMA((count,)),
        ],
        input_output_aliases=aliases,
        compiler_params=pltpu.CompilerParams(vmem_limit_bytes=12 << 20),
        cost_estimate=SMALL_COST,
        name="attention",
    )(*operands)


def route_kernel(place_ref, rows_ref, score_ref, expert_ref, out_ref, *, experts, slots):
    tokens, width = rows_ref.shape
    sigmoid = jax.nn.sigmoid(score_ref[...])
    weights = ROUTE_SCALE * sigmoid / jnp.sum(sigmoid, axis=0, keepdims=True)
    weights = weights.astype(BF16).astype(F32)
    named = expert_ref[...]
    even = lax.broadcasted_iota(jnp.int32, named.shape, 1) % 2 == 0
    slot = jnp.zeros_like(named)
    for e in range(experts):
        slot = jnp.where(
            named == e, jnp.where(even, place_ref[0, e], place_ref[1, e]), slot
        )
    index = lax.broadcasted_iota(jnp.int32, (LANES, tokens), 0)
    table = jnp.zeros((LANES, tokens), F32)
    for k in range(named.shape[0]):
        table = table + jnp.where(index == slot[k : k + 1], weights[k : k + 1], 0.0)
    row = lax.broadcasted_iota(jnp.int32, (tokens, tokens), 0)
    column = lax.broadcasted_iota(jnp.int32, (tokens, tokens), 1)
    unit = jnp.where(row == column, 1.0, 0.0).astype(BF16)
    out_ref[:, :width] = rows_ref[...]
    out_ref[:, width:] = contract(unit, table.astype(BF16), 1, 1).astype(BF16)


def route(placement, rows, scores, expert_ids, slots):
    tokens, width = rows.shape
    vmem = pl.BlockSpec(memory_space=pltpu.VMEM)
    return pl.pallas_call(
        functools.partial(route_kernel, experts=placement.shape[0], slots=slots),
        in_specs=[pl.BlockSpec(memory_space=pltpu.SMEM), vmem, vmem, vmem],
        out_specs=vmem,
        out_shape=jax.ShapeDtypeStruct((tokens, width + LANES), BF16),
        compiler_params=pltpu.CompilerParams(vmem_limit_bytes=4 << 20),
        cost_estimate=pl.CostEstimate(flops=1 << 34, bytes_accessed=1 << 25, transcendentals=0),
        name="route",
    )(*(pltpu.with_memory_space_constraint(x, pltpu.HBM) for x in (placement.T, rows, scores.T, expert_ids.T)))


def experts_kernel(*refs, parts, groups):
    rows_refs, refs = refs[:parts], refs[parts:]
    (gate_ref, up_ref, down_ref, chip_ref), refs = refs[:4], refs[4:]
    out_refs, (rows_s, act_s) = refs[: 2 * groups], refs[2 * groups :]
    slots, width, hidden = gate_ref.shape
    start = 0
    for ref in rows_refs:
        rows_s[start : start + ref.shape[0], :] = ref[...]
        start += ref.shape[0]
    table = rows_s[:, width:].astype(F32)
    lane = lax.broadcasted_iota(jnp.int32, table.shape, 1)
    for s in range(slots):
        slot = chip_ref[0] * slots + s
        weight = jnp.sum(jnp.where(lane == slot, table, 0.0), axis=1, keepdims=True)
        rows = rows_s[:, :width]
        gate = contract(rows, gate_ref[s], 1, 0)
        up = contract(rows, up_ref[s], 1, 0)
        act = gate / (1.0 + jnp.exp(-gate)) * up
        act_s[:, s * hidden : (s + 1) * hidden] = (weight * act).astype(BF16)

    total = contract(act_s[:, :hidden], down_ref[0], 1, 0)
    for s in range(1, slots):
        total = total + contract(act_s[:, s * hidden : (s + 1) * hidden], down_ref[s], 1, 0)
    start = 0
    for ref in out_refs:
        ref[...] = total[start : start + ref.shape[0]].astype(ref.dtype)
        start += ref.shape[0]


def experts(parts, gate, up, down, chip, groups):
    slots, width, hidden = gate.shape
    count = 2 * sum(groups)
    vmem = pl.BlockSpec(memory_space=pltpu.VMEM)
    outs = pl.pallas_call(
        functools.partial(experts_kernel, parts=len(parts), groups=len(groups)),
        in_specs=[vmem] * (len(parts) + 3) + [pl.BlockSpec(memory_space=pltpu.SMEM)],
        out_specs=[vmem] * (2 * len(groups)),
        out_shape=[
            jax.ShapeDtypeStruct((n, width), kind) for kind in (F32, BF16) for n in groups
        ],
        scratch_shapes=[
            pltpu.VMEM((count, parts[0].shape[1]), BF16),
            pltpu.VMEM((count, slots * hidden), BF16),
        ],
        compiler_params=pltpu.CompilerParams(vmem_limit_bytes=16 << 20),
        cost_estimate=SMALL_COST,
        name="experts",
    )(*parts, gate, up, down, chip)
    return outs[: len(groups)], outs[len(groups) :]


def halving_masks(ep):
    bits = []
    bit = ep // 2
    while bit:
        bits.append(bit)
        bit //= 2
    other = bits[:-2] + bits[-2:][::-1]
    return bits, other


def hop(x, ep, sub, masks, turn):
    pairs = [
        (e * sub + s, (e ^ masks[s % 2][turn]) * sub + s) for e in range(ep) for s in range(sub)
    ]
    return lax.ppermute(x, ("ep", "sub"), pairs)


def swap(x):
    return lax.ppermute(x, "sub", [(0, 1), (1, 0)])


def add(*terms):
    total = terms[0].astype(F32)
    for t in terms[1:]:
        total = total + t.astype(F32)
    return total


def on_device(
    queries,
    latent_cache,
    new_latent,
    lengths,
    moe_input,
    gate_scores,
    expert_ids,
    placement,
    w_gate,
    w_up,
    w_down,
):
    ep, sub = lax.axis_size("ep"), lax.axis_size("sub")
    masks = halving_masks(ep)
    turns = len(masks[0])
    width = moe_input.shape[1]
    requests, width = queries.shape[0], moe_input.shape[1]
    inputs = [queries.transpose(0, 1, 3, 2), latent_cache.transpose(0, 2, 1), new_latent]
    chip = lax.axis_index("ep").astype(jnp.int32)[None]
    slots = ep * w_gate.shape[0]
    barrier = lax.optimization_barrier
    chip, gate_scores, lengths = barrier((chip, gate_scores, lengths))

    requests = queries.shape[0]
    gate, up, down = [pltpu.with_memory_space_constraint(w, pltpu.VMEM) for w in (w_gate, w_up, w_down)]
    inputs = [pltpu.with_memory_space_constraint(x, pltpu.VMEM) for x in inputs]

    out = None
    done = 0

    def attend(count, tie):
        nonlocal out, inputs, done
        count = min(count, requests - done)
        if count == 0:
            return tie
        out = attention(lengths, inputs, done, count, out)
        done += count
        tie, out, inputs = barrier((tie, out, inputs))
        return tie

    own = route(placement, moe_input, gate_scores, expert_ids, slots)
    for turn in range(turns - 3):
        own = jnp.concatenate([own, hop(own, ep, sub, masks, turn)], axis=0)
    hop_a, hop_b, hop_c = (
        functools.partial(hop, ep=ep, sub=sub, masks=masks, turn=turn)
        for turn in range(turns - 3, turns)
    )
    n = own.shape[0]
    own, inputs = barrier((own, inputs))
    c, b, a = attend(3, (hop_c(own), hop_b(own), hop_a(own)))
    bc, ac, ab = hop_c(b), hop_c(a), hop_b(a)
    near_rows = [jnp.concatenate(x, axis=0) for x in ((own, a), (b, c))]
    near_rows += [swap(x) for x in near_rows]
    near_own, near_other = experts(near_rows, gate, up, down, chip, [4 * n])
    bc, ac, ab, near_own, near_other = barrier((bc, ac, ab, near_own, near_other))
    abc = hop_c(ab)
    ab, inputs = barrier((ab, inputs))
    abc = attend(2, abc)
    near = barrier(add(near_own[0], swap(near_other[0])))
    got_c = hop_c(near[3 * n :].astype(BF16))
    early = jnp.concatenate([ab, ac], axis=0)
    early_swap, late_swap = swap(early), swap(bc)
    abc, early_swap, late_swap, near = barrier((abc, early_swap, late_swap, near))
    far_rows = [early, bc, abc, early_swap, late_swap, swap(abc)]
    far_own, far_other = experts(far_rows, gate, up, down, chip, [3 * n, n])

    sent = add(far_own[1], swap(far_other[1])).astype(BF16)
    far = add(far_own[0], swap(far_other[0]))
    rest = far[n:].astype(BF16)
    got_ab = hop_c(sent)
    got = hop_c(rest)
    rest, inputs = barrier((rest, inputs))
    got_ab = attend(1, got_ab)
    sent = add(far[:n], got_ab).astype(BF16)
    got_a = hop_b(sent)
    got, got_a = barrier((got, got_a))
    sent = add(near[n : 2 * n], got[:n], got_a).astype(BF16)
    sent, got = barrier((sent, got))
    back_a = hop_a(sent)
    back_b = hop_b(add(near[2 * n : 3 * n], got[n:]).astype(BF16))
    sent, inputs = barrier((sent, inputs))
    back_a = attend(requests, back_a)
    total = add(near[:n], got_c, back_b, back_a)
    for turn in range(turns - 4, -1, -1):
        half = total.shape[0] // 2
        total = add(total[:half], hop(total[half:].astype(BF16), ep, sub, masks, turn))
    return out, total.astype(BF16)


def solution(mesh):
    split = ("groups", "ep", "sub")
    return jax.shard_map(
        on_device,
        mesh=mesh,
        in_specs=(
            P(split, None, None, None),
            P(split, None, None),
            P(split, None, None),
            P(split),
            P(split, None),
            P(split, None),
            P(split, None),
            P("groups", None),
            P(("groups", "ep"), None, "sub"),
            P(("groups", "ep"), None, "sub"),
            P(("groups", "ep"), "sub", None),
        ),
        out_specs=(P(split, None, None, None), P(split, None)),
        check_vma=False,
    )
```

```python
import functools

import jax
import jax.numpy as jnp
from jax import lax
from jax.experimental import pallas as pl
from jax.experimental.pallas import tpu as pltpu
from jax.sharding import PartitionSpec as P

LATENT_RANK = 512
SCORE_SCALE = 192.0 ** (-0.5)
ROUTE_SCALE = 2.5
LANES = 128
F32 = jnp.float32
BF16 = jnp.bfloat16
SMALL_COST = pl.CostEstimate(flops=1 << 20, bytes_accessed=1 << 16, transcendentals=0)


def contract(a, b, dim_a, dim_b):
    return lax.dot_general(
        a, b, (((dim_a,), (dim_b,)), ((), ())), preferred_element_type=F32
    )


def attend_request(q_steps, cached, fresh, length):
    heads, context, steps = q_steps[0].shape[1], cached.shape[1], fresh.shape[0]
    q = jnp.concatenate(q_steps, axis=1)
    padded = jnp.concatenate(
        [fresh, jnp.zeros((-steps % 16, fresh.shape[1]), fresh.dtype)], axis=0
    )
    scores = jnp.concatenate([contract(cached, q, 0, 0), contract(padded, q, 1, 0)], axis=0)
    scores = scores * SCORE_SCALE
    key = lax.broadcasted_iota(jnp.int32, scores.shape, 0)
    column = lax.broadcasted_iota(jnp.int32, scores.shape, 1)
    step = key - context
    is_new = jnp.logical_and(step >= 0, jnp.logical_and(step < steps, step * heads <= column))
    is_old = jnp.logical_and(key < context, key < length)
    scores = jnp.where(jnp.logical_or(is_old, is_new), scores, -jnp.inf)
    weights = jnp.exp(scores - jnp.max(scores, axis=0, keepdims=True))
    total = jnp.sum(weights, axis=0, keepdims=True)
    probs = (weights / total).astype(BF16)
    blended = contract(probs[:context], cached[:LATENT_RANK], 0, 1)
    blended = blended + contract(probs[context:], padded[:, :LATENT_RANK], 0, 0)
    return blended.reshape(len(q_steps), heads, LATENT_RANK).astype(BF16)


def attention_kernel(length_ref, query_ref, cache_ref, new_ref, *refs, first, count):
    out_ref, result, sems = refs[-3:]
    steps = query_ref.shape[1]
    copies = []
    for b in range(count):
        r = first + b
        result[b] = attend_request(
            [query_ref[r, s] for s in range(steps)], cache_ref[r], new_ref[r], length_ref[r]
        )
        copy = pltpu.make_async_copy(result.at[b], out_ref.at[r], sems.at[b])
        copy.start()
        copies.append(copy)
    for copy in copies:
        copy.wait()


def attention(lengths, inputs, first, count, previous):
    requests, steps, latent, heads = inputs[0].shape
    vmem = pl.BlockSpec(memory_space=pltpu.VMEM)
    hbm = pl.BlockSpec(memory_space=pl.ANY)
    in_specs = [pl.BlockSpec(memory_space=pltpu.SMEM), vmem, vmem, vmem]
    operands = [pltpu.with_memory_space_constraint(lengths, pltpu.HBM)]
    operands += [pltpu.with_memory_space_constraint(x, pltpu.VMEM) for x in inputs]
    aliases = {}
    if previous is not None:
        in_specs.append(hbm)
        aliases = {len(operands): 0}
        operands.append(pltpu.with_memory_space_constraint(previous, pltpu.HBM))
    return pl.pallas_call(
        functools.partial(attention_kernel, first=first, count=count),
        in_specs=in_specs,
        out_specs=hbm,
        out_shape=pltpu.HBM((requests, steps, heads, LATENT_RANK), BF16),
        scratch_shapes=[
            pltpu.VMEM((count, steps, heads, LATENT_RANK), BF16),
            pltpu.SemaphoreType.DMA((count,)),
        ],
        input_output_aliases=aliases,
        compiler_params=pltpu.CompilerParams(vmem_limit_bytes=12 << 20),
        cost_estimate=SMALL_COST,
        name="attention",
    )(*operands)


def route_kernel(place_ref, rows_ref, score_ref, expert_ref, out_ref, table_ref, *, experts):
    tokens, width = rows_ref.shape
    sigmoid = jax.nn.sigmoid(score_ref[...])
    weights = ROUTE_SCALE * sigmoid / jnp.sum(sigmoid, axis=0, keepdims=True)
    weights = weights.astype(BF16).astype(F32)
    named = expert_ref[...]
    even = lax.broadcasted_iota(jnp.int32, named.shape, 1) % 2 == 0
    slot = jnp.zeros_like(named)
    for e in range(experts):
        slot = jnp.where(
            named == e, jnp.where(even, place_ref[0, e], place_ref[1, e]), slot
        )
    index = lax.broadcasted_iota(jnp.int32, (LANES, tokens), 0)
    table = jnp.zeros((LANES, tokens), F32)
    for k in range(named.shape[0]):
        table = table + jnp.where(index == slot[k : k + 1], weights[k : k + 1], 0.0)
    row = lax.broadcasted_iota(jnp.int32, (tokens, tokens), 0)
    column = lax.broadcasted_iota(jnp.int32, (tokens, tokens), 1)
    unit = jnp.where(row == column, 1.0, 0.0).astype(BF16)
    table = contract(unit, table.astype(BF16), 1, 1).astype(BF16)
    out_ref[:, :width] = rows_ref[...]
    out_ref[:, width:] = table
    table_ref[...] = table


def route(placement, rows, scores, expert_ids):
    tokens, width = rows.shape
    vmem = pl.BlockSpec(memory_space=pltpu.VMEM)
    return pl.pallas_call(
        functools.partial(route_kernel, experts=placement.shape[0]),
        in_specs=[pl.BlockSpec(memory_space=pltpu.SMEM), vmem, vmem, vmem],
        out_specs=[vmem] * 2,
        out_shape=[jax.ShapeDtypeStruct((tokens, n), BF16) for n in (width + LANES, LANES)],
        compiler_params=pltpu.CompilerParams(vmem_limit_bytes=4 << 20),
        cost_estimate=pl.CostEstimate(flops=1 << 34, bytes_accessed=1 << 25, transcendentals=0),
        name="route",
    )(*(pltpu.with_memory_space_constraint(x, pltpu.HBM) for x in (placement.T, rows, scores.T, expert_ids.T)))


def experts_kernel(*refs, parts, groups):
    rows_refs, refs = refs[:parts], refs[parts:]
    (gate_ref, up_ref, down_ref, chip_ref), refs = refs[:4], refs[4:]
    out_refs, (rows_s, act_s) = refs[: 2 * groups], refs[2 * groups :]
    slots, width, hidden = gate_ref.shape
    start = 0
    for ref in rows_refs:
        rows_s[start : start + ref.shape[0], :] = ref[...]
        start += ref.shape[0]
    table = rows_s[:, width:].astype(F32)
    lane = lax.broadcasted_iota(jnp.int32, table.shape, 1)
    for s in range(slots):
        slot = chip_ref[0] * slots + s
        weight = jnp.sum(jnp.where(lane == slot, table, 0.0), axis=1, keepdims=True)
        rows = rows_s[:, :width]
        gate = contract(rows, gate_ref[s], 1, 0)
        up = contract(rows, up_ref[s], 1, 0)
        act = gate / (1.0 + jnp.exp(-gate)) * up
        act_s[:, s * hidden : (s + 1) * hidden] = (weight * act).astype(BF16)

    total = contract(act_s[:, :hidden], down_ref[0], 1, 0)
    for s in range(1, slots):
        total = total + contract(act_s[:, s * hidden : (s + 1) * hidden], down_ref[s], 1, 0)
    start = 0
    for ref in out_refs:
        ref[...] = total[start : start + ref.shape[0]].astype(ref.dtype)
        start += ref.shape[0]


def experts(parts, gate, up, down, chip, groups):
    slots, width, hidden = gate.shape
    count = 2 * sum(groups)
    vmem = pl.BlockSpec(memory_space=pltpu.VMEM)
    outs = pl.pallas_call(
        functools.partial(experts_kernel, parts=len(parts), groups=len(groups)),
        in_specs=[vmem] * (len(parts) + 3) + [pl.BlockSpec(memory_space=pltpu.SMEM)],
        out_specs=[vmem] * (2 * len(groups)),
        out_shape=[
            jax.ShapeDtypeStruct((n, width), kind) for kind in (F32, BF16) for n in groups
        ],
        scratch_shapes=[
            pltpu.VMEM((count, parts[0].shape[1]), BF16),
            pltpu.VMEM((count, slots * hidden), BF16),
        ],
        compiler_params=pltpu.CompilerParams(vmem_limit_bytes=16 << 20),
        cost_estimate=SMALL_COST,
        name="experts",
    )(*parts, gate, up, down, chip)
    return outs[: len(groups)], outs[len(groups) :]


def halving_masks(ep):
    bits = []
    bit = ep // 2
    while bit:
        bits.append(bit)
        bit //= 2
    other = bits[:-2] + bits[-2:][::-1]
    return bits, other


def hop(x, ep, sub, masks, turn):
    pairs = [
        (e * sub + s, (e ^ masks[s % 2][turn]) * sub + s) for e in range(ep) for s in range(sub)
    ]
    return lax.ppermute(x, ("ep", "sub"), pairs)


def swap(x):
    return lax.ppermute(x, "sub", [(0, 1), (1, 0)])


def add(*terms):
    total = terms[0].astype(F32)
    for t in terms[1:]:
        total = total + t.astype(F32)
    return total


def on_device(
    queries,
    latent_cache,
    new_latent,
    lengths,
    moe_input,
    gate_scores,
    expert_ids,
    placement,
    w_gate,
    w_up,
    w_down,
):
    ep, sub = lax.axis_size("ep"), lax.axis_size("sub")
    masks = halving_masks(ep)
    turns = len(masks[0])
    width = moe_input.shape[1]
    requests, width = queries.shape[0], moe_input.shape[1]
    inputs = [queries.transpose(0, 1, 3, 2), latent_cache.transpose(0, 2, 1), new_latent]
    chip = lax.axis_index("ep").astype(jnp.int32)[None]
    barrier = lax.optimization_barrier
    chip, gate_scores, lengths = barrier((chip, gate_scores, lengths))

    requests = queries.shape[0]
    gate, up, down = [pltpu.with_memory_space_constraint(w, pltpu.VMEM) for w in (w_gate, w_up, w_down)]
    inputs = [pltpu.with_memory_space_constraint(x, pltpu.VMEM) for x in inputs]

    out = None
    done = 0

    def attend(count, tie):
        nonlocal out, inputs, done
        count = min(count, requests - done)
        if count == 0:
            return tie
        out = attention(lengths, inputs, done, count, out)
        done += count
        tie, out, inputs = barrier((tie, out, inputs))
        return tie

    own, table = route(placement, moe_input, gate_scores, expert_ids)
    a = jnp.concatenate([hop(x, ep, sub, masks, 0) for x in (moe_input, table)], axis=1)
    hop_a, hop_b, hop_c = (
        functools.partial(hop, ep=ep, sub=sub, masks=masks, turn=turn)
        for turn in range(turns - 3, turns)
    )
    if turns > 3:
        own = jnp.concatenate([own, a], axis=0)
        for turn in range(1, turns - 3):
            own = jnp.concatenate([own, hop(own, ep, sub, masks, turn)], axis=0)
        a = hop_a(own)
    n = own.shape[0]
    own, inputs = barrier((own, inputs))
    c = hop_c(own)
    b, a = attend(2, (hop_b(own), a))
    bc, ab, ac = hop_c(b), hop_b(a), hop_c(a)
    near_rows = [jnp.concatenate(x, axis=0) for x in ((own, a), (b, c))]
    near_rows += [swap(x) for x in near_rows]
    near_own, near_other = experts(near_rows, gate, up, down, chip, [4 * n])
    bc, ab, ac, near_own, near_other = barrier((bc, ab, ac, near_own, near_other))
    abc = hop_c(ab)
    ab, inputs = barrier((ab, inputs))
    abc = attend(2, abc)
    near = barrier(add(near_own[0], swap(near_other[0])))
    got_c = hop_c(near[3 * n :].astype(BF16))
    early = jnp.concatenate([ab, ac], axis=0)
    early_swap, late_swap = swap(early), swap(bc)
    abc, early_swap, late_swap, near = barrier((abc, early_swap, late_swap, near))
    far_rows = [early, bc, abc, early_swap, late_swap, swap(abc)]
    far_own, far_other = experts(far_rows, gate, up, down, chip, [3 * n, n])

    sent = add(far_own[1], swap(far_other[1])).astype(BF16)
    far = add(far_own[0], swap(far_other[0]))
    rest = far[n:].astype(BF16)
    got_ab = hop_c(sent)
    got = hop_c(rest)
    rest, inputs = barrier((rest, inputs))
    got_ab = attend(1, got_ab)
    sent = add(far[:n], got_ab).astype(BF16)
    got_a = hop_b(sent)
    got, got_a = barrier((got, got_a))
    sent = add(near[n : 2 * n], got[:n], got_a).astype(BF16)
    sent, got = barrier((sent, got))
    back_a = hop_a(sent)
    back_b = hop_b(add(near[2 * n : 3 * n], got[n:]).astype(BF16))
    sent, inputs = barrier((sent, inputs))
    back_a = attend(requests, back_a)
    total = add(near[:n], got_c, back_b, back_a)
    for turn in range(turns - 4, -1, -1):
        half = total.shape[0] // 2
        total = add(total[:half], hop(total[half:].astype(BF16), ep, sub, masks, turn))
    return out, total.astype(BF16)


def solution(mesh):
    split = ("groups", "ep", "sub")
    return jax.shard_map(
        on_device,
        mesh=mesh,
        in_specs=(
            P(split, None, None, None),
            P(split, None, None),
            P(split, None, None),
            P(split),
            P(split, None),
            P(split, None),
            P(split, None),
            P("groups", None),
            P(("groups", "ep"), None, "sub"),
            P(("groups", "ep"), None, "sub"),
            P(("groups", "ep"), "sub", None),
        ),
        out_specs=(P(split, None, None, None), P(split, None)),
        check_vma=False,
    )
```
